32 devices in a mesh: groups: 1, dp: 1, expert: 16 (over z, y, core), tensor: 2 (over x).
Axes of the slice: x: 2, y: 2, z: 4, core: 2. Of those that a mesh axis runs over, the one named last changes fastest.
Arguments:
- tokens: bfloat16 [2048, 4096], P(('groups', 'dp', 'expert')), may hold values from -6 to 6
- expert_ids: int32 [2048, 2], P(('groups', 'dp', 'expert')), may hold values from 0 to 15, all different within a row; in each aligned block of 128 rows (0 to 127, 128 to 255, ...) at most 24 rows name the same one
- gate_probs: float32 [2048, 2], P(('groups', 'dp', 'expert')), may hold values from 0.2 to 1
- w_gate: bfloat16 [16, 4096, 3584], P('expert', 'dp', 'tensor'), may hold values from -0.09375 to 0.09375
- w_up: bfloat16 [16, 4096, 3584], P('expert', 'dp', 'tensor'), may hold values from -0.09375 to 0.09375
- w_down: bfloat16 [16, 3584, 4096], P('expert', 'tensor', 'dp'), may hold values from -0.09375 to 0.09375
Outputs:
- mixed: bfloat16 [2048, 4096], P(('groups', 'dp', 'expert'), 'tensor')
The draws below stay inside these ranges and needn't reach their ends.
Inputs may be any that keep to these rules, and one draw needn't show every extreme that they name: `expert_ids`: each row names 2 different experts; in each aligned block of 128 rows no expert is named by more than 24 rows, and in some blocks one expert is named by exactly 24 rows.
All inputs are finite; a program needn't handle non-finite values.
Results may differ from the reference program's by a relative error of at most 0.005.
Values may be sent and summed in bfloat16 or wider, within the bound.
No kernel may reach another device: no remote copies, remote signals or barrier semaphores. Data moves between devices by JAX's collectives and lax.ppermute only.
A program may use at most 128 MiB of HBM per device.

```python
import math
import jax
import jax.numpy as jnp
import numpy as np
from jax import lax

D = 4096
FF = 3584
EXPERTS = 16
TOP = 2
BLOCK = 128
CAP = 24
TOKENS = 2048


def block_scale(stream_key, dims, split, least, high):
    loudness = 1.0
    for axis_at, shards_of in split:
        steps = jax.random.uniform(jax.random.fold_in(jax.random.fold_in(stream_key, 6), axis_at), (shards_of,), jnp.float32, least / len(split), high / len(split))
        loudness = loudness * jnp.repeat(jnp.exp(steps), dims[axis_at] // shards_of).reshape((-1,) + (1,) * (len(dims) - 1 - axis_at))
    return loudness


def routed_block(stream_key, own, number, rows, number_of, top, limit, slope):
    ranking = jax.random.permutation(stream_key, number_of)
    crowded, common = portions_of(number_of, rows * top, limit, slope, True), portions_of(number_of, rows * top, limit, slope, False)
    places = jnp.arange(number_of)

    def named(lengths, turn):
        used = int((lengths > 0).sum())
        fixed = max(1, used // 4)
        passed = fixed + (places - fixed + turn * (used - fixed)) % max(1, number_of - fixed)
        return jnp.zeros((number_of,), jnp.int32).at[ranking[jnp.where(places < fixed, places, passed)]].set(jnp.asarray(lengths, jnp.int32))

    lengths = jnp.where(number % 4 == 0, named(crowded, number // 4), named(common, number - number // 4 - 1))
    mixed = jax.random.permutation(jax.random.fold_in(own, 3), number_of)
    giver, receiver = mixed[0:number_of // 2 * 2:2], mixed[1:number_of // 2 * 2:2]
    slack = jnp.minimum(lengths[giver] - 1, limit - lengths[receiver]) // 2
    slack = jnp.where((giver == ranking[0]) | (receiver == ranking[0]) | (lengths[receiver] == 0), 0, jnp.maximum(slack, 0))
    passed = jax.random.randint(jax.random.fold_in(own, 4), (number_of // 2,), 0, 1 << 20) % (slack + 1)
    lengths = lengths.at[giver].add(-passed).at[receiver].add(passed)
    items = jnp.searchsorted(jnp.cumsum(lengths), jnp.arange(rows * top), side="right").astype(jnp.int32)
    grid = items.reshape(top, rows).T
    grid = grid[jax.random.permutation(jax.random.fold_in(own, 1), rows)]
    turn = jax.random.randint(jax.random.fold_in(own, 2), (rows, 1), 0, top)
    return jnp.take_along_axis(grid, (jnp.arange(top)[None, :] + turn) % top, axis=1)


def portions_of(count, total, bound, skew, full):
    portions = [(1 << 20) // math.isqrt(grade ** skew) + 1 for grade in range(1, count + 1)]
    largest = bound if full else min(bound, max(-(-total // count), total * portions[0] // sum(portions)))
    least = 1 if total - largest >= count - 1 else 0
    counts, surplus = [largest] + [least] * (count - 1), total - largest - least * (count - 1)
    while surplus > 0:
        free = [i for i in range(1, count) if counts[i] < largest] or [i for i in range(1, count) if counts[i] < bound]
        whole, budget = sum([portions[i] for i in free]), surplus
        for i in free:
            extra = min(bound - counts[i], max(1, budget * portions[i] // whole), surplus)
            counts[i] = counts[i] + extra
            surplus = surplus - extra
    return np.array(counts)


def noise(own_key, extent, width, reach, shards=(), held_as=jnp.bfloat16):
    values = width * jax.random.normal(own_key, extent, jnp.float32)
    if shards:
        values = values * block_scale(own_key, extent, shards, -0.22, 0.18)
    return jnp.clip(values, -reach, reach).astype(held_as)


def setup_inputs(seed: int = 0, part: int = 0) -> dict:
    splits = jax.random.split(jax.random.key(seed), 7)
    part_splits = jax.random.split(jax.random.fold_in(splits[6], part), 7)
    tokens = noise(part_splits[0], (TOKENS, D), 1.0, 6.0, ((0, 16),))
    expert_ids_keys = jax.random.split(jax.random.fold_in(part_splits[1], 1), TOKENS // BLOCK)
    expert_ids_turns = jax.random.permutation(jax.random.fold_in(part_splits[1], 3), TOKENS // BLOCK)
    expert_ids = jax.vmap(lambda own, number: routed_block(jax.random.fold_in(part_splits[1], 2), own, number, BLOCK, EXPERTS, TOP, CAP, 2))(expert_ids_keys, expert_ids_turns).reshape((TOKENS, TOP))
    gate_probs = jnp.clip(jnp.exp(math.log(1.0) - 1.609438 * jax.random.uniform(part_splits[2], (TOKENS, TOP), jnp.float32) ** block_scale(part_splits[2], (TOKENS, TOP), ((0, 16),), -0.2, 0.2)), 0.2, 1.0)
    w_gate = noise(splits[3], (EXPERTS, D, FF), D ** -0.5, 0.09375, ((0, 16), (2, 2)))
    w_up = noise(splits[4], (EXPERTS, D, FF), D ** -0.5, 0.09375, ((0, 16), (2, 2)))
    w_down = noise(splits[5], (EXPERTS, FF, D), FF ** -0.5, 0.09375, ((0, 16), (1, 2)))
    return {"tokens": tokens, "expert_ids": expert_ids, "gate_probs": gate_probs, "w_gate": w_gate, "w_up": w_up, "w_down": w_down}


def expert_ffn(args):
    rows, gate_w, up_w, down_w = args
    gate = jnp.dot(rows, gate_w, preferred_element_type=jnp.float32)
    up = jnp.dot(rows, up_w, preferred_element_type=jnp.float32)
    hidden = (jax.nn.silu(gate) * up).astype(jnp.bfloat16)
    return jnp.dot(hidden, down_w, preferred_element_type=jnp.float32)


def reference(tokens, expert_ids, gate_probs, w_gate, w_up, w_down):
    blocks = TOKENS // BLOCK
    flat = expert_ids.reshape(blocks, BLOCK * TOP)
    onehot = (flat[:, :, None] == jnp.arange(EXPERTS, dtype=jnp.int32)[None, None, :]).astype(jnp.int32)
    before = jnp.cumsum(onehot, axis=1) - onehot
    slot = jnp.sum(before * onehot, axis=2)
    offset = (jnp.arange(blocks, dtype=jnp.int32) * CAP)[:, None]
    place = (offset + slot).reshape(TOKENS, TOP).astype(jnp.int32)
    spread = jnp.broadcast_to(tokens[:, None, :], (TOKENS, TOP, D))
    buffers = jnp.zeros((EXPERTS, blocks * CAP, D), jnp.bfloat16).at[expert_ids, place].set(spread)
    outputs = lax.map(expert_ffn, (buffers, w_gate, w_up, w_down))
    picked = outputs[expert_ids, place]
    mixed = jnp.sum(picked * gate_probs[:, :, None].astype(jnp.float32), axis=1)
    return mixed.astype(jnp.bfloat16)
```

```python
import jax
import jax.numpy as jnp
from jax import lax
from jax.sharding import PartitionSpec as P

BLOCK = 128
CAP = 24
CHUNKS = 2


def selectors(expert_ids, gate_probs, experts):
    rows = expert_ids.shape[0]
    blocks = rows // BLOCK
    match = expert_ids[:, :, None] == jnp.arange(experts, dtype=jnp.int32)
    named = jnp.any(match, axis=1)
    weight = jnp.sum(jnp.where(match, gate_probs[:, :, None], 0.0), axis=1)
    named = named.reshape(blocks, BLOCK, experts)
    weight = weight.reshape(blocks, BLOCK, experts)
    earlier = jnp.tril(jnp.ones((BLOCK, BLOCK), jnp.bfloat16), -1)
    before = jnp.einsum(
        "rs,bse->bre",
        earlier,
        named.astype(jnp.bfloat16),
        preferred_element_type=jnp.float32,
    ).astype(jnp.int32)
    slots = jnp.arange(CAP, dtype=jnp.int32)
    hit = named[..., None] & (before[..., None] == slots)
    chosen = hit.astype(jnp.bfloat16)
    high = weight.astype(jnp.bfloat16)
    rest = weight - high.astype(jnp.float32)
    middle = rest.astype(jnp.bfloat16)
    low = (rest - middle.astype(jnp.float32)).astype(jnp.bfloat16)
    weights = [jnp.where(hit, part[..., None], 0) for part in (high, middle, low)]
    return chosen, weights


def gather_over(piece, axis):
    size = lax.axis_size(axis)
    if size == 1:
        return [piece]
    me = lax.axis_index(axis)
    got = [piece]
    for step in range(1, size):
        got.append(
            lax.ppermute(piece, axis, [((i + step) % size, i) for i in range(size)])
        )
    out = []
    for rank in range(size):
        value = got[0]
        for step in range(1, size):
            value = jnp.where((me + step) % size == rank, got[step], value)
        out.append(value)
    return out


def on_device(tokens, expert_ids, gate_probs, w_gate, w_up, w_down):
    rows, width = tokens.shape
    experts = lax.axis_size("expert")
    ranks = lax.axis_size("tensor")
    me = lax.axis_index("tensor")
    blocks = rows // BLOCK
    w_gate = lax.all_gather(w_gate, "dp", axis=1, tiled=True)[0]
    w_up = lax.all_gather(w_up, "dp", axis=1, tiled=True)[0]
    w_down = lax.all_gather(w_down, "dp", axis=2, tiled=True)[0]
    chosen, weights = selectors(expert_ids, gate_probs, experts)

    share = width // ranks
    part = share // CHUNKS
    mine = lax.dynamic_slice_in_dim(tokens, me * share, share, axis=1)
    mine = mine.reshape(blocks, BLOCK, share)
    slots = experts * blocks * CAP
    gate = up = None
    for c in range(CHUNKS):
        outgoing = jnp.einsum(
            "bres,brd->ebsd",
            chosen,
            mine[:, :, c * part : (c + 1) * part],
            preferred_element_type=jnp.float32,
        ).astype(jnp.bfloat16)
        arrived = lax.all_to_all(
            outgoing.reshape(experts, blocks * CAP, part),
            "expert",
            split_axis=0,
            concat_axis=0,
            tiled=True,
        ).reshape(slots, part)
        for rank, piece in enumerate(gather_over(arrived, "tensor")):
            at = rank * share + c * part
            g = jnp.dot(piece, w_gate[at : at + part], preferred_element_type=jnp.float32)
            u = jnp.dot(piece, w_up[at : at + part], preferred_element_type=jnp.float32)
            gate = g if gate is None else gate + g
            up = u if up is None else up + u
    hidden = (jax.nn.silu(gate) * up).astype(jnp.bfloat16)

    outs = []
    for c in range(CHUNKS):
        terms = []
        for rank in range(ranks):
            at = rank * share + c * part
            terms.append(
                jnp.dot(hidden, w_down[:, at : at + part], preferred_element_type=jnp.float32)
            )
        stacked = jnp.stack(terms)
        owned = lax.dynamic_index_in_dim(stacked, me, 0, keepdims=False)
        for step in range(1, ranks):
            sent = lax.dynamic_index_in_dim(
                stacked, (me + step) % ranks, 0, keepdims=False
            ).astype(jnp.bfloat16)
            got = lax.ppermute(sent, "tensor", [(i, (i + step) % ranks) for i in range(ranks)])
            owned = owned + got.astype(jnp.float32)
        returned = lax.all_to_all(
            owned.astype(jnp.bfloat16).reshape(experts, blocks * CAP, part),
            "expert",
            split_axis=0,
            concat_axis=0,
            tiled=True,
        ).reshape(experts, blocks, CAP, part)
        mixed = sum(
            jnp.einsum("bres,ebsd->brd", w, returned, preferred_element_type=jnp.float32)
            for w in weights
        )
        outs.append(mixed.reshape(rows, part).astype(jnp.bfloat16))
    return jnp.concatenate(outs, axis=1)


def solution(mesh):
    placed = (
        P(("groups", "dp", "expert"), None),
        P(("groups", "dp", "expert"), None),
        P(("groups", "dp", "expert"), None),
        P("expert", "dp", "tensor"),
        P("expert", "dp", "tensor"),
        P("expert", "tensor", "dp"),
    )
    return jax.shard_map(
        on_device,
        mesh=mesh,
        in_specs=placed,
        out_specs=P(("groups", "dp", "expert"), "tensor"),
        check_vma=False,
    )
```

```python
import jax
import jax.numpy as jnp
from jax import lax
from jax.experimental import pallas as pl
from jax.experimental.pallas import tpu as pltpu
from jax.sharding import PartitionSpec as P

BLOCK = 128
CAP = 24
LANES = 256
VMEM_BYTES = 40 * 1024 * 1024


def tile_of(width):
    return LANES if width % LANES == 0 else 128


def lift_kernel(count, has_sums, last, *refs):
    refs = list(refs[1:])
    pieces, refs = refs[:count], refs[count:]
    gates, refs = refs[:count], refs[count:]
    ups, refs = refs[:count], refs[count:]
    gate = up = None
    if has_sums:
        gate, up = refs[0][...], refs[1][...]
        refs = refs[2:]
    for x, g, u in zip(pieces, gates, ups):
        more_gate = jnp.dot(x[...], g[...], preferred_element_type=jnp.float32)
        more_up = jnp.dot(x[...], u[...], preferred_element_type=jnp.float32)
        gate = more_gate if gate is None else gate + more_gate
        up = more_up if up is None else up + more_up
    if last:
        refs[0][...] = (gate / (1.0 + jnp.exp(-gate)) * up).astype(jnp.bfloat16)
    else:
        refs[0][...] = gate
        refs[1][...] = up


def lift(pieces, starts, w_gate, w_up, sums=None, last=False):
    rows = pieces[0].shape[0]
    hidden = w_gate.shape[1]
    tile = tile_of(hidden)
    count = len(pieces)

    def weight_spec(i):
        return pl.BlockSpec(
            (pl.Element(pieces[i].shape[1]), pl.Element(tile)),
            lambda n, at: (pl.multiple_of(at[i], 128), n * tile),
        )

    across = pl.BlockSpec((rows, tile), lambda n, at: (0, n))
    in_specs = [pl.BlockSpec(p.shape, lambda n, at: (0, 0)) for p in pieces]
    in_specs += [weight_spec(i) for i in range(count)] * 2
    args = list(pieces) + [w_gate] * count + [w_up] * count
    if sums is not None:
        in_specs += [across, across]
        args += list(sums)
    if last:
        out_shape = jax.ShapeDtypeStruct((rows, hidden), jnp.bfloat16)
        out_specs = across
    else:
        out_shape = [jax.ShapeDtypeStruct((rows, hidden), jnp.float32)] * 2
        out_specs = [across, across]
    depth = sum(p.shape[1] for p in pieces)
    return pl.pallas_call(
        lambda *refs: lift_kernel(count, sums is not None, last, *refs),
        out_shape=out_shape,
        grid_spec=pltpu.PrefetchScalarGridSpec(
            num_scalar_prefetch=1,
            grid=(hidden // tile,),
            in_specs=in_specs,
            out_specs=out_specs,
        ),
        compiler_params=pltpu.CompilerParams(vmem_limit_bytes=VMEM_BYTES),
        cost_estimate=pl.CostEstimate(
            flops=4 * rows * depth * hidden,
            bytes_accessed=4 * depth * hidden + 16 * rows * hidden,
            transcendentals=rows * hidden if last else 0,
        ),
        name="lift",
    )(jnp.stack(starts).astype(jnp.int32), *args)


def drop_kernel(at, hidden, weight, out):
    value = jnp.dot(hidden[...], weight[...], preferred_element_type=jnp.float32)
    out[...] = value.astype(out.dtype)


def drop(hidden, w_down, starts, width, dtype):
    rows, depth = hidden.shape
    tile = tile_of(width)
    tiles = width // tile
    count = len(starts)
    return pl.pallas_call(
        drop_kernel,
        out_shape=jax.ShapeDtypeStruct((rows, count * width), dtype),
        grid_spec=pltpu.PrefetchScalarGridSpec(
            num_scalar_prefetch=1,
            grid=(count, tiles),
            in_specs=[
                pl.BlockSpec((rows, depth), lambda i, j, at: (0, 0)),
                pl.BlockSpec(
                    (pl.Element(depth), pl.Element(tile)),
                    lambda i, j, at: (0, pl.multiple_of(at[i] + j * tile, 128)),
                ),
            ],
            out_specs=pl.BlockSpec((rows, tile), lambda i, j, at: (0, i * tiles + j)),
        ),
        compiler_params=pltpu.CompilerParams(vmem_limit_bytes=VMEM_BYTES),
        cost_estimate=pl.CostEstimate(
            flops=2 * rows * depth * count * width,
            bytes_accessed=2 * depth * count * width + 4 * rows * count * width,
            transcendentals=0,
        ),
        name="drop",
    )(jnp.stack(starts).astype(jnp.int32), hidden, w_down)


def selectors(expert_ids, gate_probs, experts):
    rows = expert_ids.shape[0]
    blocks = rows // BLOCK
    match = expert_ids.T[:, None, :] == jnp.arange(experts, dtype=jnp.int32)[None, :, None]
    named = jnp.any(match, axis=0)
    weight = jnp.sum(jnp.where(match, gate_probs.T[:, None, :], 0.0), axis=0)
    row = jnp.arange(rows, dtype=jnp.int32)
    same = row[:, None] // BLOCK == row[None, :] // BLOCK
    earlier = ((row[:, None] < row[None, :]) & same).astype(jnp.bfloat16)
    before = jnp.dot(named.astype(jnp.bfloat16), earlier, preferred_element_type=jnp.float32)
    place = before.astype(jnp.int32) + (row // BLOCK * CAP)[None, :]
    slots = jnp.arange(blocks * CAP, dtype=jnp.int32)
    hit = named[:, None, :] & (place[:, None, :] == slots[None, :, None])
    high = weight.astype(jnp.bfloat16)
    rest = weight - high.astype(jnp.float32)
    middle = rest.astype(jnp.bfloat16)
    low = (rest - middle.astype(jnp.float32)).astype(jnp.bfloat16)
    flat = (experts * blocks * CAP, rows)
    chosen = hit.astype(jnp.bfloat16).reshape(flat)
    weights = [
        jnp.where(hit, part[:, None, :], 0).astype(jnp.bfloat16).reshape(flat)
        for part in (high, middle, low)
    ]
    return chosen, weights


def swap(value, experts):
    slots, width = value.shape
    return lax.all_to_all(
        value.reshape(experts, slots // experts, width),
        "expert",
        split_axis=0,
        concat_axis=0,
        tiled=True,
    ).reshape(slots, width)


def mix(weights, returned):
    return sum(
        lax.dot_general(
            w, returned, (((0,), (0,)), ((), ())), preferred_element_type=jnp.float32
        )
        for w in weights
    )


def on_device(tokens, expert_ids, gate_probs, w_gate, w_up, w_down):
    width = tokens.shape[1]
    experts = lax.axis_size("expert")
    ranks = lax.axis_size("tensor")
    me = lax.axis_index("tensor")
    w_gate = lax.all_gather(w_gate, "dp", axis=1, tiled=True)[0]
    w_up = lax.all_gather(w_up, "dp", axis=1, tiled=True)[0]
    w_down = lax.all_gather(w_down, "dp", axis=2, tiled=True)[0]
    chosen, weights = selectors(expert_ids, gate_probs, experts)

    def rank_at(step):
        return lax.rem(me + step, ranks)

    def send_up(value, step):
        return lax.ppermute(value, "tensor", [(i, (i + step) % ranks) for i in range(ranks)])

    share = width // ranks
    shared = round(2 * share / 3 / LANES) * LANES
    direct_at = ranks * shared

    def placed(features):
        return jnp.dot(chosen, features, preferred_element_type=jnp.float32).astype(jnp.bfloat16)

    mine = lax.dynamic_slice_in_dim(tokens, me * shared, shared, axis=1)
    own = swap(placed(mine), experts)
    direct = swap(placed(tokens[:, direct_at:]), experts)
    sums = lift([own], [me * shared], w_gate, w_up)
    for step in range(1, ranks):
        other = send_up(own, ranks - step)
        sums = lift([other], [rank_at(step) * shared], w_gate, w_up, sums)
    hidden = lift([direct], [jnp.int32(direct_at)], w_gate, w_up, sums, last=True)

    early = share - shared
    partial = drop(
        hidden, w_down, [jnp.int32(rank * share) for rank in range(ranks)], early, jnp.bfloat16
    )
    returned = swap(partial, experts)
    owned = drop(hidden, w_down, [me * share + early], shared, jnp.float32)
    for step in range(1, ranks):
        sent = drop(hidden, w_down, [rank_at(step) * share + early], shared, jnp.bfloat16)
        owned = owned + send_up(sent, step).astype(jnp.float32)
    first = mix(weights, returned)

    def part_of(rank):
        return lax.dynamic_slice_in_dim(first, rank * early, early, axis=1)

    mixed = part_of(me)
    for step in range(1, ranks):
        mixed = mixed + send_up(part_of(rank_at(step)), step)
    late = mix(weights, swap(owned.astype(jnp.bfloat16), experts))
    return jnp.concatenate([mixed.astype(jnp.bfloat16), late.astype(jnp.bfloat16)], axis=1)


def solution(mesh):
    placed = (
        P(("groups", "dp", "expert"), None),
        P(("groups", "dp", "expert"), None),
        P(("groups", "dp", "expert"), None),
        P("expert", "dp", "tensor"),
        P("expert", "dp", "tensor"),
        P("expert", "tensor", "dp"),
    )
    return jax.shard_map(
        on_device,
        mesh=mesh,
        in_specs=placed,
        out_specs=P(("groups", "dp", "expert"), "tensor"),
        check_vma=False,
    )
```

```python
import jax
import jax.numpy as jnp
from jax import lax
from jax.experimental import pallas as pl
from jax.experimental.pallas import tpu as pltpu
from jax.sharding import PartitionSpec as P

BLOCK = 128
CAP = 24
LANES = 256
VMEM_BYTES = 36 * 1024 * 1024


def tile_of(width):
    return LANES if width % LANES == 0 else 128


def fetch_rows(source, start, target, sems):
    tiles, depth, tile = target.shape

    def copy(n):
        return pltpu.make_async_copy(
            source.at[pl.ds(start, depth), pl.ds(pl.multiple_of(n * tile, 128), tile)],
            target.at[n],
            sems.at[n],
        )

    for n in range(tiles):
        copy(n).start()
    return copy


def fetch_columns(source, starts, width, target, sems):
    tiles, depth, tile = target.shape
    each = width // tile

    def copy(n):
        at = pl.multiple_of(starts[n // each] + (n % each) * tile, 128)
        return pltpu.make_async_copy(source.at[:, pl.ds(at, tile)], target.at[n], sems.at[n])

    for n in range(tiles):
        copy(n).start()
    return copy


def lift_tiles(piece, sums, gate_tiles, up_tiles, copies, write):
    tiles, depth, tile = gate_tiles.shape

    @pl.loop(0, tiles)
    def _(n):
        at = pl.ds(pl.multiple_of(n * tile, 128), tile)
        copies[0](n).wait()
        gate = jnp.dot(piece[...], gate_tiles[n], preferred_element_type=jnp.float32)
        copies[1](n).wait()
        up = jnp.dot(piece[...], up_tiles[n], preferred_element_type=jnp.float32)
        if sums is not None:
            gate = gate + sums[0][:, at]
            up = up + sums[1][:, at]
        write(at, gate, up)


def drop_tiles(hidden, down_tiles, copy, out):
    tiles, depth, tile = down_tiles.shape

    for n in range(tiles):
        copy(n).wait()
        value = jnp.dot(hidden[...], down_tiles[n], preferred_element_type=jnp.float32)
        out[:, n * tile : (n + 1) * tile] = value.astype(out.dtype)


def vmem():
    return pl.BlockSpec(memory_space=pltpu.VMEM)


def weight_scratch(tiles, depth, tile):
    return [pltpu.VMEM((tiles, depth, tile), jnp.bfloat16), pltpu.SemaphoreType.DMA((tiles,))]


def lift(piece, start, w_gate, w_up, sums=None):
    rows, depth = piece.shape
    hidden = w_gate.shape[1]
    tile = tile_of(hidden)

    def kernel(at, piece, w_gate, w_up, *refs):
        given, (gate, up), scratch = refs[:-6], refs[-6:-4], refs[-4:]
        begin = pl.multiple_of(at[0], 128)
        copies = [
            fetch_rows(w_gate, begin, scratch[0], scratch[1]),
            fetch_rows(w_up, begin, scratch[2], scratch[3]),
        ]

        def write(at, gate_tile, up_tile):
            gate[:, at] = gate_tile
            up[:, at] = up_tile

        lift_tiles(piece, given or None, scratch[0], scratch[2], copies, write)

    given = [] if sums is None else list(sums)
    return pl.pallas_call(
        kernel,
        out_shape=[jax.ShapeDtypeStruct((rows, hidden), jnp.float32)] * 2,
        in_specs=[pl.BlockSpec(memory_space=pltpu.SMEM), vmem()]
        + [pl.BlockSpec(memory_space=pltpu.HBM)] * 2
        + [vmem()] * len(given),
        out_specs=[vmem(), vmem()],
        scratch_shapes=weight_scratch(hidden // tile, depth, tile) * 2,
        compiler_params=pltpu.CompilerParams(vmem_limit_bytes=VMEM_BYTES),
        cost_estimate=pl.CostEstimate(
            flops=4 * rows * depth * hidden,
            bytes_accessed=4 * depth * hidden,
            transcendentals=0,
        ),
        name="lift",
    )(jnp.reshape(start, (1,)).astype(jnp.int32), piece, w_gate, w_up, *given)


def finish(piece, start, w_gate, w_up, sums, w_down, columns, width):
    rows, depth = piece.shape
    hidden = w_gate.shape[1]
    tile = tile_of(hidden)
    wide = tile_of(width)
    count = len(columns)

    def kernel(at, piece, w_gate, w_up, w_down, gate, up, value, out, *scratch):
        begin = pl.multiple_of(at[0], 128)
        copies = [
            fetch_rows(w_gate, begin, scratch[0], scratch[1]),
            fetch_rows(w_up, begin, scratch[2], scratch[3]),
        ]
        starts = [at[1 + i] for i in range(count)]
        down = fetch_columns(w_down, starts, width, scratch[4], scratch[5])

        def write(at, gate_tile, up_tile):
            silu = gate_tile / (1.0 + jnp.exp(-gate_tile))
            value[:, at] = (silu * up_tile).astype(jnp.bfloat16)

        lift_tiles(piece, (gate, up), scratch[0], scratch[2], copies, write)
        drop_tiles(value, scratch[4], down, out)

    return pl.pallas_call(
        kernel,
        out_shape=[
            jax.ShapeDtypeStruct((rows, hidden), jnp.bfloat16),
            jax.ShapeDtypeStruct((rows, count * width), jnp.bfloat16),
        ],
        in_specs=[pl.BlockSpec(memory_space=pltpu.SMEM), vmem()]
        + [pl.BlockSpec(memory_space=pltpu.HBM)] * 3
        + [vmem()] * 2,
        out_specs=[vmem(), vmem()],
        scratch_shapes=weight_scratch(hidden // tile, depth, tile) * 2
        + weight_scratch(count * width // wide, hidden, wide),
        compiler_params=pltpu.CompilerParams(vmem_limit_bytes=VMEM_BYTES),
        cost_estimate=pl.CostEstimate(
            flops=4 * rows * depth * hidden + 2 * rows * hidden * count * width,
            bytes_accessed=4 * depth * hidden + 2 * hidden * count * width,
            transcendentals=rows * hidden,
        ),
        name="finish",
    )(
        jnp.stack([start] + columns).astype(jnp.int32),
        piece,
        w_gate,
        w_up,
        w_down,
        *sums,
    )


def drop(hidden, w_down, start, width, dtype):
    rows, depth = hidden.shape
    tile = tile_of(width)

    def kernel(at, hidden, w_down, out, *scratch):
        copy = fetch_columns(w_down, [at[0]], width, scratch[0], scratch[1])
        drop_tiles(hidden, scratch[0], copy, out)

    return pl.pallas_call(
        kernel,
        out_shape=jax.ShapeDtypeStruct((rows, width), dtype),
        in_specs=[
            pl.BlockSpec(memory_space=pltpu.SMEM),
            vmem(),
            pl.BlockSpec(memory_space=pltpu.HBM),
        ],
        out_specs=vmem(),
        scratch_shapes=weight_scratch(width // tile, depth, tile),
        compiler_params=pltpu.CompilerParams(vmem_limit_bytes=VMEM_BYTES),
        cost_estimate=pl.CostEstimate(
            flops=2 * rows * depth * width, bytes_accessed=2 * depth * width, transcendentals=0
        ),
        name="drop",
    )(jnp.reshape(start, (1,)).astype(jnp.int32), hidden, w_down)


def selectors(expert_ids, gate_probs, experts):
    rows = expert_ids.shape[0]
    blocks = rows // BLOCK
    match = expert_ids.T[:, None, :] == jnp.arange(experts, dtype=jnp.int32)[None, :, None]
    named = jnp.any(match, axis=0)
    weight = jnp.sum(jnp.where(match, gate_probs.T[:, None, :], 0.0), axis=0)
    row = jnp.arange(rows, dtype=jnp.int32)
    same = row[:, None] // BLOCK == row[None, :] // BLOCK
    earlier = ((row[:, None] < row[None, :]) & same).astype(jnp.bfloat16)
    before = jnp.dot(named.astype(jnp.bfloat16), earlier, preferred_element_type=jnp.float32)
    place = before.astype(jnp.int32) + (row // BLOCK * CAP)[None, :]
    slots = jnp.arange(blocks * CAP, dtype=jnp.int32)
    hit = named[:, None, :] & (place[:, None, :] == slots[None, :, None])
    high = weight.astype(jnp.bfloat16)
    rest = weight - high.astype(jnp.float32)
    middle = rest.astype(jnp.bfloat16)
    low = (rest - middle.astype(jnp.float32)).astype(jnp.bfloat16)
    flat = (experts * blocks * CAP, rows)
    chosen = hit.astype(jnp.bfloat16).reshape(flat)
    weights = [
        jnp.where(hit, part[:, None, :], 0).astype(jnp.bfloat16).reshape(flat)
        for part in (high, middle, low)
    ]
    return chosen, weights


def swap(value, experts):
    slots, width = value.shape
    return lax.all_to_all(
        value.reshape(experts, slots // experts, width),
        "expert",
        split_axis=0,
        concat_axis=0,
        tiled=True,
    ).reshape(slots, width)


def mix(weights, returned):
    return sum(
        lax.dot_general(
            w, returned, (((0,), (0,)), ((), ())), preferred_element_type=jnp.float32
        )
        for w in weights
    )


def on_device(tokens, expert_ids, gate_probs, w_gate, w_up, w_down):
    width = tokens.shape[1]
    experts = lax.axis_size("expert")
    ranks = lax.axis_size("tensor")
    me = lax.axis_index("tensor")
    w_gate = lax.all_gather(w_gate, "dp", axis=1, tiled=True)[0]
    w_up = lax.all_gather(w_up, "dp", axis=1, tiled=True)[0]
    w_down = lax.all_gather(w_down, "dp", axis=2, tiled=True)[0]
    chosen, weights = selectors(expert_ids, gate_probs, experts)

    def rank_at(step):
        return lax.rem(me + step, ranks)

    def send_up(value, step):
        return lax.ppermute(value, "tensor", [(i, (i + step) % ranks) for i in range(ranks)])

    share = width // ranks
    shared = round(2 * share / 3 / LANES) * LANES
    direct_at = ranks * shared

    def placed(features):
        return jnp.dot(chosen, features, preferred_element_type=jnp.float32).astype(jnp.bfloat16)

    mine = lax.dynamic_slice_in_dim(tokens, me * shared, shared, axis=1)
    own = swap(placed(mine), experts)
    direct = swap(placed(tokens[:, direct_at:]), experts)
    sums = lift(own, me * shared, w_gate, w_up)
    for step in range(1, ranks):
        other = send_up(own, ranks - step)
        sums = lift(other, rank_at(step) * shared, w_gate, w_up, sums)
    early = share - shared
    hidden, partial = finish(
        direct,
        jnp.int32(direct_at),
        w_gate,
        w_up,
        sums,
        w_down,
        [jnp.int32(rank * share) for rank in range(ranks)],
        early,
    )
    returned = swap(partial, experts)
    owned = drop(hidden, w_down, me * share + early, shared, jnp.float32)
    for step in range(1, ranks):
        sent = drop(hidden, w_down, rank_at(step) * share + early, shared, jnp.bfloat16)
        owned = owned + send_up(sent, step).astype(jnp.float32)
    first = mix(weights, returned)

    def part_of(rank):
        return lax.dynamic_slice_in_dim(first, rank * early, early, axis=1)

    mixed = part_of(me)
    for step in range(1, ranks):
        mixed = mixed + send_up(part_of(rank_at(step)), step)
    late = mix(weights, swap(owned.astype(jnp.bfloat16), experts))
    return jnp.concatenate([mixed.astype(jnp.bfloat16), late.astype(jnp.bfloat16)], axis=1)


def solution(mesh):
    placed = (
        P(("groups", "dp", "expert"), None),
        P(("groups", "dp", "expert"), None),
        P(("groups", "dp", "expert"), None),
        P("expert", "dp", "tensor"),
        P("expert", "dp", "tensor"),
        P("expert", "tensor", "dp"),
    )
    return jax.shard_map(
        on_device,
        mesh=mesh,
        in_specs=placed,
        out_specs=P(("groups", "dp", "expert"), "tensor"),
        check_vma=False,
    )
```

```python
import jax
import jax.numpy as jnp
from jax import lax
from jax.experimental import pallas as pl
from jax.experimental.pallas import tpu as pltpu
from jax.sharding import PartitionSpec as P

BLOCK = 128
CAP = 24
LANES = 256
STEP = 256
VMEM_BYTES = 50 * 1024 * 1024


def tile_of(width):
    return LANES if width % LANES == 0 else 128


def fetch(source, row, column, target, sems):
    depth, width = target.shape

    def copy(n):
        size = min(STEP, depth - n * STEP)
        return pltpu.make_async_copy(
            source.at[pl.ds(row + n * STEP, size), pl.ds(column, width)],
            target.at[pl.ds(n * STEP, size)],
            sems.at[n],
        )

    return [copy(n) for n in range(pl.cdiv(depth, STEP))]


def chunks_of(depth):
    steps = pl.cdiv(depth, STEP)
    count = pl.cdiv(steps, 3)
    edges = [steps * i // count for i in range(count + 1)]
    return list(zip(edges[:-1], edges[1:]))


def lift_pieces(pieces, weights, sums, gate, up, last):
    tile = tile_of(gate.shape[1])
    work = [
        (piece, weight, span)
        for piece, weight in zip(pieces, weights)
        for span in chunks_of(piece.shape[1])
    ]
    for number, (piece, (gate_rows, up_rows, gate_copies, up_copies), span) in enumerate(work):
        for n in range(*span):
            gate_copies[n].wait()
            up_copies[n].wait()
        at = pl.ds(span[0] * STEP, min(span[1] * STEP, piece.shape[1]) - span[0] * STEP)
        final = number == len(work) - 1
        before = sums if number == 0 else (gate, up)

        @pl.loop(0, gate.shape[1] // tile)
        def _(n):
            across = pl.ds(pl.multiple_of(n * tile, 128), tile)
            x = piece[:, at]
            g = jnp.dot(x, gate_rows[at, across], preferred_element_type=jnp.float32)
            u = jnp.dot(x, up_rows[at, across], preferred_element_type=jnp.float32)
            if before is not None:
                g = g + before[0][:, across]
                u = u + before[1][:, across]
            if final and last is not None:
                last[:, across] = (g / (1.0 + jnp.exp(-g)) * u).astype(jnp.bfloat16)
            else:
                gate[:, across] = g
                up[:, across] = u


def drop_columns(hidden, weight, copies, out, start):
    for copy in copies:
        copy.wait()
    width = weight.shape[1]
    for at in range(0, width, LANES):
        end = min(at + LANES, width)
        value = jnp.dot(hidden[...], weight[:, at:end], preferred_element_type=jnp.float32)
        out[:, start + at : start + end] = value.astype(out.dtype)


def vmem():
    return pl.BlockSpec(memory_space=pltpu.VMEM)


def hbm():
    return pl.BlockSpec(memory_space=pl.ANY)


def buffer(depth, width):
    return [
        pltpu.VMEM((depth, width), jnp.bfloat16),
        pltpu.SemaphoreType.DMA((pl.cdiv(depth, STEP),)),
    ]


def start_lift(at, pieces, w_gate, w_up, scratch):
    weights = []
    for i, piece in enumerate(pieces):
        begin = pl.multiple_of(at[i], 128)
        rows = scratch[4 * i : 4 * i + 4]
        gate_copies = fetch(w_gate, begin, 0, rows[0], rows[1])
        up_copies = fetch(w_up, begin, 0, rows[2], rows[3])
        for one, other in zip(gate_copies, up_copies):
            one.start()
            other.start()
        weights.append((rows[0], rows[2], gate_copies, up_copies))
    return weights


def lift(piece, start, w_gate, w_up):
    rows, depth = piece.shape
    hidden = w_gate.shape[1]

    def kernel(at, piece, w_gate, w_up, gate, up, *scratch):
        weights = start_lift(at, [piece], w_gate, w_up, scratch)
        lift_pieces([piece], weights, None, gate, up, None)

    return pl.pallas_call(
        kernel,
        out_shape=[jax.ShapeDtypeStruct((rows, hidden), jnp.float32)] * 2,
        in_specs=[pl.BlockSpec(memory_space=pltpu.SMEM), vmem(), hbm(), hbm()],
        out_specs=[vmem(), vmem()],
        scratch_shapes=buffer(depth, hidden) * 2,
        compiler_params=pltpu.CompilerParams(vmem_limit_bytes=VMEM_BYTES),
        cost_estimate=pl.CostEstimate(
            flops=4 * rows * depth * hidden,
            bytes_accessed=4 * depth * hidden,
            transcendentals=0,
        ),
        name="lift",
    )(jnp.reshape(start, (1,)).astype(jnp.int32), piece, w_gate, w_up)


def finish(pieces, starts, w_gate, w_up, sums, w_down, columns, width):
    rows = pieces[0].shape[0]
    depth = sum(piece.shape[1] for piece in pieces)
    hidden = w_gate.shape[1]
    count = len(pieces)

    def kernel(at, *refs):
        given, refs = refs[:count], refs[count:]
        w_gate, w_up, w_down, gate, up, value, out = refs[:7]
        gate_sum, up_sum = refs[7:9]
        scratch = refs[9:]
        weights = start_lift(at, given, w_gate, w_up, scratch)
        scratch = scratch[4 * count :]
        downs = []
        for i in range(len(columns)):
            begin = pl.multiple_of(at[count + i], 128)
            copies = fetch(w_down, 0, begin, scratch[2 * i], scratch[2 * i + 1])
            for copy in copies:
                copy.start()
            downs.append(copies)
        lift_pieces(given, weights, (gate, up), gate_sum, up_sum, value)
        for i, copies in enumerate(downs):
            drop_columns(value, scratch[2 * i], copies, out, i * width)

    scratch = [pltpu.VMEM((rows, hidden), jnp.float32)] * 2
    for piece in pieces:
        scratch += buffer(piece.shape[1], hidden) * 2
    for _ in columns:
        scratch += buffer(hidden, width)
    return pl.pallas_call(
        kernel,
        out_shape=[
            jax.ShapeDtypeStruct((rows, hidden), jnp.bfloat16),
            jax.ShapeDtypeStruct((rows, len(columns) * width), jnp.bfloat16),
        ],
        in_specs=[pl.BlockSpec(memory_space=pltpu.SMEM)]
        + [vmem()] * count
        + [hbm()] * 3
        + [vmem()] * 2,
        out_specs=[vmem(), vmem()],
        scratch_shapes=scratch,
        compiler_params=pltpu.CompilerParams(vmem_limit_bytes=VMEM_BYTES - 10 * 1024 * 1024),
        cost_estimate=pl.CostEstimate(
            flops=4 * rows * depth * hidden + 2 * rows * hidden * len(columns) * width,
            bytes_accessed=4 * depth * hidden + 2 * hidden * len(columns) * width,
            transcendentals=rows * hidden,
        ),
        name="finish",
    )(
        jnp.stack(list(starts) + list(columns)).astype(jnp.int32),
        *pieces,
        w_gate,
        w_up,
        w_down,
        *sums,
    )


def drop(hidden, w_down, start, width, dtype):
    rows, depth = hidden.shape

    def kernel(at, hidden, w_down, out, weight, sems):
        copies = fetch(w_down, 0, pl.multiple_of(at[0], 128), weight, sems)
        for copy in copies:
            copy.start()
        drop_columns(hidden, weight, copies, out, 0)

    return pl.pallas_call(
        kernel,
        out_shape=jax.ShapeDtypeStruct((rows, width), dtype),
        in_specs=[pl.BlockSpec(memory_space=pltpu.SMEM), vmem(), hbm()],
        out_specs=vmem(),
        scratch_shapes=buffer(depth, width),
        compiler_params=pltpu.CompilerParams(vmem_limit_bytes=VMEM_BYTES),
        cost_estimate=pl.CostEstimate(
            flops=2 * rows * depth * width, bytes_accessed=2 * depth * width, transcendentals=0
        ),
        name="drop",
    )(jnp.reshape(start, (1,)).astype(jnp.int32), hidden, w_down)


def selectors(expert_ids, gate_probs, experts):
    rows = expert_ids.shape[0]
    blocks = rows // BLOCK
    match = expert_ids.T[:, None, :] == jnp.arange(experts, dtype=jnp.int32)[None, :, None]
    named = jnp.any(match, axis=0)
    weight = jnp.sum(jnp.where(match, gate_probs.T[:, None, :], 0.0), axis=0)
    row = jnp.arange(rows, dtype=jnp.int32)
    same = row[:, None] // BLOCK == row[None, :] // BLOCK
    earlier = ((row[:, None] < row[None, :]) & same).astype(jnp.bfloat16)
    before = jnp.dot(named.astype(jnp.bfloat16), earlier, preferred_element_type=jnp.float32)
    place = before.astype(jnp.int32) + (row // BLOCK * CAP)[None, :]
    slots = jnp.arange(blocks * CAP, dtype=jnp.int32)
    hit = named[:, None, :] & (place[:, None, :] == slots[None, :, None])
    high = weight.astype(jnp.bfloat16)
    rest = weight - high.astype(jnp.float32)
    middle = rest.astype(jnp.bfloat16)
    low = (rest - middle.astype(jnp.float32)).astype(jnp.bfloat16)
    flat = (experts * blocks * CAP, rows)
    chosen = hit.astype(jnp.bfloat16).reshape(flat)
    weights = [
        jnp.where(hit, part[:, None, :], 0).astype(jnp.bfloat16).reshape(flat)
        for part in (high, middle, low)
    ]
    return chosen, weights


def swap(value, experts):
    slots, width = value.shape
    return lax.all_to_all(
        value.reshape(experts, slots // experts, width),
        "expert",
        split_axis=0,
        concat_axis=0,
        tiled=True,
    ).reshape(slots, width)


def mix(weights, returned):
    return sum(
        lax.dot_general(
            w, returned, (((0,), (0,)), ((), ())), preferred_element_type=jnp.float32
        )
        for w in weights
    )


def on_device(tokens, expert_ids, gate_probs, w_gate, w_up, w_down):
    width = tokens.shape[1]
    experts = lax.axis_size("expert")
    ranks = lax.axis_size("tensor")
    me = lax.axis_index("tensor")
    w_gate = lax.all_gather(w_gate, "dp", axis=1, tiled=True)[0]
    w_up = lax.all_gather(w_up, "dp", axis=1, tiled=True)[0]
    w_down = lax.all_gather(w_down, "dp", axis=2, tiled=True)[0]
    chosen, weights = selectors(expert_ids, gate_probs, experts)

    def rank_at(step):
        return lax.rem(me + step, ranks)

    def send_up(value, step):
        return lax.ppermute(value, "tensor", [(i, (i + step) % ranks) for i in range(ranks)])

    share = width // ranks
    shared = round(2 * share / 3 / LANES) * LANES
    direct_at = ranks * shared

    def placed(features):
        return jnp.dot(chosen, features, preferred_element_type=jnp.float32).astype(jnp.bfloat16)

    mine = lax.dynamic_slice_in_dim(tokens, me * shared, shared, axis=1)
    own = swap(placed(mine), experts)
    direct = swap(placed(tokens[:, direct_at:]), experts)
    sums = lift(own, me * shared, w_gate, w_up)
    pieces, starts = [], []
    for step in range(1, ranks):
        pieces.append(send_up(own, ranks - step))
        starts.append(rank_at(step) * shared)
    pieces.append(direct)
    starts.append(jnp.int32(direct_at))
    reduced = round(share * 9 / 16 / 128) * 128
    early = share - reduced
    columns = [jnp.int32(rank * share) for rank in range(ranks)]
    hidden, partial = finish(pieces, starts, w_gate, w_up, sums, w_down, columns, early)
    returned = swap(partial, experts)
    owned = drop(hidden, w_down, me * share + early, reduced, jnp.float32)
    for step in range(1, ranks):
        sent = drop(hidden, w_down, rank_at(step) * share + early, reduced, jnp.bfloat16)
        owned = owned + send_up(sent, step).astype(jnp.float32)
    first = mix(weights, returned)

    def part_of(rank):
        return lax.dynamic_slice_in_dim(first, rank * early, early, axis=1)

    mixed = part_of(me)
    for step in range(1, ranks):
        mixed = mixed + send_up(part_of(rank_at(step)), step)
    late = mix(weights, swap(owned.astype(jnp.bfloat16), experts))
    return jnp.concatenate([mixed.astype(jnp.bfloat16), late.astype(jnp.bfloat16)], axis=1)


def solution(mesh):
    placed = (
        P(("groups", "dp", "expert"), None),
        P(("groups", "dp", "expert"), None),
        P(("groups", "dp", "expert"), None),
        P("expert", "dp", "tensor"),
        P("expert", "dp", "tensor"),
        P("expert", "tensor", "dp"),
    )
    return jax.shard_map(
        on_device,
        mesh=mesh,
        in_specs=placed,
        out_specs=P(("groups", "dp", "expert"), "tensor"),
        check_vma=False,
    )
```

```python
import jax
import jax.numpy as jnp
from jax import lax
from jax.experimental import pallas as pl
from jax.experimental.pallas import tpu as pltpu
from jax.sharding import PartitionSpec as P

BLOCK = 128
CAP = 24
LANES = 256
STEP = 256
VMEM_BYTES = 50 * 1024 * 1024


def tile_of(width):
    return LANES if width % LANES == 0 else 128


def fetch(source, row, column, target, sems):
    depth, width = target.shape

    def copy(n):
        size = min(STEP, depth - n * STEP)
        return pltpu.make_async_copy(
            source.at[pl.ds(row + n * STEP, size), pl.ds(column, width)],
            target.at[pl.ds(n * STEP, size)],
            sems.at[n],
        )

    return [copy(n) for n in range(pl.cdiv(depth, STEP))]


def chunks_of(depth):
    steps = pl.cdiv(depth, STEP)
    count = pl.cdiv(steps, 3)
    edges = [steps * i // count for i in range(count + 1)]
    return list(zip(edges[:-1], edges[1:]))


def lift_pieces(pieces, weights, sums, gate, up, last):
    tile = tile_of(gate.shape[1])
    work = [
        (piece, weight, span)
        for piece, weight in zip(pieces, weights)
        for span in chunks_of(piece.shape[1])
    ]
    for number, (piece, (gate_rows, up_rows, gate_copies, up_copies), span) in enumerate(work):
        for n in range(*span):
            gate_copies[n].wait()
            up_copies[n].wait()
        at = pl.ds(span[0] * STEP, min(span[1] * STEP, piece.shape[1]) - span[0] * STEP)
        final = number == len(work) - 1
        before = sums if number == 0 else (gate, up)

        @pl.loop(0, gate.shape[1] // tile)
        def _(n):
            across = pl.ds(pl.multiple_of(n * tile, 128), tile)
            both = jnp.concatenate([gate_rows[at, across], up_rows[at, across]], axis=1)
            product = jnp.dot(piece[:, at], both, preferred_element_type=jnp.float32)
            g, u = product[:, :tile], product[:, tile:]
            if before is not None:
                g = g + before[0][:, across]
                u = u + before[1][:, across]
            if final and last is not None:
                last[:, across] = (g / (1.0 + jnp.exp(-g)) * u).astype(jnp.bfloat16)
            else:
                gate[:, across] = g
                up[:, across] = u


def drop_columns(hidden, weight, copies, out, start):
    for copy in copies:
        copy.wait()
    width = weight.shape[1]
    for at in range(0, width, 2 * LANES):
        end = min(at + 2 * LANES, width)
        value = jnp.dot(hidden[...], weight[:, at:end], preferred_element_type=jnp.float32)
        out[:, start + at : start + end] = value.astype(out.dtype)


def vmem():
    return pl.BlockSpec(memory_space=pltpu.VMEM)


def hbm():
    return pl.BlockSpec(memory_space=pl.ANY)


def buffer(depth, width):
    return [
        pltpu.VMEM((depth, width), jnp.bfloat16),
        pltpu.SemaphoreType.DMA((pl.cdiv(depth, STEP),)),
    ]


def start_lift(at, pieces, w_gate, w_up, scratch):
    weights = []
    for i, piece in enumerate(pieces):
        begin = pl.multiple_of(at[i], 128)
        rows = scratch[4 * i : 4 * i + 4]
        gate_copies = fetch(w_gate, begin, 0, rows[0], rows[1])
        up_copies = fetch(w_up, begin, 0, rows[2], rows[3])
        for one, other in zip(gate_copies, up_copies):
            one.start()
            other.start()
        weights.append((rows[0], rows[2], gate_copies, up_copies))
    return weights


def lift(piece, start, w_gate, w_up):
    rows, depth = piece.shape
    hidden = w_gate.shape[1]

    def kernel(at, piece, w_gate, w_up, gate, up, *scratch):
        weights = start_lift(at, [piece], w_gate, w_up, scratch)
        lift_pieces([piece], weights, None, gate, up, None)

    return pl.pallas_call(
        kernel,
        out_shape=[jax.ShapeDtypeStruct((rows, hidden), jnp.float32)] * 2,
        in_specs=[pl.BlockSpec(memory_space=pltpu.SMEM), vmem(), hbm(), hbm()],
        out_specs=[vmem(), vmem()],
        scratch_shapes=buffer(depth, hidden) * 2,
        compiler_params=pltpu.CompilerParams(vmem_limit_bytes=VMEM_BYTES),
        cost_estimate=pl.CostEstimate(
            flops=4 * rows * depth * hidden,
            bytes_accessed=4 * depth * hidden,
            transcendentals=0,
        ),
        name="lift",
    )(jnp.reshape(start, (1,)).astype(jnp.int32), piece, w_gate, w_up)


def finish(pieces, starts, w_gate, w_up, sums, w_down, columns, width):
    rows = pieces[0].shape[0]
    depth = sum(piece.shape[1] for piece in pieces)
    hidden = w_gate.shape[1]
    count = len(pieces)

    def kernel(at, *refs):
        given, refs = refs[:count], refs[count:]
        w_gate, w_up, w_down, gate, up, value, out = refs[:7]
        gate_sum, up_sum = refs[7:9]
        scratch = refs[9:]
        weights = start_lift(at, given, w_gate, w_up, scratch)
        scratch = scratch[4 * count :]
        downs = []
        for i in range(len(columns)):
            begin = pl.multiple_of(at[count + i], 128)
            copies = fetch(w_down, 0, begin, scratch[2 * i], scratch[2 * i + 1])
            for copy in copies:
                copy.start()
            downs.append(copies)
        lift_pieces(given, weights, (gate, up), gate_sum, up_sum, value)
        for i, copies in enumerate(downs):
            drop_columns(value, scratch[2 * i], copies, out, i * width)

    scratch = [pltpu.VMEM((rows, hidden), jnp.float32)] * 2
    for piece in pieces:
        scratch += buffer(piece.shape[1], hidden) * 2
    for _ in columns:
        scratch += buffer(hidden, width)
    return pl.pallas_call(
        kernel,
        out_shape=[
            jax.ShapeDtypeStruct((rows, hidden), jnp.bfloat16),
            jax.ShapeDtypeStruct((rows, len(columns) * width), jnp.bfloat16),
        ],
        in_specs=[pl.BlockSpec(memory_space=pltpu.SMEM)]
        + [vmem()] * count
        + [hbm()] * 3
        + [vmem()] * 2,
        out_specs=[vmem(), vmem()],
        scratch_shapes=scratch,
        compiler_params=pltpu.CompilerParams(vmem_limit_bytes=VMEM_BYTES - 10 * 1024 * 1024),
        cost_estimate=pl.CostEstimate(
            flops=4 * rows * depth * hidden + 2 * rows * hidden * len(columns) * width,
            bytes_accessed=4 * depth * hidden + 2 * hidden * len(columns) * width,
            transcendentals=rows * hidden,
        ),
        name="finish",
    )(
        jnp.stack(list(starts) + list(columns)).astype(jnp.int32),
        *pieces,
        w_gate,
        w_up,
        w_down,
        *sums,
    )


def drop(hidden, w_down, start, width, dtype):
    rows, depth = hidden.shape

    def kernel(at, hidden, w_down, out, weight, sems):
        copies = fetch(w_down, 0, pl.multiple_of(at[0], 128), weight, sems)
        for copy in copies:
            copy.start()
        drop_columns(hidden, weight, copies, out, 0)

    return pl.pallas_call(
        kernel,
        out_shape=jax.ShapeDtypeStruct((rows, width), dtype),
        in_specs=[pl.BlockSpec(memory_space=pltpu.SMEM), vmem(), hbm()],
        out_specs=vmem(),
        scratch_shapes=buffer(depth, width),
        compiler_params=pltpu.CompilerParams(vmem_limit_bytes=VMEM_BYTES),
        cost_estimate=pl.CostEstimate(
            flops=2 * rows * depth * width, bytes_accessed=2 * depth * width, transcendentals=0
        ),
        name="drop",
    )(jnp.reshape(start, (1,)).astype(jnp.int32), hidden, w_down)


def selectors(expert_ids, gate_probs, order):
    experts = order.shape[0]
    rows = expert_ids.shape[0]
    blocks = rows // BLOCK
    match = expert_ids.T[:, None, :] == order[None, :, None]
    named = jnp.any(match, axis=0)
    weight = jnp.sum(jnp.where(match, gate_probs.T[:, None, :], 0.0), axis=0)
    row = jnp.arange(rows, dtype=jnp.int32)
    same = row[:, None] // BLOCK == row[None, :] // BLOCK
    earlier = ((row[:, None] < row[None, :]) & same).astype(jnp.bfloat16)
    before = jnp.dot(named.astype(jnp.bfloat16), earlier, preferred_element_type=jnp.float32)
    place = before.astype(jnp.int32) + (row // BLOCK * CAP)[None, :]
    slots = jnp.arange(blocks * CAP, dtype=jnp.int32)
    hit = named[:, None, :] & (place[:, None, :] == slots[None, :, None])
    high = weight.astype(jnp.bfloat16)
    rest = weight - high.astype(jnp.float32)
    middle = rest.astype(jnp.bfloat16)
    low = (rest - middle.astype(jnp.float32)).astype(jnp.bfloat16)
    flat = (experts * blocks * CAP, rows)
    chosen = hit.astype(jnp.bfloat16).reshape(flat)
    weights = [
        jnp.where(hit, part[:, None, :], 0).astype(jnp.bfloat16).reshape(flat)
        for part in (high, middle, low)
    ]
    return chosen, weights


def flip(value, bits):
    size = lax.axis_size("expert")
    return lax.ppermute(value, "expert", [(i, i ^ bits) for i in range(size)])


def far_first(pairs):
    return list(range(pairs - 1, 0, -1))


def dispatch(even, odd, pairs):
    slots = even.shape[0] // pairs
    other = flip(odd, 1)

    def both(j):
        at = slice(j * slots, (j + 1) * slots)
        return jnp.concatenate([even[at], other[at]], axis=0)

    arrived = {j: flip(both(j), 2 * j) for j in far_first(pairs)}
    arrived[0] = both(0)
    return jnp.concatenate([arrived[j] for j in range(pairs)], axis=0)


def give_back(value, pairs):
    slots = value.shape[0] // (2 * pairs)

    def of(j):
        return value[2 * j * slots : 2 * (j + 1) * slots]

    arrived = {j: flip(of(j), 2 * j) for j in far_first(pairs)}
    arrived[0] = of(0)
    even = jnp.concatenate([arrived[j][:slots] for j in range(pairs)], axis=0)
    odd = jnp.concatenate([arrived[j][slots:] for j in range(pairs)], axis=0)
    return jnp.concatenate([even, flip(odd, 1)], axis=0)


def mix(weights, returned):
    return sum(
        lax.dot_general(
            w, returned, (((0,), (0,)), ((), ())), preferred_element_type=jnp.float32
        )
        for w in weights
    )


def on_device(tokens, expert_ids, gate_probs, w_gate, w_up, w_down):
    width = tokens.shape[1]
    experts = lax.axis_size("expert")
    ranks = lax.axis_size("tensor")
    me = lax.axis_index("tensor")
    w_gate = lax.all_gather(w_gate, "dp", axis=1, tiled=True)[0]
    w_up = lax.all_gather(w_up, "dp", axis=1, tiled=True)[0]
    w_down = lax.all_gather(w_down, "dp", axis=2, tiled=True)[0]
    pairs = experts // 2
    near = jnp.arange(experts, dtype=jnp.int32)
    near = jnp.where(near < pairs, 2 * near, 2 * (near - pairs) + 1)
    order = near ^ lax.axis_index("expert").astype(jnp.int32)
    chosen, weights = selectors(expert_ids, gate_probs, order)
    half = chosen.shape[0] // 2

    def rank_at(step):
        return lax.rem(me + step, ranks)

    def send_up(value, step):
        return lax.ppermute(value, "tensor", [(i, (i + step) % ranks) for i in range(ranks)])

    share = width // ranks
    shared = round(2 * share / 3 / LANES) * LANES
    direct_at = ranks * shared

    def placed(features):
        def rows_of(part):
            value = jnp.dot(part, features, preferred_element_type=jnp.float32)
            return value.astype(jnp.bfloat16)

        return dispatch(rows_of(chosen[:half]), rows_of(chosen[half:]), pairs)

    mine = lax.dynamic_slice_in_dim(tokens, me * shared, shared, axis=1)
    own = placed(mine)
    direct = placed(tokens[:, direct_at:])
    sums = lift(own, me * shared, w_gate, w_up)
    pieces, starts = [], []
    for step in range(1, ranks):
        pieces.append(send_up(own, ranks - step))
        starts.append(rank_at(step) * shared)
    pieces.append(direct)
    starts.append(jnp.int32(direct_at))
    reduced = round(share * 9 / 16 / 128) * 128
    early = share - reduced
    columns = [jnp.int32(rank * share) for rank in range(ranks)]
    hidden, partial = finish(pieces, starts, w_gate, w_up, sums, w_down, columns, early)
    returned = give_back(partial, pairs)
    owned = drop(hidden, w_down, me * share + early, reduced, jnp.float32)
    for step in range(1, ranks):
        sent = drop(hidden, w_down, rank_at(step) * share + early, reduced, jnp.bfloat16)
        owned = owned + send_up(sent, step).astype(jnp.float32)
    first = mix(weights, returned)

    def part_of(rank):
        return lax.dynamic_slice_in_dim(first, rank * early, early, axis=1)

    mixed = part_of(me)
    for step in range(1, ranks):
        mixed = mixed + send_up(part_of(rank_at(step)), step)
    late = mix(weights, give_back(owned.astype(jnp.bfloat16), pairs))
    return jnp.concatenate([mixed.astype(jnp.bfloat16), late.astype(jnp.bfloat16)], axis=1)


def solution(mesh):
    placed = (
        P(("groups", "dp", "expert"), None),
        P(("groups", "dp", "expert"), None),
        P(("groups", "dp", "expert"), None),
        P("expert", "dp", "tensor"),
        P("expert", "dp", "tensor"),
        P("expert", "tensor", "dp"),
    )
    return jax.shard_map(
        on_device,
        mesh=mesh,
        in_specs=placed,
        out_specs=P(("groups", "dp", "expert"), "tensor"),
        check_vma=False,
    )
```

```python
import jax
import jax.numpy as jnp
from jax import lax
from jax.experimental import pallas as pl
from jax.experimental.pallas import tpu as pltpu
from jax.sharding import PartitionSpec as P

BLOCK = 128
CAP = 24
LANES = 256
VMEM_BYTES = 50 * 1024 * 1024
CUTS = 3


def tile_of(width):
    for tile in (LANES, 128):
        if width % tile == 0:
            return tile
    return width


def tile_copies(tiles, copy):
    for n in range(tiles):
        copy(n).start()
    return copy


def span(n, tile):
    return pl.ds(pl.multiple_of(n * tile, 128), tile)


def fetch_rows(source, start, target, column, sems):
    tiles, depth, both = target.shape
    tile = both // 2
    return tile_copies(
        tiles,
        lambda n: pltpu.make_async_copy(
            source.at[pl.ds(start, depth), span(n, tile)],
            target.at[n, :, pl.ds(column, tile)],
            sems.at[n],
        ),
    )


def fetch_sums(source, target, sems):
    tiles, rows, tile = target.shape
    return tile_copies(
        tiles,
        lambda n: pltpu.make_async_copy(source.at[:, span(n, tile)], target.at[n], sems.at[n]),
    )


def fetch_columns(source, starts, width, target, sems):
    tiles, depth, tile = target.shape
    each = width // tile

    def copy(n):
        at = pl.multiple_of(starts[n // each] + (n % each) * tile, 128)
        return pltpu.make_async_copy(source.at[:, pl.ds(at, tile)], target.at[n], sems.at[n])

    return tile_copies(tiles, copy)


def drop_tiles(hidden, down_tiles, copy, out):
    tiles, depth, tile = down_tiles.shape
    for n in range(tiles):
        copy(n).wait()
        value = jnp.dot(hidden[...], down_tiles[n], preferred_element_type=jnp.float32)
        out[:, n * tile : (n + 1) * tile] = value.astype(out.dtype)


def vmem():
    return pl.BlockSpec(memory_space=pltpu.VMEM)


def hbm():
    return pl.BlockSpec(memory_space=pl.ANY)


def buffer(shape, dtype=jnp.bfloat16):
    return [pltpu.VMEM(shape, dtype), pltpu.SemaphoreType.DMA((shape[0],))]


def lift(piece, start, w_gate, w_up, sums=None, back=None):
    rows, depth = piece.shape
    hidden = w_gate.shape[1]
    tile = tile_of(hidden)
    tiles = hidden // tile
    given = [] if sums is None else list(sums)
    scalars = [start]
    scratch = buffer((tiles, depth, 2 * tile)) + [pltpu.SemaphoreType.DMA((tiles,))]
    for _ in given:
        scratch += buffer((tiles, rows, tile), jnp.float32)
    flops = 4 * rows * depth * hidden
    moved = 4 * depth * hidden + 16 * rows * hidden
    if back is None:
        for _ in range(2):
            scratch += buffer((tiles, rows, tile), jnp.float32)
        args = [piece, w_gate, w_up] + given
        out_shape = [jax.ShapeDtypeStruct((rows, hidden), jnp.float32)] * 2
        out_specs = [hbm(), hbm()]
    else:
        w_down, columns, width = back
        wide = tile_of(width)
        scratch += buffer((len(columns) * width // wide, hidden, wide))
        scalars += list(columns)
        args = [piece, w_gate, w_up] + given + [w_down]
        out_shape = [
            jax.ShapeDtypeStruct((rows, hidden), jnp.bfloat16),
            jax.ShapeDtypeStruct((rows, len(columns) * width), jnp.bfloat16),
        ]
        out_specs = [vmem(), vmem()]
        flops += 2 * rows * hidden * len(columns) * width
        moved += 2 * hidden * len(columns) * width

    def kernel(at, *refs):
        piece, w_gate, w_up = refs[:3]
        sums = refs[3 : 3 + len(given)]
        first, second = refs[len(args) : len(args) + 2]
        both, gate_sems, up_sems = refs[len(args) + 2 : len(args) + 5]
        extra = refs[len(args) + 5 :]
        begin = pl.multiple_of(at[0], 128)
        waits = [
            fetch_rows(w_gate, begin, both, 0, gate_sems),
            fetch_rows(w_up, begin, both, tile, up_sems),
        ]
        for i, source in enumerate(sums):
            waits.append(fetch_sums(source, extra[2 * i], extra[2 * i + 1]))
        before, extra = extra[: 2 * len(given) : 2], extra[2 * len(given) :]
        if back is not None:
            starts = [at[1 + i] for i in range(len(columns))]
            down = fetch_columns(refs[len(args) - 1], starts, width, extra[0], extra[1])

        def store(i, n):
            target = (first, second)[i]
            return pltpu.make_async_copy(
                extra[2 * i].at[n], target.at[:, span(n, tile)], extra[2 * i + 1].at[n]
            )

        @pl.loop(0, tiles)
        def _(n):
            for wait in waits:
                wait(n).wait()
            product = jnp.dot(piece[...], both[n], preferred_element_type=jnp.float32)
            gate, up = product[:, :tile], product[:, tile:]
            if given:
                gate = gate + before[0][n]
                up = up + before[1][n]
            if back is None:
                extra[0][n] = gate
                extra[2][n] = up
                store(0, n).start()
                store(1, n).start()
            else:
                silu = gate / (1.0 + jnp.exp(-gate))
                first[:, span(n, tile)] = (silu * up).astype(jnp.bfloat16)

        if back is None:
            for n in range(tiles):
                store(0, n).wait()
                store(1, n).wait()
        else:
            drop_tiles(first, extra[0], down, second)

    return pl.pallas_call(
        kernel,
        out_shape=out_shape,
        in_specs=[pl.BlockSpec(memory_space=pltpu.SMEM), vmem()] + [hbm()] * (len(args) - 1),
        out_specs=out_specs,
        scratch_shapes=scratch,
        compiler_params=pltpu.CompilerParams(vmem_limit_bytes=VMEM_BYTES),
        cost_estimate=pl.CostEstimate(
            flops=flops,
            bytes_accessed=moved,
            transcendentals=rows * hidden,
        ),
        name="lift",
    )(jnp.stack(scalars).astype(jnp.int32), *args)


def drop(hidden, w_down, start, width, dtype):
    rows, depth = hidden.shape
    tile = tile_of(width)

    def kernel(at, hidden, w_down, out, *scratch):
        copy = fetch_columns(w_down, [at[0]], width, scratch[0], scratch[1])
        drop_tiles(hidden, scratch[0], copy, out)

    return pl.pallas_call(
        kernel,
        out_shape=jax.ShapeDtypeStruct((rows, width), dtype),
        in_specs=[pl.BlockSpec(memory_space=pltpu.SMEM), vmem(), hbm()],
        out_specs=vmem(),
        scratch_shapes=buffer((width // tile, depth, tile)),
        compiler_params=pltpu.CompilerParams(vmem_limit_bytes=VMEM_BYTES),
        cost_estimate=pl.CostEstimate(
            flops=2 * rows * depth * width, bytes_accessed=2 * depth * width, transcendentals=0
        ),
        name="drop",
    )(jnp.reshape(start, (1,)).astype(jnp.int32), hidden, w_down)


def selectors(expert_ids, gate_probs, experts):
    rows = expert_ids.shape[0]
    blocks = rows // BLOCK
    match = expert_ids.T[:, None, :] == jnp.arange(experts, dtype=jnp.int32)[None, :, None]
    named = jnp.any(match, axis=0)
    weight = jnp.sum(jnp.where(match, gate_probs.T[:, None, :], 0.0), axis=0)
    row = jnp.arange(rows, dtype=jnp.int32)
    same = row[:, None] // BLOCK == row[None, :] // BLOCK
    earlier = ((row[:, None] < row[None, :]) & same).astype(jnp.bfloat16)
    before = jnp.dot(named.astype(jnp.bfloat16), earlier, preferred_element_type=jnp.float32)
    place = before.astype(jnp.int32) + (row // BLOCK * CAP)[None, :]
    slots = jnp.arange(blocks * CAP, dtype=jnp.int32)
    hit = named[:, None, :] & (place[:, None, :] == slots[None, :, None])
    high = weight.astype(jnp.bfloat16)
    rest = weight - high.astype(jnp.float32)
    middle = rest.astype(jnp.bfloat16)
    low = (rest - middle.astype(jnp.float32)).astype(jnp.bfloat16)
    flat = (experts * blocks * CAP, rows)
    chosen = hit.astype(jnp.bfloat16).reshape(flat)
    weights = [
        jnp.where(hit, part[:, None, :], 0).astype(jnp.bfloat16).reshape(flat)
        for part in (high, middle, low)
    ]
    return chosen, weights


def swap(value, experts):
    slots, width = value.shape
    return lax.all_to_all(
        value.reshape(experts, slots // experts, width),
        "expert",
        split_axis=0,
        concat_axis=0,
        tiled=True,
    ).reshape(slots, width)


def mix(weights, returned):
    return sum(
        lax.dot_general(
            w, returned, (((0,), (0,)), ((), ())), preferred_element_type=jnp.float32
        )
        for w in weights
    )


def on_device(tokens, expert_ids, gate_probs, w_gate, w_up, w_down):
    width = tokens.shape[1]
    experts = lax.axis_size("expert")
    ranks = lax.axis_size("tensor")
    me = lax.axis_index("tensor")
    w_gate = lax.all_gather(w_gate, "dp", axis=1, tiled=True)[0]
    w_up = lax.all_gather(w_up, "dp", axis=1, tiled=True)[0]
    w_down = lax.all_gather(w_down, "dp", axis=2, tiled=True)[0]
    chosen, weights = selectors(expert_ids, gate_probs, experts)

    def rank_at(step):
        return lax.rem(me + step, ranks)

    def send_up(value, step):
        return lax.ppermute(value, "tensor", [(i, (i + step) % ranks) for i in range(ranks)])

    share = width // ranks
    shared = share // 4 * 3
    direct_at = ranks * shared

    def placed(features):
        return jnp.dot(chosen, features, preferred_element_type=jnp.float32).astype(jnp.bfloat16)

    mine = lax.dynamic_slice_in_dim(tokens, me * shared, shared, axis=1)
    own = swap(placed(mine), experts)
    cut = shared // CUTS
    others = []
    for at in range(0, shared, cut):
        for step in range(1, ranks):
            sent = send_up(own[:, at : at + cut], ranks - step)
            others.append((sent, rank_at(step) * shared + at))
    direct = swap(placed(tokens[:, direct_at:]), experts)
    sums = lift(own, me * shared, w_gate, w_up)
    for piece, at in others[: 1 - ranks]:
        sums = lift(piece, at, w_gate, w_up, sums)
    sums = lift(direct, jnp.int32(direct_at), w_gate, w_up, sums)
    for piece, at in others[1 - ranks : -1]:
        sums = lift(piece, at, w_gate, w_up, sums)

    early = share // 8 * 3
    columns = [jnp.int32(rank * share) for rank in range(ranks)]
    piece, at = others[-1]
    hidden, partial = lift(piece, at, w_gate, w_up, sums, (w_down, columns, early))
    returned = swap(partial, experts)
    cut = pl.cdiv(share - early, 2 * LANES) * LANES
    owned = []
    for at in range(early, share, cut):
        cut = min(cut, share - at)
        arrived = [
            send_up(drop(hidden, w_down, rank_at(step) * share + at, cut, jnp.bfloat16), step)
            for step in range(1, ranks)
        ]
        value = drop(hidden, w_down, me * share + at, cut, jnp.float32)
        for other in arrived:
            value = value + other.astype(jnp.float32)
        owned.append(value.astype(jnp.bfloat16))
    returned, *owned = lax.optimization_barrier((returned, *owned))
    first = mix(weights, returned)

    def part_of(rank):
        return lax.dynamic_slice_in_dim(first, rank * early, early, axis=1)

    mixed = part_of(me)
    for step in range(1, ranks):
        mixed = mixed + send_up(part_of(rank_at(step)), step)
    late = mix(weights, swap(jnp.concatenate(owned, axis=1), experts))
    return jnp.concatenate([mixed.astype(jnp.bfloat16), late.astype(jnp.bfloat16)], axis=1)


def solution(mesh):
    placed = (
        P(("groups", "dp", "expert"), None),
        P(("groups", "dp", "expert"), None),
        P(("groups", "dp", "expert"), None),
        P("expert", "dp", "tensor"),
        P("expert", "dp", "tensor"),
        P("expert", "tensor", "dp"),
    )
    return jax.shard_map(
        on_device,
        mesh=mesh,
        in_specs=placed,
        out_specs=P(("groups", "dp", "expert"), "tensor"),
        check_vma=False,
    )
```

```python
import jax
import jax.numpy as jnp
from jax import lax
from jax.experimental import pallas as pl
from jax.experimental.pallas import tpu as pltpu
from jax.sharding import PartitionSpec as P

BLOCK = 128
CAP = 24
LANES = 256
VMEM_BYTES = 50 * 1024 * 1024


def tile_of(width, most=LANES):
    for tile in range(most, 127, -128):
        if width % tile == 0:
            return tile
    return width


def tile_copies(tiles, copy):
    for n in range(tiles):
        copy(n).start()
    return copy


def span(n, tile):
    return pl.ds(pl.multiple_of(n * tile, 128), tile)


def fetch_rows(source, start, target, row, depth, column, sems):
    tiles, _, both = target.shape
    tile = both // 2
    return tile_copies(
        tiles,
        lambda n: pltpu.make_async_copy(
            source.at[pl.ds(start, depth), span(n, tile)],
            target.at[n, pl.ds(row, depth), pl.ds(column, tile)],
            sems.at[n],
        ),
    )


def fetch_sums(source, target, sems):
    tiles, rows, tile = target.shape
    return tile_copies(
        tiles,
        lambda n: pltpu.make_async_copy(source.at[:, span(n, tile)], target.at[n], sems.at[n]),
    )


def fetch_columns(source, starts, width, target, sems):
    tiles, depth, tile = target.shape
    each = width // tile

    def copy(n):
        at = pl.multiple_of(starts[n // each] + (n % each) * tile, 128)
        return pltpu.make_async_copy(source.at[:, pl.ds(at, tile)], target.at[n], sems.at[n])

    return tile_copies(tiles, copy)


def drop_tiles(hidden, down_tiles, copy, out):
    tiles, depth, tile = down_tiles.shape
    for n in range(tiles):
        copy(n).wait()
        value = jnp.dot(hidden[...], down_tiles[n], preferred_element_type=jnp.float32)
        out[:, n * tile : (n + 1) * tile] = value.astype(out.dtype)


def vmem():
    return pl.BlockSpec(memory_space=pltpu.VMEM)


def hbm():
    return pl.BlockSpec(memory_space=pl.ANY)


def buffer(shape, dtype=jnp.bfloat16):
    return [pltpu.VMEM(shape, dtype), pltpu.SemaphoreType.DMA((shape[0],))]


def lift(pieces, starts, w_gate, w_up, sums=None, back=None):
    rows = pieces[0].shape[0]
    depths = [piece.shape[1] for piece in pieces]
    depth = sum(depths)
    count = len(pieces)
    hidden = w_gate.shape[1]
    tile = tile_of(hidden)
    tiles = hidden // tile
    given = [] if sums is None else list(sums)
    scalars = list(starts)
    scratch = [pltpu.VMEM((rows, depth), jnp.bfloat16)]
    scratch += [pltpu.VMEM((tiles, depth, 2 * tile), jnp.bfloat16)]
    scratch += [pltpu.SemaphoreType.DMA((tiles,))] * (2 * count)
    for _ in given:
        scratch += buffer((tiles, rows, tile), jnp.float32)
    flops = 4 * rows * depth * hidden
    moved = 4 * depth * hidden + 16 * rows * hidden
    if back is None:
        for _ in range(2):
            scratch += buffer((tiles, rows, tile), jnp.float32)
        args = [*pieces, w_gate, w_up] + given
        out_shape = [jax.ShapeDtypeStruct((rows, hidden), jnp.float32)] * 2
        out_specs = [hbm(), hbm()]
    else:
        w_down, columns, width = back
        wide = tile_of(width, 1024)
        scratch += buffer((len(columns) * width // wide, hidden, wide))
        scalars += list(columns)
        args = [*pieces, w_gate, w_up] + given + [w_down]
        out_shape = [
            jax.ShapeDtypeStruct((rows, hidden), jnp.bfloat16),
            jax.ShapeDtypeStruct((rows, len(columns) * width), jnp.bfloat16),
        ]
        out_specs = [vmem(), vmem()]
        flops += 2 * rows * hidden * len(columns) * width
        moved += 2 * hidden * len(columns) * width

    def kernel(at, *refs):
        parts, (w_gate, w_up) = refs[:count], refs[count : count + 2]
        sums = refs[count + 2 : count + 2 + len(given)]
        first, second = refs[len(args) : len(args) + 2]
        whole, both = refs[len(args) + 2 : len(args) + 4]
        sems = refs[len(args) + 4 : len(args) + 4 + 2 * count]
        extra = refs[len(args) + 4 + 2 * count :]
        waits = []
        row = 0
        for i, part in enumerate(parts):
            begin = pl.multiple_of(at[i], 128)
            for source, column, sem in ((w_gate, 0, sems[2 * i]), (w_up, tile, sems[2 * i + 1])):
                waits.append(fetch_rows(source, begin, both, row, depths[i], column, sem))
            row += depths[i]
        for i, source in enumerate(sums):
            waits.append(fetch_sums(source, extra[2 * i], extra[2 * i + 1]))
        before, extra = extra[: 2 * len(given) : 2], extra[2 * len(given) :]
        if back is not None:
            ranges = [at[count + i] for i in range(len(columns))]
            down = fetch_columns(refs[len(args) - 1], ranges, width, extra[0], extra[1])
        row = 0
        for part, size in zip(parts, depths):
            whole[:, row : row + size] = part[...]
            row += size

        def store(i, n):
            target = (first, second)[i]
            return pltpu.make_async_copy(
                extra[2 * i].at[n], target.at[:, span(n, tile)], extra[2 * i + 1].at[n]
            )

        @pl.loop(0, tiles)
        def _(n):
            for wait in waits:
                wait(n).wait()
            product = jnp.dot(whole[...], both[n], preferred_element_type=jnp.float32)
            gate, up = product[:, :tile], product[:, tile:]
            if given:
                gate = gate + before[0][n]
                up = up + before[1][n]
            if back is None:
                extra[0][n] = gate
                extra[2][n] = up
                store(0, n).start()
                store(1, n).start()
            else:
                silu = gate / (1.0 + jnp.exp(-gate))
                first[:, span(n, tile)] = (silu * up).astype(jnp.bfloat16)

        if back is None:
            for n in range(tiles):
                store(0, n).wait()
                store(1, n).wait()
        else:
            drop_tiles(first, extra[0], down, second)

    return pl.pallas_call(
        kernel,
        out_shape=out_shape,
        in_specs=[pl.BlockSpec(memory_space=pltpu.SMEM)]
        + [vmem()] * count
        + [hbm()] * (len(args) - count),
        out_specs=out_specs,
        scratch_shapes=scratch,
        compiler_params=pltpu.CompilerParams(vmem_limit_bytes=VMEM_BYTES),
        cost_estimate=pl.CostEstimate(
            flops=flops,
            bytes_accessed=moved,
            transcendentals=rows * hidden,
        ),
        name="lift",
    )(jnp.stack(scalars).astype(jnp.int32), *args)


def drop(hidden, w_down, start, width, dtype):
    rows, depth = hidden.shape
    tile = tile_of(width, 1024)

    def kernel(at, hidden, w_down, out, *scratch):
        copy = fetch_columns(w_down, [at[0]], width, scratch[0], scratch[1])
        drop_tiles(hidden, scratch[0], copy, out)

    return pl.pallas_call(
        kernel,
        out_shape=jax.ShapeDtypeStruct((rows, width), dtype),
        in_specs=[pl.BlockSpec(memory_space=pltpu.SMEM), vmem(), hbm()],
        out_specs=vmem(),
        scratch_shapes=buffer((width // tile, depth, tile)),
        compiler_params=pltpu.CompilerParams(vmem_limit_bytes=VMEM_BYTES),
        cost_estimate=pl.CostEstimate(
            flops=2 * rows * depth * width, bytes_accessed=2 * depth * width, transcendentals=0
        ),
        name="drop",
    )(jnp.reshape(start, (1,)).astype(jnp.int32), hidden, w_down)


def selectors(expert_ids, gate_probs, experts):
    rows = expert_ids.shape[0]
    blocks = rows // BLOCK
    match = expert_ids.T[:, None, :] == jnp.arange(experts, dtype=jnp.int32)[None, :, None]
    named = jnp.any(match, axis=0)
    weight = jnp.sum(jnp.where(match, gate_probs.T[:, None, :], 0.0), axis=0)
    row = jnp.arange(rows, dtype=jnp.int32)
    same = row[:, None] // BLOCK == row[None, :] // BLOCK
    earlier = ((row[:, None] < row[None, :]) & same).astype(jnp.bfloat16)
    before = jnp.dot(named.astype(jnp.bfloat16), earlier, preferred_element_type=jnp.float32)
    place = before.astype(jnp.int32) + (row // BLOCK * CAP)[None, :]
    slots = jnp.arange(blocks * CAP, dtype=jnp.int32)
    hit = named[:, None, :] & (place[:, None, :] == slots[None, :, None])
    high = weight.astype(jnp.bfloat16)
    rest = weight - high.astype(jnp.float32)
    middle = rest.astype(jnp.bfloat16)
    low = (rest - middle.astype(jnp.float32)).astype(jnp.bfloat16)
    flat = (experts * blocks * CAP, rows)
    chosen = hit.astype(jnp.bfloat16).reshape(flat)
    weights = [
        jnp.where(hit, part[:, None, :], 0).astype(jnp.bfloat16).reshape(flat)
        for part in (high, middle, low)
    ]
    return chosen, weights


def swap(value, experts):
    slots, width = value.shape
    return lax.all_to_all(
        value.reshape(experts, slots // experts, width),
        "expert",
        split_axis=0,
        concat_axis=0,
        tiled=True,
    ).reshape(slots, width)


def mix(weights, returned):
    return sum(
        lax.dot_general(
            w, returned, (((0,), (0,)), ((), ())), preferred_element_type=jnp.float32
        )
        for w in weights
    )


def on_device(tokens, expert_ids, gate_probs, w_gate, w_up, w_down):
    width = tokens.shape[1]
    experts = lax.axis_size("expert")
    ranks = lax.axis_size("tensor")
    me = lax.axis_index("tensor")
    w_gate = lax.all_gather(w_gate, "dp", axis=1, tiled=True)[0]
    w_up = lax.all_gather(w_up, "dp", axis=1, tiled=True)[0]
    w_down = lax.all_gather(w_down, "dp", axis=2, tiled=True)[0]
    chosen, weights = selectors(expert_ids, gate_probs, experts)

    def rank_at(step):
        return lax.rem(me + step, ranks)

    def send_up(value, step):
        return lax.ppermute(value, "tensor", [(i, (i + step) % ranks) for i in range(ranks)])

    share = width // ranks
    shared = round(share * 5 / 8 / LANES) * LANES
    direct_at = ranks * shared

    def placed(features):
        return jnp.dot(chosen, features, preferred_element_type=jnp.float32).astype(jnp.bfloat16)

    mine = lax.dynamic_slice_in_dim(tokens, me * shared, shared, axis=1)
    own = swap(placed(mine), experts)
    cut = pl.cdiv(shared, 2 * LANES) * LANES
    others = []
    for begin, end in ((0, cut), (cut, shared)):
        for step in range(1, ranks):
            sent = send_up(own[:, begin:end], ranks - step)
            others.append((sent, rank_at(step) * shared + begin))
    direct = swap(placed(tokens[:, direct_at:]), experts)
    sums = lift([own], [me * shared], w_gate, w_up)
    for piece, at in others[:-1]:
        sums = lift([piece], [at], w_gate, w_up, sums)

    early = round(share * 7 / 16 / 128) * 128
    columns = [jnp.int32(rank * share) for rank in range(ranks)]
    last, last_at = others[-1]
    hidden, partial = lift(
        [last, direct],
        [last_at, jnp.int32(direct_at)],
        w_gate,
        w_up,
        sums,
        (w_down, columns, early),
    )
    returned = swap(partial, experts)
    edges = [early, early + pl.cdiv(share - early, 256) * 128, share]
    owned = []
    for at, end in zip(edges[:-1], edges[1:]):
        cut = end - at
        arrived = [
            send_up(drop(hidden, w_down, rank_at(step) * share + at, cut, jnp.bfloat16), step)
            for step in range(1, ranks)
        ]
        value = drop(hidden, w_down, me * share + at, cut, jnp.float32)
        for other in arrived:
            value = value + other.astype(jnp.float32)
        owned.append(value.astype(jnp.bfloat16))
    returned, *owned = lax.optimization_barrier((returned, *owned))
    first = mix(weights, returned)

    def part_of(rank):
        return lax.dynamic_slice_in_dim(first, rank * early, early, axis=1)

    mixed = part_of(me)
    for step in range(1, ranks):
        mixed = mixed + send_up(part_of(rank_at(step)), step)
    late = mix(weights, swap(jnp.concatenate(owned, axis=1), experts))
    return jnp.concatenate([mixed.astype(jnp.bfloat16), late.astype(jnp.bfloat16)], axis=1)


def solution(mesh):
    placed = (
        P(("groups", "dp", "expert"), None),
        P(("groups", "dp", "expert"), None),
        P(("groups", "dp", "expert"), None),
        P("expert", "dp", "tensor"),
        P("expert", "dp", "tensor"),
        P("expert", "tensor", "dp"),
    )
    return jax.shard_map(
        on_device,
        mesh=mesh,
        in_specs=placed,
        out_specs=P(("groups", "dp", "expert"), "tensor"),
        check_vma=False,
    )
```

```python
import jax
import jax.numpy as jnp
from jax import lax
from jax.experimental import pallas as pl
from jax.experimental.pallas import tpu as pltpu
from jax.sharding import PartitionSpec as P

BLOCK = 128
CAP = 24
LANES = 256
VMEM_BYTES = 50 * 1024 * 1024


def tile_of(width, most=LANES):
    for tile in range(most, 127, -128):
        if width % tile == 0:
            return tile
    return width


def vmem():
    return pl.BlockSpec(memory_space=pltpu.VMEM)


def hbm():
    return pl.BlockSpec(memory_space=pl.ANY)


def dma(count):
    return pltpu.SemaphoreType.DMA((count,))


def in_turn(groups, ahead):
    for group in groups[:ahead]:
        for copy in group:
            copy.start()
    left = iter(range(len(groups)))

    def wait():
        now = next(left)
        if now + ahead < len(groups):
            for copy in groups[now + ahead]:
                copy.start()
        for copy in groups[now]:
            copy.wait()

    return wait


def column_groups(source, starts, width, target, sems):
    tiles, depth, tile = target.shape
    each = width // tile
    groups = []
    for n in range(tiles):
        at = pl.multiple_of(starts[n // each] + (n % each) * tile, 128)
        groups.append(
            [pltpu.make_async_copy(source.at[:, pl.ds(at, tile)], target.at[n], sems.at[n])]
        )
    return groups


def drop_tile(hidden, tiles, n, out):
    tile = tiles.shape[2]
    value = jnp.dot(hidden[...], tiles[n], preferred_element_type=jnp.float32)
    out[:, n * tile : (n + 1) * tile] = value.astype(out.dtype)


def lift(pieces, starts, w_gate, w_up, sums=None, back=None):
    rows = pieces[0].shape[0]
    depths = [piece.shape[1] for piece in pieces]
    depth = sum(depths)
    count = len(pieces)
    hidden = w_gate.shape[1]
    tile = tile_of(hidden)
    tiles = hidden // tile
    given = [] if sums is None else [sums]
    scalars = list(starts)
    args = [*pieces, w_gate, w_up, *given]
    scratch = [
        pltpu.VMEM((rows, depth), jnp.bfloat16),
        pltpu.VMEM((tiles, depth, 2 * tile), jnp.bfloat16),
        pltpu.VMEM((tiles, rows, 2 * tile), jnp.float32),
    ]
    scratch += [dma(tiles)] * (2 * count + 2)
    flops = 4 * rows * depth * hidden
    moved = 4 * depth * hidden + 16 * rows * hidden
    if back is None:
        out_shape = [jax.ShapeDtypeStruct((tiles, rows, 2 * tile), jnp.float32)]
        out_specs = [hbm()]
    else:
        w_down, columns, width = back
        wide = tile_of(width, 1024)
        drops = len(columns) * width // wide
        scratch += [pltpu.VMEM((drops, hidden, wide), jnp.bfloat16), dma(drops)]
        scalars += list(columns)
        args += [w_down]
        out_shape = [
            jax.ShapeDtypeStruct((rows, hidden), jnp.bfloat16),
            jax.ShapeDtypeStruct((rows, len(columns) * width), jnp.bfloat16),
        ]
        out_specs = [vmem(), vmem()]
        flops += 2 * rows * hidden * len(columns) * width
        moved += 2 * hidden * len(columns) * width

    def kernel(at, *refs):
        parts, refs = refs[:count], refs[count:]
        (gate_from, up_from), refs = refs[:2], refs[2:]
        before, refs = refs[: len(given)], refs[len(given) :]
        more = len(args) - count - 2 - len(given)
        down_from, refs = refs[:more], refs[more:]
        outs, refs = refs[: len(out_shape)], refs[len(out_shape) :]
        whole, both, totals = refs[:3]
        sems, (sum_sems, out_sems) = refs[3 : 3 + 2 * count], refs[3 + 2 * count : 5 + 2 * count]
        groups = []
        for n in range(tiles):
            across = pl.ds(n * tile, tile)
            group = []
            row = 0
            for i, size in enumerate(depths):
                begin = pl.multiple_of(at[i], 128)
                for side, source in enumerate((gate_from, up_from)):
                    group.append(
                        pltpu.make_async_copy(
                            source.at[pl.ds(begin, size), across],
                            both.at[n, pl.ds(row, size), pl.ds(side * tile, tile)],
                            sems[2 * i + side].at[n],
                        )
                    )
                row += size
            for source in before:
                group.append(
                    pltpu.make_async_copy(source.at[n], totals.at[n], sum_sems.at[n])
                )
            groups.append(group)
        if back is not None:
            ranges = [at[count + i] for i in range(len(columns))]
            groups += column_groups(down_from[0], ranges, width, refs[-2], refs[-1])
        wait = in_turn(groups, 2)
        row = 0
        for part, size in zip(parts, depths):
            whole[:, row : row + size] = part[...]
            row += size

        def store(n):
            return pltpu.make_async_copy(totals.at[n], outs[0].at[n], out_sems.at[n])

        def settle(n, product):
            if given:
                product = product + totals[n]
            if back is None:
                totals[n] = product
                store(n).start()
            else:
                gate, up = product[:, :tile], product[:, tile:]
                value = gate / (1.0 + jnp.exp(-gate)) * up
                outs[0][:, n * tile : (n + 1) * tile] = value.astype(jnp.bfloat16)

        held = None
        for n in range(tiles):
            wait()
            product = jnp.dot(whole[...], both[n], preferred_element_type=jnp.float32)
            if held is not None:
                settle(n - 1, held)
            held = product
        settle(tiles - 1, held)
        if back is None:
            for n in range(tiles):
                store(n).wait()
        else:
            for n in range(drops):
                wait()
                drop_tile(outs[0], refs[-2], n, outs[1])

    return pl.pallas_call(
        kernel,
        out_shape=out_shape,
        in_specs=[pl.BlockSpec(memory_space=pltpu.SMEM)]
        + [vmem()] * count
        + [hbm()] * (len(args) - count),
        out_specs=out_specs,
        scratch_shapes=scratch,
        compiler_params=pltpu.CompilerParams(vmem_limit_bytes=VMEM_BYTES),
        cost_estimate=pl.CostEstimate(
            flops=flops,
            bytes_accessed=moved,
            transcendentals=rows * hidden,
        ),
        name="lift",
    )(jnp.stack(scalars).astype(jnp.int32), *args)


def drop(hidden, w_down, start, width, dtype):
    rows, depth = hidden.shape
    tile = tile_of(width, 1024)

    def kernel(at, hidden, w_down, out, weight, sems):
        wait = in_turn(column_groups(w_down, [at[0]], width, weight, sems), 2)
        for n in range(width // tile):
            wait()
            drop_tile(hidden, weight, n, out)

    return pl.pallas_call(
        kernel,
        out_shape=jax.ShapeDtypeStruct((rows, width), dtype),
        in_specs=[pl.BlockSpec(memory_space=pltpu.SMEM), vmem(), hbm()],
        out_specs=vmem(),
        scratch_shapes=[
            pltpu.VMEM((width // tile, depth, tile), jnp.bfloat16),
            dma(width // tile),
        ],
        compiler_params=pltpu.CompilerParams(vmem_limit_bytes=VMEM_BYTES),
        cost_estimate=pl.CostEstimate(
            flops=2 * rows * depth * width, bytes_accessed=2 * depth * width, transcendentals=0
        ),
        name="drop",
    )(jnp.reshape(start, (1,)).astype(jnp.int32), hidden, w_down)


def selectors(expert_ids, gate_probs, experts):
    rows = expert_ids.shape[0]
    blocks = rows // BLOCK
    match = expert_ids.T[:, None, :] == jnp.arange(experts, dtype=jnp.int32)[None, :, None]
    named = jnp.any(match, axis=0)
    weight = jnp.sum(jnp.where(match, gate_probs.T[:, None, :], 0.0), axis=0)
    row = jnp.arange(rows, dtype=jnp.int32)
    same = row[:, None] // BLOCK == row[None, :] // BLOCK
    earlier = ((row[:, None] < row[None, :]) & same).astype(jnp.bfloat16)
    before = jnp.dot(named.astype(jnp.bfloat16), earlier, preferred_element_type=jnp.float32)
    place = before.astype(jnp.int32) + (row // BLOCK * CAP)[None, :]
    slots = jnp.arange(blocks * CAP, dtype=jnp.int32)
    hit = named[:, None, :] & (place[:, None, :] == slots[None, :, None])
    high = weight.astype(jnp.bfloat16)
    rest = weight - high.astype(jnp.float32)
    middle = rest.astype(jnp.bfloat16)
    low = (rest - middle.astype(jnp.float32)).astype(jnp.bfloat16)
    flat = (experts * blocks * CAP, rows)
    chosen = hit.astype(jnp.bfloat16).reshape(flat)
    weights = [
        jnp.where(hit, part[:, None, :], 0).astype(jnp.bfloat16).reshape(flat)
        for part in (high, middle, low)
    ]
    return chosen, weights


def swap(value, experts):
    slots, width = value.shape
    return lax.all_to_all(
        value.reshape(experts, slots // experts, width),
        "expert",
        split_axis=0,
        concat_axis=0,
        tiled=True,
    ).reshape(slots, width)


def mix(weights, returned):
    return sum(
        lax.dot_general(
            w, returned, (((0,), (0,)), ((), ())), preferred_element_type=jnp.float32
        )
        for w in weights
    )


def on_device(tokens, expert_ids, gate_probs, w_gate, w_up, w_down):
    width = tokens.shape[1]
    experts = lax.axis_size("expert")
    ranks = lax.axis_size("tensor")
    me = lax.axis_index("tensor")
    w_gate = lax.all_gather(w_gate, "dp", axis=1, tiled=True)[0]
    w_up = lax.all_gather(w_up, "dp", axis=1, tiled=True)[0]
    w_down = lax.all_gather(w_down, "dp", axis=2, tiled=True)[0]
    chosen, weights = selectors(expert_ids, gate_probs, experts)

    def rank_at(step):
        return lax.rem(me + step, ranks)

    def send_up(value, step):
        return lax.ppermute(value, "tensor", [(i, (i + step) % ranks) for i in range(ranks)])

    share = width // ranks
    shared = round(share * 5 / 8 / LANES) * LANES
    direct_at = ranks * shared

    def placed(features):
        return jnp.dot(chosen, features, preferred_element_type=jnp.float32).astype(jnp.bfloat16)

    mine = lax.dynamic_slice_in_dim(tokens, me * shared, shared, axis=1)
    own = swap(placed(mine), experts)
    cut = pl.cdiv(shared, 2 * LANES) * LANES
    others = []
    for begin, end in ((0, cut), (cut, shared)):
        for step in range(1, ranks):
            sent = send_up(own[:, begin:end], ranks - step)
            others.append((sent, rank_at(step) * shared + begin))
    direct = swap(placed(tokens[:, direct_at:]), experts)
    (sums,) = lift([own], [me * shared], w_gate, w_up)
    for piece, at in others[:-1]:
        (sums,) = lift([piece], [at], w_gate, w_up, sums)

    early = round(share * 7 / 16 / 128) * 128
    columns = [jnp.int32(rank * share) for rank in range(ranks)]
    last, last_at = others[-1]
    hidden, partial = lift(
        [last, direct],
        [last_at, jnp.int32(direct_at)],
        w_gate,
        w_up,
        sums,
        (w_down, columns, early),
    )
    returned = swap(partial, experts)
    edges = [early, early + pl.cdiv(share - early, 256) * 128, share]
    owned = []
    for at, end in zip(edges[:-1], edges[1:]):
        cut = end - at
        arrived = [
            send_up(drop(hidden, w_down, rank_at(step) * share + at, cut, jnp.bfloat16), step)
            for step in range(1, ranks)
        ]
        value = drop(hidden, w_down, me * share + at, cut, jnp.float32)
        for other in arrived:
            value = value + other.astype(jnp.float32)
        owned.append(value.astype(jnp.bfloat16))
    returned, *owned = lax.optimization_barrier((returned, *owned))
    first = mix(weights, returned)

    def part_of(rank):
        return lax.dynamic_slice_in_dim(first, rank * early, early, axis=1)

    mixed = part_of(me)
    for step in range(1, ranks):
        mixed = mixed + send_up(part_of(rank_at(step)), step)
    late = mix(weights, swap(jnp.concatenate(owned, axis=1), experts))
    return jnp.concatenate([mixed.astype(jnp.bfloat16), late.astype(jnp.bfloat16)], axis=1)


def solution(mesh):
    placed = (
        P(("groups", "dp", "expert"), None),
        P(("groups", "dp", "expert"), None),
        P(("groups", "dp", "expert"), None),
        P("expert", "dp", "tensor"),
        P("expert", "dp", "tensor"),
        P("expert", "tensor", "dp"),
    )
    return jax.shard_map(
        on_device,
        mesh=mesh,
        in_specs=placed,
        out_specs=P(("groups", "dp", "expert"), "tensor"),
        check_vma=False,
    )
```

```python
import jax
import jax.numpy as jnp
from jax import lax
from jax.experimental import pallas as pl
from jax.experimental.pallas import tpu as pltpu
from jax.sharding import PartitionSpec as P

BLOCK = 128
CAP = 24
LANES = 256
VMEM_BYTES = 50 * 1024 * 1024


def tile_of(width, most=LANES):
    for tile in range(most, 127, -128):
        if width % tile == 0:
            return tile
    return width


def vmem():
    return pl.BlockSpec(memory_space=pltpu.VMEM)


def hbm():
    return pl.BlockSpec(memory_space=pl.ANY)


def dma(count):
    return pltpu.SemaphoreType.DMA((count,))


def in_turn(groups, ahead):
    for group in groups[:ahead]:
        for copy in group:
            copy.start()
    left = iter(range(len(groups)))

    def wait():
        now = next(left)
        if now + ahead < len(groups):
            for copy in groups[now + ahead]:
                copy.start()
        for copy in groups[now]:
            copy.wait()

    return wait


def column_groups(source, starts, width, target, sems):
    tiles, depth, tile = target.shape
    each = width // tile
    groups = []
    for n in range(tiles):
        at = pl.multiple_of(starts[n // each] + (n % each) * tile, 128)
        groups.append(
            [pltpu.make_async_copy(source.at[:, pl.ds(at, tile)], target.at[n], sems.at[n])]
        )
    return groups


def drop_tile(hidden, tiles, n, out):
    tile = tiles.shape[2]
    value = jnp.dot(hidden[...], tiles[n], preferred_element_type=jnp.float32)
    out[:, n * tile : (n + 1) * tile] = value.astype(out.dtype)


def lift(pieces, starts, w_gate, w_up, sums=None, back=None):
    rows = pieces[0].shape[0]
    depths = [piece.shape[1] for piece in pieces]
    depth = sum(depths)
    count = len(pieces)
    hidden = w_gate.shape[1]
    tile = tile_of(hidden)
    tiles = hidden // tile
    given = [] if sums is None else [sums]
    scalars = list(starts)
    args = [*pieces, w_gate, w_up, *given]
    scratch = [
        pltpu.VMEM((rows, depth), jnp.bfloat16),
        pltpu.VMEM((tiles, depth, 2 * tile), jnp.bfloat16),
        pltpu.VMEM((tiles, rows, 2 * tile), jnp.float32),
    ]
    scratch += [dma(tiles)] * (2 * count + 2)
    flops = 4 * rows * depth * hidden
    moved = 4 * depth * hidden + 16 * rows * hidden
    if back is None:
        out_shape = [jax.ShapeDtypeStruct((tiles, rows, 2 * tile), jnp.float32)]
        out_specs = [hbm()]
    else:
        w_down, columns, width = back
        wide = tile_of(width, 1024)
        drops = len(columns) * width // wide
        scratch += [pltpu.VMEM((drops, hidden, wide), jnp.bfloat16), dma(drops)]
        scalars += list(columns)
        args += [w_down]
        out_shape = [
            jax.ShapeDtypeStruct((rows, hidden), jnp.bfloat16),
            jax.ShapeDtypeStruct((rows, len(columns) * width), jnp.bfloat16),
        ]
        out_specs = [vmem(), vmem()]
        flops += 2 * rows * hidden * len(columns) * width
        moved += 2 * hidden * len(columns) * width

    def kernel(at, *refs):
        parts, refs = refs[:count], refs[count:]
        (gate_from, up_from), refs = refs[:2], refs[2:]
        before, refs = refs[: len(given)], refs[len(given) :]
        more = len(args) - count - 2 - len(given)
        down_from, refs = refs[:more], refs[more:]
        outs, refs = refs[: len(out_shape)], refs[len(out_shape) :]
        whole, both, totals = refs[:3]
        sems, (sum_sems, out_sems) = refs[3 : 3 + 2 * count], refs[3 + 2 * count : 5 + 2 * count]
        groups = []
        for n in range(tiles):
            across = pl.ds(n * tile, tile)
            group = []
            row = 0
            for i, size in enumerate(depths):
                begin = pl.multiple_of(at[i], 128)
                for side, source in enumerate((gate_from, up_from)):
                    group.append(
                        pltpu.make_async_copy(
                            source.at[pl.ds(begin, size), across],
                            both.at[n, pl.ds(row, size), pl.ds(side * tile, tile)],
                            sems[2 * i + side].at[n],
                        )
                    )
                row += size
            for source in before:
                group.append(
                    pltpu.make_async_copy(source.at[n], totals.at[n], sum_sems.at[n])
                )
            groups.append(group)
        if back is not None:
            ranges = [at[count + i] for i in range(len(columns))]
            groups += column_groups(down_from[0], ranges, width, refs[-2], refs[-1])
        wait = in_turn(groups, 2)
        row = 0
        for part, size in zip(parts, depths):
            whole[:, row : row + size] = part[...]
            row += size

        def store(n):
            return pltpu.make_async_copy(totals.at[n], outs[0].at[n], out_sems.at[n])

        def settle(n, product):
            if given:
                product = product + totals[n]
            if back is None:
                totals[n] = product
                store(n).start()
            else:
                gate, up = product[:, :tile], product[:, tile:]
                value = gate / (1.0 + jnp.exp(-gate)) * up
                outs[0][:, n * tile : (n + 1) * tile] = value.astype(jnp.bfloat16)

        held = None
        for n in range(tiles):
            wait()
            product = jnp.dot(whole[...], both[n], preferred_element_type=jnp.float32)
            if held is not None:
                settle(n - 1, held)
            held = product
        settle(tiles - 1, held)
        if back is None:
            for n in range(tiles):
                store(n).wait()
        else:
            for n in range(drops):
                wait()
                drop_tile(outs[0], refs[-2], n, outs[1])

    return pl.pallas_call(
        kernel,
        out_shape=out_shape,
        in_specs=[pl.BlockSpec(memory_space=pltpu.SMEM)]
        + [vmem()] * count
        + [hbm()] * (len(args) - count),
        out_specs=out_specs,
        scratch_shapes=scratch,
        compiler_params=pltpu.CompilerParams(vmem_limit_bytes=VMEM_BYTES),
        cost_estimate=pl.CostEstimate(
            flops=flops,
            bytes_accessed=moved,
            transcendentals=rows * hidden,
        ),
        name="lift",
    )(jnp.stack(scalars).astype(jnp.int32), *args)


def drop(hidden, w_down, start, width, dtype):
    rows, depth = hidden.shape
    tile = tile_of(width, 1024)

    def kernel(at, hidden, w_down, out, weight, sems):
        wait = in_turn(column_groups(w_down, [at[0]], width, weight, sems), 2)
        for n in range(width // tile):
            wait()
            drop_tile(hidden, weight, n, out)

    return pl.pallas_call(
        kernel,
        out_shape=jax.ShapeDtypeStruct((rows, width), dtype),
        in_specs=[pl.BlockSpec(memory_space=pltpu.SMEM), vmem(), hbm()],
        out_specs=vmem(),
        scratch_shapes=[
            pltpu.VMEM((width // tile, depth, tile), jnp.bfloat16),
            dma(width // tile),
        ],
        compiler_params=pltpu.CompilerParams(vmem_limit_bytes=VMEM_BYTES),
        cost_estimate=pl.CostEstimate(
            flops=2 * rows * depth * width, bytes_accessed=2 * depth * width, transcendentals=0
        ),
        name="drop",
    )(jnp.reshape(start, (1,)).astype(jnp.int32), hidden, w_down)


def selectors(expert_ids, gate_probs, order):
    experts = order.shape[0]
    rows = expert_ids.shape[0]
    blocks = rows // BLOCK
    match = expert_ids.T[:, None, :] == order[None, :, None]
    named = jnp.any(match, axis=0)
    weight = jnp.sum(jnp.where(match, gate_probs.T[:, None, :], 0.0), axis=0)
    row = jnp.arange(rows, dtype=jnp.int32)
    same = row[:, None] // BLOCK == row[None, :] // BLOCK
    earlier = ((row[:, None] < row[None, :]) & same).astype(jnp.bfloat16)
    before = jnp.dot(named.astype(jnp.bfloat16), earlier, preferred_element_type=jnp.float32)
    place = before.astype(jnp.int32) + (row // BLOCK * CAP)[None, :]
    slots = jnp.arange(blocks * CAP, dtype=jnp.int32)
    hit = named[:, None, :] & (place[:, None, :] == slots[None, :, None])
    high = weight.astype(jnp.bfloat16)
    rest = weight - high.astype(jnp.float32)
    middle = rest.astype(jnp.bfloat16)
    low = (rest - middle.astype(jnp.float32)).astype(jnp.bfloat16)
    flat = (experts * blocks * CAP, rows)
    chosen = hit.astype(jnp.bfloat16).reshape(flat)
    weights = [
        jnp.where(hit, part[:, None, :], 0).astype(jnp.bfloat16).reshape(flat)
        for part in (high, middle, low)
    ]
    return chosen, weights


def swap(value, experts):
    slots, width = value.shape
    return lax.all_to_all(
        value.reshape(experts, slots // experts, width),
        "expert",
        split_axis=0,
        concat_axis=0,
        tiled=True,
    ).reshape(slots, width)


def flip(value, bits):
    size = lax.axis_size("expert")
    return lax.ppermute(value, "expert", [(i, i ^ bits) for i in range(size)])


def near_order(experts):
    place = jnp.arange(experts, dtype=jnp.int32)
    pairs = experts // 2
    apart = jnp.where(place < pairs, 2 * place, 2 * (place - pairs) + 1)
    return apart ^ lax.axis_index("expert").astype(jnp.int32)


def send_pairs(value, experts):
    pairs = experts // 2
    rows = value.shape[0] // pairs
    pair = lax.axis_index("expert") // 2

    def of(j):
        return lax.dynamic_slice_in_dim(value, (pair ^ j) * rows, rows, axis=0)

    arrived = {j: flip(of(j), 2 * j) for j in range(pairs - 1, 0, -1)}
    arrived[0] = of(0)
    return [arrived[j] for j in range(pairs)]


def split_pairs(arrived):
    pairs = len(arrived)
    both, width = arrived[0].shape
    slots = both // 2

    def kernel(core, *refs):
        pieces, (mine, other) = refs[:pairs], refs[pairs:]
        first = core[0] == 0
        for j in range(0, pairs, 2):
            values = [piece[...].astype(jnp.float32) for piece in pieces[j : j + 2]]
            top = jnp.concatenate([value[:slots] for value in values], axis=0)
            bottom = jnp.concatenate([value[slots:] for value in values], axis=0)
            at = slice(j * slots, (j + 2) * slots)
            mine[at] = jnp.where(first, top, bottom).astype(jnp.bfloat16)
            other[at] = jnp.where(first, bottom, top).astype(jnp.bfloat16)

    core = lax.axis_index("expert").astype(jnp.int32) % 2
    mine, other = pl.pallas_call(
        kernel,
        out_shape=[jax.ShapeDtypeStruct((pairs * slots, width), jnp.bfloat16)] * 2,
        in_specs=[pl.BlockSpec(memory_space=pltpu.SMEM)] + [vmem()] * pairs,
        out_specs=[vmem(), vmem()],
        compiler_params=pltpu.CompilerParams(vmem_limit_bytes=VMEM_BYTES // 2),
        cost_estimate=pl.CostEstimate(
            flops=2 * pairs * both * width,
            bytes_accessed=4 * pairs * both * width,
            transcendentals=0,
        ),
        name="split_pairs",
    )(core.reshape(1), *arrived)
    return mine, flip(other, 1)


def mix(weights, returned):
    return sum(
        lax.dot_general(
            w, returned, (((0,), (0,)), ((), ())), preferred_element_type=jnp.float32
        )
        for w in weights
    )


def on_device(tokens, expert_ids, gate_probs, w_gate, w_up, w_down):
    width = tokens.shape[1]
    experts = lax.axis_size("expert")
    ranks = lax.axis_size("tensor")
    me = lax.axis_index("tensor")
    w_gate = lax.all_gather(w_gate, "dp", axis=1, tiled=True)[0]
    w_up = lax.all_gather(w_up, "dp", axis=1, tiled=True)[0]
    w_down = lax.all_gather(w_down, "dp", axis=2, tiled=True)[0]
    chosen, weights = selectors(expert_ids, gate_probs, jnp.arange(experts, dtype=jnp.int32))
    near_weights = selectors(expert_ids, gate_probs, near_order(experts))[1]

    def rank_at(step):
        return lax.rem(me + step, ranks)

    def send_up(value, step):
        return lax.ppermute(value, "tensor", [(i, (i + step) % ranks) for i in range(ranks)])

    share = width // ranks
    shared = round(share * 5 / 8 / LANES) * LANES
    direct_at = ranks * shared

    def placed(features):
        return jnp.dot(chosen, features, preferred_element_type=jnp.float32).astype(jnp.bfloat16)

    mine = lax.dynamic_slice_in_dim(tokens, me * shared, shared, axis=1)
    own = swap(placed(mine), experts)
    cut = pl.cdiv(shared, 2 * LANES) * LANES
    others = []
    for begin, end in ((0, cut), (cut, shared)):
        for step in range(1, ranks):
            sent = send_up(own[:, begin:end], ranks - step)
            others.append((sent, rank_at(step) * shared + begin))
    direct = swap(placed(tokens[:, direct_at:]), experts)
    (sums,) = lift([own], [me * shared], w_gate, w_up)
    for piece, at in others[:-1]:
        (sums,) = lift([piece], [at], w_gate, w_up, sums)

    early = round(share * 3 / 8 / 128) * 128
    columns = [jnp.int32(rank * share) for rank in range(ranks)]
    last, last_at = others[-1]
    hidden, partial = lift(
        [last, direct],
        [last_at, jnp.int32(direct_at)],
        w_gate,
        w_up,
        sums,
        (w_down, columns, early),
    )
    arrived = send_pairs(partial, experts)
    edges = [early, early + pl.cdiv(share - early, 256) * 128, share]
    owned = []
    for at, end in zip(edges[:-1], edges[1:]):
        cut = end - at
        received = [
            send_up(drop(hidden, w_down, rank_at(step) * share + at, cut, jnp.bfloat16), step)
            for step in range(1, ranks)
        ]
        value = drop(hidden, w_down, me * share + at, cut, jnp.float32)
        for other in received:
            value = value + other.astype(jnp.float32)
        owned.append(value.astype(jnp.bfloat16))
    arrived, owned = lax.optimization_barrier((arrived, owned))
    mine, passed = split_pairs(arrived)
    half = mine.shape[0]
    first = mix([w[:half] for w in near_weights], mine)
    first = first + mix([w[half:] for w in near_weights], passed)

    def part_of(rank):
        return lax.dynamic_slice_in_dim(first, rank * early, early, axis=1)

    mixed = part_of(me)
    for step in range(1, ranks):
        mixed = mixed + send_up(part_of(rank_at(step)), step)
    late = mix(weights, swap(jnp.concatenate(owned, axis=1), experts))
    return jnp.concatenate([mixed.astype(jnp.bfloat16), late.astype(jnp.bfloat16)], axis=1)


def solution(mesh):
    placed = (
        P(("groups", "dp", "expert"), None),
        P(("groups", "dp", "expert"), None),
        P(("groups", "dp", "expert"), None),
        P("expert", "dp", "tensor"),
        P("expert", "dp", "tensor"),
        P("expert", "tensor", "dp"),
    )
    return jax.shard_map(
        on_device,
        mesh=mesh,
        in_specs=placed,
        out_specs=P(("groups", "dp", "expert"), "tensor"),
        check_vma=False,
    )
```

```python
import jax
import jax.numpy as jnp
from jax import lax
from jax.experimental import pallas as pl
from jax.experimental.pallas import tpu as pltpu
from jax.sharding import PartitionSpec as P

TOP = 2
BLOCK = 128
CAP = 24
LANES = 256
VMEM_BYTES = 50 * 1024 * 1024


def tile_of(width, most=LANES):
    for tile in range(most, 127, -128):
        if width % tile == 0:
            return tile
    return width


def vmem():
    return pl.BlockSpec(memory_space=pltpu.VMEM)


def hbm():
    return pl.BlockSpec(memory_space=pl.ANY)


def dma(count):
    return pltpu.SemaphoreType.DMA((count,))


def in_turn(groups, ahead):
    for group in groups[:ahead]:
        for copy in group:
            copy.start()
    left = iter(range(len(groups)))

    def wait():
        now = next(left)
        if now + ahead < len(groups):
            for copy in groups[now + ahead]:
                copy.start()
        for copy in groups[now]:
            copy.wait()

    return wait


def column_groups(source, starts, width, target, sems):
    tiles, depth, tile = target.shape
    each = width // tile
    groups = []
    for n in range(tiles):
        at = pl.multiple_of(starts[n // each] + (n % each) * tile, 128)
        groups.append(
            [pltpu.make_async_copy(source.at[:, pl.ds(at, tile)], target.at[n], sems.at[n])]
        )
    return groups


def drop_tile(hidden, tiles, n, out):
    tile = tiles.shape[2]
    value = jnp.dot(hidden[...], tiles[n], preferred_element_type=jnp.float32)
    out[:, n * tile : (n + 1) * tile] = value.astype(out.dtype)


def lift(pieces, starts, w_gate, w_up, sums=None, back=None):
    rows = pieces[0].shape[0]
    depths = [piece.shape[1] for piece in pieces]
    depth = sum(depths)
    count = len(pieces)
    hidden = w_gate.shape[1]
    tile = tile_of(hidden)
    tiles = hidden // tile
    given = [] if sums is None else [sums]
    scalars = list(starts)
    args = [*pieces, w_gate, w_up, *given]
    scratch = [
        pltpu.VMEM((rows, depth), jnp.bfloat16),
        pltpu.VMEM((tiles, depth, 2 * tile), jnp.bfloat16),
        pltpu.VMEM((tiles, rows, 2 * tile), jnp.float32),
    ]
    scratch += [dma(tiles)] * (2 * count + 2)
    flops = 4 * rows * depth * hidden
    moved = 4 * depth * hidden + 16 * rows * hidden
    if back is None:
        out_shape = [jax.ShapeDtypeStruct((tiles, rows, 2 * tile), jnp.float32)]
        out_specs = [hbm()]
    else:
        w_down, columns, width = back
        wide = tile_of(width, 1024)
        drops = len(columns) * width // wide
        scratch += [pltpu.VMEM((drops, hidden, wide), jnp.bfloat16), dma(drops)]
        scalars += list(columns)
        args += [w_down]
        out_shape = [
            jax.ShapeDtypeStruct((rows, hidden), jnp.bfloat16),
            jax.ShapeDtypeStruct((rows, len(columns) * width), jnp.bfloat16),
        ]
        out_specs = [vmem(), vmem()]
        flops += 2 * rows * hidden * len(columns) * width
        moved += 2 * hidden * len(columns) * width

    def kernel(at, *refs):
        parts, refs = refs[:count], refs[count:]
        (gate_from, up_from), refs = refs[:2], refs[2:]
        before, refs = refs[: len(given)], refs[len(given) :]
        more = len(args) - count - 2 - len(given)
        down_from, refs = refs[:more], refs[more:]
        outs, refs = refs[: len(out_shape)], refs[len(out_shape) :]
        whole, both, totals = refs[:3]
        sems, (sum_sems, out_sems) = refs[3 : 3 + 2 * count], refs[3 + 2 * count : 5 + 2 * count]
        groups = []
        for n in range(tiles):
            across = pl.ds(n * tile, tile)
            group = []
            row = 0
            for i, size in enumerate(depths):
                begin = pl.multiple_of(at[i], 128)
                for side, source in enumerate((gate_from, up_from)):
                    group.append(
                        pltpu.make_async_copy(
                            source.at[pl.ds(begin, size), across],
                            both.at[n, pl.ds(row, size), pl.ds(side * tile, tile)],
                            sems[2 * i + side].at[n],
                        )
                    )
                row += size
            for source in before:
                group.append(
                    pltpu.make_async_copy(source.at[n], totals.at[n], sum_sems.at[n])
                )
            groups.append(group)
        if back is not None:
            ranges = [at[count + i] for i in range(len(columns))]
            groups += column_groups(down_from[0], ranges, width, refs[-2], refs[-1])
        wait = in_turn(groups, 2)
        row = 0
        for part, size in zip(parts, depths):
            whole[:, row : row + size] = part[...]
            row += size

        def store(n):
            return pltpu.make_async_copy(totals.at[n], outs[0].at[n], out_sems.at[n])

        def settle(n, product):
            if given:
                product = product + totals[n]
            if back is None:
                totals[n] = product
                store(n).start()
            else:
                gate, up = product[:, :tile], product[:, tile:]
                value = gate / (1.0 + jnp.exp(-gate)) * up
                outs[0][:, n * tile : (n + 1) * tile] = value.astype(jnp.bfloat16)

        held = None
        for n in range(tiles):
            wait()
            product = jnp.dot(whole[...], both[n], preferred_element_type=jnp.float32)
            if held is not None:
                settle(n - 1, held)
            held = product
        settle(tiles - 1, held)
        if back is None:
            for n in range(tiles):
                store(n).wait()
        else:
            for n in range(drops):
                wait()
                drop_tile(outs[0], refs[-2], n, outs[1])

    return pl.pallas_call(
        kernel,
        out_shape=out_shape,
        in_specs=[pl.BlockSpec(memory_space=pltpu.SMEM)]
        + [vmem()] * count
        + [hbm()] * (len(args) - count),
        out_specs=out_specs,
        scratch_shapes=scratch,
        compiler_params=pltpu.CompilerParams(vmem_limit_bytes=VMEM_BYTES),
        cost_estimate=pl.CostEstimate(
            flops=flops,
            bytes_accessed=moved,
            transcendentals=rows * hidden,
        ),
        name="lift",
    )(jnp.stack(scalars).astype(jnp.int32), *args)


def drop(hidden, w_down, start, width, dtype):
    rows, depth = hidden.shape
    tile = tile_of(width, 1024)

    def kernel(at, hidden, w_down, out, weight, sems):
        wait = in_turn(column_groups(w_down, [at[0]], width, weight, sems), 2)
        for n in range(width // tile):
            wait()
            drop_tile(hidden, weight, n, out)

    return pl.pallas_call(
        kernel,
        out_shape=jax.ShapeDtypeStruct((rows, width), dtype),
        in_specs=[pl.BlockSpec(memory_space=pltpu.SMEM), vmem(), hbm()],
        out_specs=vmem(),
        scratch_shapes=[
            pltpu.VMEM((width // tile, depth, tile), jnp.bfloat16),
            dma(width // tile),
        ],
        compiler_params=pltpu.CompilerParams(vmem_limit_bytes=VMEM_BYTES),
        cost_estimate=pl.CostEstimate(
            flops=2 * rows * depth * width, bytes_accessed=2 * depth * width, transcendentals=0
        ),
        name="drop",
    )(jnp.reshape(start, (1,)).astype(jnp.int32), hidden, w_down)


def selectors(expert_ids, gate_probs, experts):
    rows = expert_ids.shape[0]
    blocks = rows // BLOCK
    match = expert_ids.T[:, None, :] == jnp.arange(experts, dtype=jnp.int32)[None, :, None]
    named = jnp.any(match, axis=0)
    weight = jnp.sum(jnp.where(match, gate_probs.T[:, None, :], 0.0), axis=0)
    row = jnp.arange(rows, dtype=jnp.int32)
    same = row[:, None] // BLOCK == row[None, :] // BLOCK
    earlier = ((row[:, None] < row[None, :]) & same).astype(jnp.bfloat16)
    before = jnp.dot(named.astype(jnp.bfloat16), earlier, preferred_element_type=jnp.float32)
    place = before.astype(jnp.int32) + (row // BLOCK * CAP)[None, :]
    slots = jnp.arange(blocks * CAP, dtype=jnp.int32)
    hit = named[:, None, :] & (place[:, None, :] == slots[None, :, None])
    high = weight.astype(jnp.bfloat16)
    rest = weight - high.astype(jnp.float32)
    middle = rest.astype(jnp.bfloat16)
    low = (rest - middle.astype(jnp.float32)).astype(jnp.bfloat16)
    flat = (experts * blocks * CAP, rows)
    return [
        jnp.where(hit, part[:, None, :], 0).astype(jnp.bfloat16).reshape(flat)
        for part in (high, middle, low)
    ]


def place(tokens, expert_ids, experts, start, width):
    rows = tokens.shape[0]
    slots = rows // BLOCK * CAP

    def kernel(at, ids, tokens, chosen, out, part, picked, sem):
        begin = pl.multiple_of(at[0], 128)
        copy = pltpu.make_async_copy(tokens.at[:, pl.ds(begin, width)], part, sem)
        copy.start()
        expert = lax.broadcasted_iota(jnp.int32, (experts, rows), 0)
        named = jnp.zeros((experts, rows), jnp.float32)
        for k in range(TOP):
            named = named + jnp.where(ids[k : k + 1] == expert, 1.0, 0.0)
        row = lax.broadcasted_iota(jnp.int32, (rows, rows), 0)
        later = lax.broadcasted_iota(jnp.int32, (rows, rows), 1)
        same = row // BLOCK == later // BLOCK
        earlier = jnp.where((row < later) & same, 1.0, 0.0).astype(jnp.bfloat16)
        before = jnp.dot(
            named.astype(jnp.bfloat16), earlier, preferred_element_type=jnp.float32
        ).astype(jnp.int32)
        block = lax.broadcasted_iota(jnp.int32, (experts, rows), 1) // BLOCK
        where = jnp.where(named > 0.0, before + block * CAP, -1)
        slot = lax.broadcasted_iota(jnp.int32, (slots, rows), 0)
        for e in range(experts):
            picked[e * slots : (e + 1) * slots] = jnp.where(where[e : e + 1] == slot, 1.0, 0.0)
        chosen[...] = picked[...].astype(jnp.bfloat16)
        copy.wait()
        value = jnp.dot(chosen[...], part[...], preferred_element_type=jnp.float32)
        out[...] = value.astype(jnp.bfloat16)

    return pl.pallas_call(
        kernel,
        out_shape=[
            jax.ShapeDtypeStruct((experts * slots, rows), jnp.bfloat16),
            jax.ShapeDtypeStruct((experts * slots, width), jnp.bfloat16),
        ],
        in_specs=[pl.BlockSpec(memory_space=pltpu.SMEM), vmem(), hbm()],
        out_specs=[vmem(), vmem()],
        scratch_shapes=[
            pltpu.VMEM((rows, width), jnp.bfloat16),
            pltpu.VMEM((experts * slots, rows), jnp.float32),
            pltpu.SemaphoreType.DMA,
        ],
        compiler_params=pltpu.CompilerParams(vmem_limit_bytes=VMEM_BYTES // 2),
        cost_estimate=pl.CostEstimate(
            flops=2 * experts * slots * rows * width,
            bytes_accessed=2 * rows * width,
            transcendentals=0,
        ),
        name="place",
    )(jnp.reshape(start, (1,)).astype(jnp.int32), expert_ids.T, tokens)


def swap(value, experts):
    slots, width = value.shape
    return lax.all_to_all(
        value.reshape(experts, slots // experts, width),
        "expert",
        split_axis=0,
        concat_axis=0,
        tiled=True,
    ).reshape(slots, width)


def mix(weights, returned):
    return sum(
        lax.dot_general(
            w, returned, (((0,), (0,)), ((), ())), preferred_element_type=jnp.float32
        )
        for w in weights
    )


def on_device(tokens, expert_ids, gate_probs, w_gate, w_up, w_down):
    width = tokens.shape[1]
    experts = lax.axis_size("expert")
    ranks = lax.axis_size("tensor")
    me = lax.axis_index("tensor")
    w_gate = lax.all_gather(w_gate, "dp", axis=1, tiled=True)[0]
    w_up = lax.all_gather(w_up, "dp", axis=1, tiled=True)[0]
    w_down = lax.all_gather(w_down, "dp", axis=2, tiled=True)[0]
    weights = selectors(expert_ids, gate_probs, experts)

    def rank_at(step):
        return lax.rem(me + step, ranks)

    def send_up(value, step):
        return lax.ppermute(value, "tensor", [(i, (i + step) % ranks) for i in range(ranks)])

    share = width // ranks
    shared = round(share * 5 / 8 / LANES) * LANES
    direct_at = ranks * shared

    chosen, placed = place(tokens, expert_ids, experts, me * shared, shared)
    own = swap(placed, experts)
    cut = pl.cdiv(shared, 2 * LANES) * LANES
    others = []
    for begin, end in ((0, cut), (cut, shared)):
        for step in range(1, ranks):
            sent = send_up(own[:, begin:end], ranks - step)
            others.append((sent, rank_at(step) * shared + begin))
    placed = jnp.dot(chosen, tokens[:, direct_at:], preferred_element_type=jnp.float32)
    direct = swap(placed.astype(jnp.bfloat16), experts)
    (sums,) = lift([own], [me * shared], w_gate, w_up)
    for piece, at in others[:-1]:
        (sums,) = lift([piece], [at], w_gate, w_up, sums)

    early = round(share * 7 / 16 / 128) * 128
    columns = [jnp.int32(rank * share) for rank in range(ranks)]
    last, last_at = others[-1]
    hidden, partial = lift(
        [last, direct],
        [last_at, jnp.int32(direct_at)],
        w_gate,
        w_up,
        sums,
        (w_down, columns, early),
    )
    returned = swap(partial, experts)
    edges = [early, early + pl.cdiv(share - early, 256) * 128, share]
    owned = []
    for at, end in zip(edges[:-1], edges[1:]):
        cut = end - at
        arrived = [
            send_up(drop(hidden, w_down, rank_at(step) * share + at, cut, jnp.bfloat16), step)
            for step in range(1, ranks)
        ]
        value = drop(hidden, w_down, me * share + at, cut, jnp.float32)
        for other in arrived:
            value = value + other.astype(jnp.float32)
        owned.append(value.astype(jnp.bfloat16))
    returned, owned = lax.optimization_barrier((returned, jnp.concatenate(owned, axis=1)))
    first = mix(weights, returned)

    def part_of(rank):
        return lax.dynamic_slice_in_dim(first, rank * early, early, axis=1)

    mixed = part_of(me)
    for step in range(1, ranks):
        mixed = mixed + send_up(part_of(rank_at(step)), step)
    late = mix(weights, swap(owned, experts))
    return jnp.concatenate([mixed.astype(jnp.bfloat16), late.astype(jnp.bfloat16)], axis=1)


def solution(mesh):
    placed = (
        P(("groups", "dp", "expert"), None),
        P(("groups", "dp", "expert"), None),
        P(("groups", "dp", "expert"), None),
        P("expert", "dp", "tensor"),
        P("expert", "dp", "tensor"),
        P("expert", "tensor", "dp"),
    )
    return jax.shard_map(
        on_device,
        mesh=mesh,
        in_specs=placed,
        out_specs=P(("groups", "dp", "expert"), "tensor"),
        check_vma=False,
    )
```

```python
import jax
import jax.numpy as jnp
from jax import lax
from jax.experimental import pallas as pl
from jax.experimental.pallas import tpu as pltpu
from jax.sharding import PartitionSpec as P

TOP = 2
BLOCK = 128
CAP = 24
LANES = 256
VMEM_BYTES = 50 * 1024 * 1024


def tile_of(width, most=LANES):
    for tile in range(most, 127, -128):
        if width % tile == 0:
            return tile
    return width


def vmem():
    return pl.BlockSpec(memory_space=pltpu.VMEM)


def hbm():
    return pl.BlockSpec(memory_space=pl.ANY)


def dma(count):
    return pltpu.SemaphoreType.DMA((count,))


def in_turn(groups, ahead):
    for group in groups[:ahead]:
        for copy in group:
            copy.start()
    left = iter(range(len(groups)))

    def wait():
        now = next(left)
        if now + ahead < len(groups):
            for copy in groups[now + ahead]:
                copy.start()
        for copy in groups[now]:
            copy.wait()

    return wait


def column_groups(source, starts, width, target, sems):
    tiles, depth, tile = target.shape
    each = width // tile
    groups = []
    for n in range(tiles):
        at = pl.multiple_of(starts[n // each] + (n % each) * tile, 128)
        groups.append(
            [pltpu.make_async_copy(source.at[:, pl.ds(at, tile)], target.at[n], sems.at[n])]
        )
    return groups


def drop_tile(hidden, tiles, n, out):
    tile = tiles.shape[2]
    value = jnp.dot(hidden[...], tiles[n], preferred_element_type=jnp.float32)
    out[:, n * tile : (n + 1) * tile] = value.astype(out.dtype)


def lift(pieces, starts, w_gate, w_up, sums=None, back=None):
    rows = pieces[0].shape[0]
    depths = [piece.shape[1] for piece in pieces]
    depth = sum(depths)
    count = len(pieces)
    hidden = w_gate.shape[1]
    tile = tile_of(hidden)
    tiles = hidden // tile
    given = [] if sums is None else [sums]
    scalars = list(starts)
    args = [*pieces, w_gate, w_up, *given]
    scratch = [
        pltpu.VMEM((rows, depth), jnp.bfloat16),
        pltpu.VMEM((tiles, depth, 2 * tile), jnp.bfloat16),
        pltpu.VMEM((tiles, rows, 2 * tile), jnp.float32),
    ]
    scratch += [dma(tiles)] * (2 * count + 2)
    flops = 4 * rows * depth * hidden
    moved = 4 * depth * hidden + 16 * rows * hidden
    if back is None:
        out_shape = [jax.ShapeDtypeStruct((tiles, rows, 2 * tile), jnp.float32)]
        out_specs = [hbm()]
    else:
        w_down, columns, width = back
        wide = tile_of(width, 1024)
        drops = len(columns) * width // wide
        scratch += [pltpu.VMEM((drops, hidden, wide), jnp.bfloat16), dma(drops)]
        scalars += list(columns)
        args += [w_down]
        out_shape = [
            jax.ShapeDtypeStruct((rows, hidden), jnp.bfloat16),
            jax.ShapeDtypeStruct((rows, len(columns) * width), jnp.bfloat16),
        ]
        out_specs = [vmem(), vmem()]
        flops += 2 * rows * hidden * len(columns) * width
        moved += 2 * hidden * len(columns) * width

    def kernel(at, *refs):
        parts, refs = refs[:count], refs[count:]
        (gate_from, up_from), refs = refs[:2], refs[2:]
        before, refs = refs[: len(given)], refs[len(given) :]
        more = len(args) - count - 2 - len(given)
        down_from, refs = refs[:more], refs[more:]
        outs, refs = refs[: len(out_shape)], refs[len(out_shape) :]
        whole, both, totals = refs[:3]
        sems, (sum_sems, out_sems) = refs[3 : 3 + 2 * count], refs[3 + 2 * count : 5 + 2 * count]
        groups = []
        for n in range(tiles):
            across = pl.ds(n * tile, tile)
            group = []
            row = 0
            for i, size in enumerate(depths):
                begin = pl.multiple_of(at[i], 128)
                for side, source in enumerate((gate_from, up_from)):
                    group.append(
                        pltpu.make_async_copy(
                            source.at[pl.ds(begin, size), across],
                            both.at[n, pl.ds(row, size), pl.ds(side * tile, tile)],
                            sems[2 * i + side].at[n],
                        )
                    )
                row += size
            for source in before:
                group.append(
                    pltpu.make_async_copy(source.at[n], totals.at[n], sum_sems.at[n])
                )
            groups.append(group)
        if back is not None:
            ranges = [at[count + i] for i in range(len(columns))]
            groups += column_groups(down_from[0], ranges, width, refs[-2], refs[-1])
        wait = in_turn(groups, 2)
        row = 0
        for part, size in zip(parts, depths):
            whole[:, row : row + size] = part[...]
            row += size

        def store(n):
            return pltpu.make_async_copy(totals.at[n], outs[0].at[n], out_sems.at[n])

        def settle(n, product):
            if given:
                product = product + totals[n]
            if back is None:
                totals[n] = product
                store(n).start()
            else:
                gate, up = product[:, :tile], product[:, tile:]
                value = gate / (1.0 + jnp.exp(-gate)) * up
                outs[0][:, n * tile : (n + 1) * tile] = value.astype(jnp.bfloat16)

        held = None
        for n in range(tiles):
            wait()
            product = jnp.dot(whole[...], both[n], preferred_element_type=jnp.float32)
            if held is not None:
                settle(n - 1, held)
            held = product
        settle(tiles - 1, held)
        if back is None:
            for n in range(tiles):
                store(n).wait()
        else:
            for n in range(drops):
                wait()
                drop_tile(outs[0], refs[-2], n, outs[1])

    return pl.pallas_call(
        kernel,
        out_shape=out_shape,
        in_specs=[pl.BlockSpec(memory_space=pltpu.SMEM)]
        + [vmem()] * count
        + [hbm()] * (len(args) - count),
        out_specs=out_specs,
        scratch_shapes=scratch,
        compiler_params=pltpu.CompilerParams(vmem_limit_bytes=VMEM_BYTES),
        cost_estimate=pl.CostEstimate(
            flops=flops,
            bytes_accessed=moved,
            transcendentals=rows * hidden,
        ),
        name="lift",
    )(jnp.stack(scalars).astype(jnp.int32), *args)


def drop(hidden, w_down, start, width, dtype):
    rows, depth = hidden.shape
    tile = tile_of(width, 1024)

    def kernel(at, hidden, w_down, out, weight, sems):
        wait = in_turn(column_groups(w_down, [at[0]], width, weight, sems), 2)
        for n in range(width // tile):
            wait()
            drop_tile(hidden, weight, n, out)

    return pl.pallas_call(
        kernel,
        out_shape=jax.ShapeDtypeStruct((rows, width), dtype),
        in_specs=[pl.BlockSpec(memory_space=pltpu.SMEM), vmem(), hbm()],
        out_specs=vmem(),
        scratch_shapes=[
            pltpu.VMEM((width // tile, depth, tile), jnp.bfloat16),
            dma(width // tile),
        ],
        compiler_params=pltpu.CompilerParams(vmem_limit_bytes=VMEM_BYTES),
        cost_estimate=pl.CostEstimate(
            flops=2 * rows * depth * width, bytes_accessed=2 * depth * width, transcendentals=0
        ),
        name="drop",
    )(jnp.reshape(start, (1,)).astype(jnp.int32), hidden, w_down)


def selectors(expert_ids, gate_probs, experts):
    rows = expert_ids.shape[0]
    blocks = rows // BLOCK
    match = expert_ids.T[:, None, :] == jnp.arange(experts, dtype=jnp.int32)[None, :, None]
    named = jnp.any(match, axis=0)
    weight = jnp.sum(jnp.where(match, gate_probs.T[:, None, :], 0.0), axis=0)
    row = jnp.arange(rows, dtype=jnp.int32)
    same = row[:, None] // BLOCK == row[None, :] // BLOCK
    earlier = ((row[:, None] < row[None, :]) & same).astype(jnp.bfloat16)
    before = jnp.dot(named.astype(jnp.bfloat16), earlier, preferred_element_type=jnp.float32)
    place = before.astype(jnp.int32) + (row // BLOCK * CAP)[None, :]
    slots = jnp.arange(blocks * CAP, dtype=jnp.int32)
    hit = named[:, None, :] & (place[:, None, :] == slots[None, :, None])
    high = weight.astype(jnp.bfloat16)
    rest = weight - high.astype(jnp.float32)
    middle = rest.astype(jnp.bfloat16)
    low = (rest - middle.astype(jnp.float32)).astype(jnp.bfloat16)
    flat = (experts * blocks * CAP, rows)
    return [
        jnp.where(hit, part[:, None, :], 0).astype(jnp.bfloat16).reshape(flat)
        for part in (high, middle, low)
    ]


def place(tokens, expert_ids, experts, start, width):
    rows = tokens.shape[0]
    slots = rows // BLOCK * CAP

    def kernel(at, ids, tokens, chosen, out, part, picked, sem):
        begin = pl.multiple_of(at[0], 128)
        copy = pltpu.make_async_copy(tokens.at[:, pl.ds(begin, width)], part, sem)
        copy.start()
        expert = lax.broadcasted_iota(jnp.int32, (experts, rows), 0)
        named = jnp.zeros((experts, rows), jnp.float32)
        for k in range(TOP):
            named = named + jnp.where(ids[k : k + 1] == expert, 1.0, 0.0)
        row = lax.broadcasted_iota(jnp.int32, (rows, rows), 0)
        later = lax.broadcasted_iota(jnp.int32, (rows, rows), 1)
        same = row // BLOCK == later // BLOCK
        earlier = jnp.where((row < later) & same, 1.0, 0.0).astype(jnp.bfloat16)
        before = jnp.dot(
            named.astype(jnp.bfloat16), earlier, preferred_element_type=jnp.float32
        ).astype(jnp.int32)
        block = lax.broadcasted_iota(jnp.int32, (experts, rows), 1) // BLOCK
        where = jnp.where(named > 0.0, before + block * CAP, -1)
        slot = lax.broadcasted_iota(jnp.int32, (slots, rows), 0)
        for e in range(experts):
            picked[e * slots : (e + 1) * slots] = jnp.where(where[e : e + 1] == slot, 1.0, 0.0)
        chosen[...] = picked[...].astype(jnp.bfloat16)
        copy.wait()
        value = jnp.dot(chosen[...], part[...], preferred_element_type=jnp.float32)
        out[...] = value.astype(jnp.bfloat16)

    return pl.pallas_call(
        kernel,
        out_shape=[
            jax.ShapeDtypeStruct((experts * slots, rows), jnp.bfloat16),
            jax.ShapeDtypeStruct((experts * slots, width), jnp.bfloat16),
        ],
        in_specs=[pl.BlockSpec(memory_space=pltpu.SMEM), vmem(), hbm()],
        out_specs=[vmem(), vmem()],
        scratch_shapes=[
            pltpu.VMEM((rows, width), jnp.bfloat16),
            pltpu.VMEM((experts * slots, rows), jnp.float32),
            pltpu.SemaphoreType.DMA,
        ],
        compiler_params=pltpu.CompilerParams(vmem_limit_bytes=VMEM_BYTES // 2),
        cost_estimate=pl.CostEstimate(
            flops=2 * experts * slots * rows * width,
            bytes_accessed=2 * rows * width,
            transcendentals=0,
        ),
        name="place",
    )(jnp.reshape(start, (1,)).astype(jnp.int32), expert_ids.T, tokens)


def swap(value, experts):
    slots, width = value.shape
    return lax.all_to_all(
        value.reshape(experts, slots // experts, width),
        "expert",
        split_axis=0,
        concat_axis=0,
        tiled=True,
    ).reshape(slots, width)


def mix(weights, returned):
    return sum(
        lax.dot_general(
            w, returned, (((0,), (0,)), ((), ())), preferred_element_type=jnp.float32
        )
        for w in weights
    )


def on_device(tokens, expert_ids, gate_probs, w_gate, w_up, w_down):
    width = tokens.shape[1]
    experts = lax.axis_size("expert")
    ranks = lax.axis_size("tensor")
    me = lax.axis_index("tensor")
    w_gate = lax.all_gather(w_gate, "dp", axis=1, tiled=True)[0]
    w_up = lax.all_gather(w_up, "dp", axis=1, tiled=True)[0]
    w_down = lax.all_gather(w_down, "dp", axis=2, tiled=True)[0]
    weights = selectors(expert_ids, gate_probs, experts)

    def rank_at(step):
        return lax.rem(me + step, ranks)

    def send_up(value, step):
        return lax.ppermute(value, "tensor", [(i, (i + step) % ranks) for i in range(ranks)])

    share = width // ranks
    shared = round(share * 5 / 8 / LANES) * LANES
    direct_at = ranks * shared

    chosen, placed = place(tokens, expert_ids, experts, me * shared, shared)
    later = jnp.dot(chosen, tokens[:, direct_at:], preferred_element_type=jnp.float32)
    placed, later = lax.optimization_barrier((placed, later.astype(jnp.bfloat16)))
    own = swap(placed, experts)
    cut = pl.cdiv(shared, 2 * LANES) * LANES
    others = []
    for begin, end in ((0, cut), (cut, shared)):
        for step in range(1, ranks):
            sent = send_up(own[:, begin:end], ranks - step)
            others.append((sent, rank_at(step) * shared + begin))
    direct = swap(later, experts)
    (sums,) = lift([own], [me * shared], w_gate, w_up)
    for piece, at in others[:-1]:
        (sums,) = lift([piece], [at], w_gate, w_up, sums)

    early = round(share * 7 / 16 / 128) * 128
    columns = [jnp.int32(rank * share) for rank in range(ranks)]
    last, last_at = others[-1]
    hidden, partial = lift(
        [last, direct],
        [last_at, jnp.int32(direct_at)],
        w_gate,
        w_up,
        sums,
        (w_down, columns, early),
    )
    returned = swap(partial, experts)
    edges = [early, early + pl.cdiv(share - early, 256) * 128, share]
    owned = []
    for at, end in zip(edges[:-1], edges[1:]):
        cut = end - at
        arrived = [
            send_up(drop(hidden, w_down, rank_at(step) * share + at, cut, jnp.bfloat16), step)
            for step in range(1, ranks)
        ]
        value = drop(hidden, w_down, me * share + at, cut, jnp.float32)
        for other in arrived:
            value = value + other.astype(jnp.float32)
        owned.append(value.astype(jnp.bfloat16))
    returned, owned = lax.optimization_barrier((returned, jnp.concatenate(owned, axis=1)))
    first = mix(weights, returned)

    def part_of(rank):
        return lax.dynamic_slice_in_dim(first, rank * early, early, axis=1)

    mixed = part_of(me)
    for step in range(1, ranks):
        mixed = mixed + send_up(part_of(rank_at(step)), step)
    late = mix(weights, swap(owned, experts))
    return jnp.concatenate([mixed.astype(jnp.bfloat16), late.astype(jnp.bfloat16)], axis=1)


def solution(mesh):
    placed = (
        P(("groups", "dp", "expert"), None),
        P(("groups", "dp", "expert"), None),
        P(("groups", "dp", "expert"), None),
        P("expert", "dp", "tensor"),
        P("expert", "dp", "tensor"),
        P("expert", "tensor", "dp"),
    )
    return jax.shard_map(
        on_device,
        mesh=mesh,
        in_specs=placed,
        out_specs=P(("groups", "dp", "expert"), "tensor"),
        check_vma=False,
    )
```

```python
import jax
import jax.numpy as jnp
from jax import lax
from jax.experimental import pallas as pl
from jax.experimental.pallas import tpu as pltpu
from jax.sharding import PartitionSpec as P

TOP = 2
BLOCK = 128
CAP = 24
LANES = 256
VMEM_BYTES = 50 * 1024 * 1024


def tile_of(width, most=LANES):
    for tile in range(most, 127, -128):
        if width % tile == 0:
            return tile
    return width


def vmem():
    return pl.BlockSpec(memory_space=pltpu.VMEM)


def hbm():
    return pl.BlockSpec(memory_space=pl.ANY)


def dma(count):
    return pltpu.SemaphoreType.DMA((count,))


def in_turn(groups, ahead):
    for group in groups[:ahead]:
        for copy in group:
            copy.start()
    left = iter(range(len(groups)))

    def wait():
        now = next(left)
        if now + ahead < len(groups):
            for copy in groups[now + ahead]:
                copy.start()
        for copy in groups[now]:
            copy.wait()

    return wait


def column_groups(source, starts, width, target, sems):
    tiles, depth, tile = target.shape
    each = width // tile
    groups = []
    for n in range(tiles):
        at = pl.multiple_of(starts[n // each] + (n % each) * tile, 128)
        groups.append(
            [pltpu.make_async_copy(source.at[:, pl.ds(at, tile)], target.at[n], sems.at[n])]
        )
    return groups


def drop_tile(hidden, tiles, n, out):
    tile = tiles.shape[2]
    value = jnp.dot(hidden[...], tiles[n], preferred_element_type=jnp.float32)
    out[:, n * tile : (n + 1) * tile] = value.astype(out.dtype)


def lift(pieces, starts, w_gate, w_up, sums=None, back=None):
    rows = pieces[0].shape[0]
    depths = [piece.shape[1] for piece in pieces]
    depth = sum(depths)
    count = len(pieces)
    hidden = w_gate.shape[1]
    tile = tile_of(hidden)
    tiles = hidden // tile
    given = [] if sums is None else [sums]
    scalars = list(starts)
    args = [*pieces, w_gate, w_up, *given]
    scratch = [
        pltpu.VMEM((rows, depth), jnp.bfloat16),
        pltpu.VMEM((tiles, depth, 2 * tile), jnp.bfloat16),
        pltpu.VMEM((tiles, rows, 2 * tile), jnp.float32),
    ]
    scratch += [dma(tiles)] * (2 * count + 2)
    flops = 4 * rows * depth * hidden
    moved = 4 * depth * hidden + 16 * rows * hidden
    if back is None:
        out_shape = [jax.ShapeDtypeStruct((tiles, rows, 2 * tile), jnp.float32)]
        out_specs = [hbm()]
    else:
        w_down, columns, width = back
        wide = tile_of(width, 1024)
        drops = len(columns) * width // wide
        scratch += [pltpu.VMEM((drops, hidden, wide), jnp.bfloat16), dma(drops)]
        scalars += list(columns)
        args += [w_down]
        out_shape = [
            jax.ShapeDtypeStruct((rows, hidden), jnp.bfloat16),
            jax.ShapeDtypeStruct((rows, len(columns) * width), jnp.bfloat16),
        ]
        out_specs = [vmem(), vmem()]
        flops += 2 * rows * hidden * len(columns) * width
        moved += 2 * hidden * len(columns) * width

    def kernel(at, *refs):
        parts, refs = refs[:count], refs[count:]
        (gate_from, up_from), refs = refs[:2], refs[2:]
        before, refs = refs[: len(given)], refs[len(given) :]
        more = len(args) - count - 2 - len(given)
        down_from, refs = refs[:more], refs[more:]
        outs, refs = refs[: len(out_shape)], refs[len(out_shape) :]
        whole, both, totals = refs[:3]
        sems, (sum_sems, out_sems) = refs[3 : 3 + 2 * count], refs[3 + 2 * count : 5 + 2 * count]
        groups = []
        for n in range(tiles):
            across = pl.ds(n * tile, tile)
            group = []
            row = 0
            for i, size in enumerate(depths):
                begin = pl.multiple_of(at[i], 128)
                for side, source in enumerate((gate_from, up_from)):
                    group.append(
                        pltpu.make_async_copy(
                            source.at[pl.ds(begin, size), across],
                            both.at[n, pl.ds(row, size), pl.ds(side * tile, tile)],
                            sems[2 * i + side].at[n],
                        )
                    )
                row += size
            for source in before:
                group.append(
                    pltpu.make_async_copy(source.at[n], totals.at[n], sum_sems.at[n])
                )
            groups.append(group)
        if back is not None:
            ranges = [at[count + i] for i in range(len(columns))]
            groups += column_groups(down_from[0], ranges, width, refs[-2], refs[-1])
        wait = in_turn(groups, 2)
        row = 0
        for part, size in zip(parts, depths):
            whole[:, row : row + size] = part[...]
            row += size

        def store(n):
            return pltpu.make_async_copy(totals.at[n], outs[0].at[n], out_sems.at[n])

        def settle(n, product):
            if given:
                product = product + totals[n]
            if back is None:
                totals[n] = product
                store(n).start()
            else:
                gate, up = product[:, :tile], product[:, tile:]
                value = gate / (1.0 + jnp.exp(-gate)) * up
                outs[0][:, n * tile : (n + 1) * tile] = value.astype(jnp.bfloat16)

        held = None
        for n in range(tiles):
            wait()
            product = jnp.dot(whole[...], both[n], preferred_element_type=jnp.float32)
            if held is not None:
                settle(n - 1, held)
            held = product
        settle(tiles - 1, held)
        if back is None:
            for n in range(tiles):
                store(n).wait()
        else:
            for n in range(drops):
                wait()
                drop_tile(outs[0], refs[-2], n, outs[1])

    return pl.pallas_call(
        kernel,
        out_shape=out_shape,
        in_specs=[pl.BlockSpec(memory_space=pltpu.SMEM)]
        + [vmem()] * count
        + [hbm()] * (len(args) - count),
        out_specs=out_specs,
        scratch_shapes=scratch,
        compiler_params=pltpu.CompilerParams(vmem_limit_bytes=VMEM_BYTES),
        cost_estimate=pl.CostEstimate(
            flops=flops,
            bytes_accessed=moved,
            transcendentals=rows * hidden,
        ),
        name="lift",
    )(jnp.stack(scalars).astype(jnp.int32), *args)


def drop(hidden, w_down, start, width, dtype):
    rows, depth = hidden.shape
    tile = tile_of(width, 1024)

    def kernel(at, hidden, w_down, out, weight, sems):
        wait = in_turn(column_groups(w_down, [at[0]], width, weight, sems), 2)
        for n in range(width // tile):
            wait()
            drop_tile(hidden, weight, n, out)

    return pl.pallas_call(
        kernel,
        out_shape=jax.ShapeDtypeStruct((rows, width), dtype),
        in_specs=[pl.BlockSpec(memory_space=pltpu.SMEM), vmem(), hbm()],
        out_specs=vmem(),
        scratch_shapes=[
            pltpu.VMEM((width // tile, depth, tile), jnp.bfloat16),
            dma(width // tile),
        ],
        compiler_params=pltpu.CompilerParams(vmem_limit_bytes=VMEM_BYTES),
        cost_estimate=pl.CostEstimate(
            flops=2 * rows * depth * width, bytes_accessed=2 * depth * width, transcendentals=0
        ),
        name="drop",
    )(jnp.reshape(start, (1,)).astype(jnp.int32), hidden, w_down)


def selectors(expert_ids, gate_probs, experts):
    rows = expert_ids.shape[0]
    blocks = rows // BLOCK
    match = expert_ids.T[:, None, :] == jnp.arange(experts, dtype=jnp.int32)[None, :, None]
    named = jnp.any(match, axis=0)
    weight = jnp.sum(jnp.where(match, gate_probs.T[:, None, :], 0.0), axis=0)
    row = jnp.arange(rows, dtype=jnp.int32)
    same = row[:, None] // BLOCK == row[None, :] // BLOCK
    earlier = ((row[:, None] < row[None, :]) & same).astype(jnp.bfloat16)
    before = jnp.dot(named.astype(jnp.bfloat16), earlier, preferred_element_type=jnp.float32)
    place = before.astype(jnp.int32) + (row // BLOCK * CAP)[None, :]
    slots = jnp.arange(blocks * CAP, dtype=jnp.int32)
    hit = named[:, None, :] & (place[:, None, :] == slots[None, :, None])
    high = weight.astype(jnp.bfloat16)
    rest = weight - high.astype(jnp.float32)
    middle = rest.astype(jnp.bfloat16)
    low = (rest - middle.astype(jnp.float32)).astype(jnp.bfloat16)
    flat = (experts * blocks * CAP, rows)
    return [
        jnp.where(hit, part[:, None, :], 0).astype(jnp.bfloat16).reshape(flat)
        for part in (high, middle, low)
    ]


def place(tokens, expert_ids, experts, start, width):
    rows = tokens.shape[0]
    slots = rows // BLOCK * CAP

    def kernel(at, ids, tokens, chosen, out, part, picked, sem):
        begin = pl.multiple_of(at[0], 128)
        copy = pltpu.make_async_copy(tokens.at[:, pl.ds(begin, width)], part, sem)
        copy.start()
        expert = lax.broadcasted_iota(jnp.int32, (experts, rows), 0)
        named = jnp.zeros((experts, rows), jnp.float32)
        for k in range(TOP):
            named = named + jnp.where(ids[k : k + 1] == expert, 1.0, 0.0)
        row = lax.broadcasted_iota(jnp.int32, (rows, rows), 0)
        later = lax.broadcasted_iota(jnp.int32, (rows, rows), 1)
        same = row // BLOCK == later // BLOCK
        earlier = jnp.where((row < later) & same, 1.0, 0.0).astype(jnp.bfloat16)
        before = jnp.dot(
            named.astype(jnp.bfloat16), earlier, preferred_element_type=jnp.float32
        ).astype(jnp.int32)
        block = lax.broadcasted_iota(jnp.int32, (experts, rows), 1) // BLOCK
        where = jnp.where(named > 0.0, before + block * CAP, -1)
        slot = lax.broadcasted_iota(jnp.int32, (slots, rows), 0)
        for e in range(experts):
            picked[e * slots : (e + 1) * slots] = jnp.where(where[e : e + 1] == slot, 1.0, 0.0)
        chosen[...] = picked[...].astype(jnp.bfloat16)
        copy.wait()
        value = jnp.dot(chosen[...], part[...], preferred_element_type=jnp.float32)
        out[...] = value.astype(jnp.bfloat16)

    return pl.pallas_call(
        kernel,
        out_shape=[
            jax.ShapeDtypeStruct((experts * slots, rows), jnp.bfloat16),
            jax.ShapeDtypeStruct((experts * slots, width), jnp.bfloat16),
        ],
        in_specs=[pl.BlockSpec(memory_space=pltpu.SMEM), vmem(), hbm()],
        out_specs=[vmem(), vmem()],
        scratch_shapes=[
            pltpu.VMEM((rows, width), jnp.bfloat16),
            pltpu.VMEM((experts * slots, rows), jnp.float32),
            pltpu.SemaphoreType.DMA,
        ],
        compiler_params=pltpu.CompilerParams(vmem_limit_bytes=VMEM_BYTES // 2),
        cost_estimate=pl.CostEstimate(
            flops=2 * experts * slots * rows * width,
            bytes_accessed=2 * rows * width,
            transcendentals=0,
        ),
        name="place",
    )(jnp.reshape(start, (1,)).astype(jnp.int32), expert_ids.T, tokens)


def swap(value, experts):
    slots, width = value.shape
    return lax.all_to_all(
        value.reshape(experts, slots // experts, width),
        "expert",
        split_axis=0,
        concat_axis=0,
        tiled=True,
    ).reshape(slots, width)


def mix(weights, returned):
    return sum(
        lax.dot_general(
            w, returned, (((0,), (0,)), ((), ())), preferred_element_type=jnp.float32
        )
        for w in weights
    )


def mix_last(weights, returned, first):
    rows = weights[0].shape[1]
    early = first[0].shape[1]
    late = returned.shape[1]
    count = len(weights)

    def kernel(*refs):
        parts, back, terms, out = refs[:count], refs[count], refs[count + 1 : -1], refs[-1]
        out[:, :early] = sum(term[...] for term in terms).astype(jnp.bfloat16)
        for at in range(0, late, 2 * LANES):
            end = min(at + 2 * LANES, late)
            out[:, early + at : early + end] = mix(
                [part[...] for part in parts], back[:, at:end]
            ).astype(jnp.bfloat16)

    return pl.pallas_call(
        kernel,
        out_shape=jax.ShapeDtypeStruct((rows, early + late), jnp.bfloat16),
        in_specs=[vmem()] * (count + 1 + len(first)),
        out_specs=vmem(),
        compiler_params=pltpu.CompilerParams(vmem_limit_bytes=VMEM_BYTES // 2),
        cost_estimate=pl.CostEstimate(
            flops=2 * count * returned.shape[0] * rows * late,
            bytes_accessed=2 * rows * (early + late),
            transcendentals=0,
        ),
        name="mix_last",
    )(*weights, returned, *first)


def on_device(tokens, expert_ids, gate_probs, w_gate, w_up, w_down):
    width = tokens.shape[1]
    experts = lax.axis_size("expert")
    ranks = lax.axis_size("tensor")
    me = lax.axis_index("tensor")
    w_gate = lax.all_gather(w_gate, "dp", axis=1, tiled=True)[0]
    w_up = lax.all_gather(w_up, "dp", axis=1, tiled=True)[0]
    w_down = lax.all_gather(w_down, "dp", axis=2, tiled=True)[0]
    weights = selectors(expert_ids, gate_probs, experts)

    def rank_at(step):
        return lax.rem(me + step, ranks)

    def send_up(value, step):
        return lax.ppermute(value, "tensor", [(i, (i + step) % ranks) for i in range(ranks)])

    share = width // ranks
    shared = round(share * 5 / 8 / LANES) * LANES
    direct_at = ranks * shared

    chosen, placed = place(tokens, expert_ids, experts, me * shared, shared)
    own = swap(placed, experts)
    cut = pl.cdiv(shared, 2 * LANES) * LANES
    others = []
    for begin, end in ((0, cut), (cut, shared)):
        for step in range(1, ranks):
            sent = send_up(own[:, begin:end], ranks - step)
            others.append((sent, rank_at(step) * shared + begin))
    placed = jnp.dot(chosen, tokens[:, direct_at:], preferred_element_type=jnp.float32)
    direct = swap(placed.astype(jnp.bfloat16), experts)
    (sums,) = lift([own], [me * shared], w_gate, w_up)
    for piece, at in others[:-1]:
        (sums,) = lift([piece], [at], w_gate, w_up, sums)

    early = round(share * 3 / 8 / 128) * 128
    columns = [jnp.int32(rank * share) for rank in range(ranks)]
    last, last_at = others[-1]
    hidden, partial = lift(
        [last, direct],
        [last_at, jnp.int32(direct_at)],
        w_gate,
        w_up,
        sums,
        (w_down, columns, early),
    )
    returned = swap(partial, experts)
    edges = [early, early + (share - early) // 512 * 256, share] if share - early >= 512 else [early, share]
    owned = []
    for at, end in zip(edges[:-1], edges[1:]):
        cut = end - at
        arrived = [
            send_up(drop(hidden, w_down, rank_at(step) * share + at, cut, jnp.bfloat16), step)
            for step in range(1, ranks)
        ]
        value = drop(hidden, w_down, me * share + at, cut, jnp.float32)
        for other in arrived:
            value = value + other.astype(jnp.float32)
        owned.append(value.astype(jnp.bfloat16))
    returned, owned = lax.optimization_barrier((returned, jnp.concatenate(owned, axis=1)))
    first = mix(weights, returned)

    def part_of(rank):
        return lax.dynamic_slice_in_dim(first, rank * early, early, axis=1)

    terms = [part_of(me)]
    for step in range(1, ranks):
        terms.append(send_up(part_of(rank_at(step)), step))
    return mix_last(weights, swap(owned, experts), terms)


def solution(mesh):
    placed = (
        P(("groups", "dp", "expert"), None),
        P(("groups", "dp", "expert"), None),
        P(("groups", "dp", "expert"), None),
        P("expert", "dp", "tensor"),
        P("expert", "dp", "tensor"),
        P("expert", "tensor", "dp"),
    )
    return jax.shard_map(
        on_device,
        mesh=mesh,
        in_specs=placed,
        out_specs=P(("groups", "dp", "expert"), "tensor"),
        check_vma=False,
    )
```

```python
import jax
import jax.numpy as jnp
from jax import lax
from jax.experimental import pallas as pl
from jax.experimental.pallas import tpu as pltpu
from jax.sharding import PartitionSpec as P

TOP = 2
BLOCK = 128
CAP = 24
LANES = 256
VMEM_BYTES = 50 * 1024 * 1024


def tile_of(width, most=LANES):
    for tile in range(most, 127, -128):
        if width % tile == 0:
            return tile
    return width


def vmem():
    return pl.BlockSpec(memory_space=pltpu.VMEM)


def hbm():
    return pl.BlockSpec(memory_space=pl.ANY)


def dma(count):
    return pltpu.SemaphoreType.DMA((count,))


def in_turn(groups, ahead):
    for group in groups[:ahead]:
        for copy in group:
            copy.start()
    left = iter(range(len(groups)))

    def wait():
        now = next(left)
        if now + ahead < len(groups):
            for copy in groups[now + ahead]:
                copy.start()
        for copy in groups[now]:
            copy.wait()

    return wait


def column_groups(source, starts, width, target, sems):
    tiles, depth, tile = target.shape
    each = width // tile
    groups = []
    for n in range(tiles):
        at = pl.multiple_of(starts[n // each] + (n % each) * tile, 128)
        groups.append(
            [pltpu.make_async_copy(source.at[:, pl.ds(at, tile)], target.at[n], sems.at[n])]
        )
    return groups


def drop_tile(hidden, tiles, n, out):
    tile = tiles.shape[2]
    value = jnp.dot(hidden[...], tiles[n], preferred_element_type=jnp.float32)
    out[:, n * tile : (n + 1) * tile] = value.astype(out.dtype)


def lift(pieces, starts, w_gate, w_up, sums=None, back=None):
    rows = pieces[0].shape[0]
    depths = [piece.shape[1] for piece in pieces]
    depth = sum(depths)
    count = len(pieces)
    hidden = w_gate.shape[1]
    tile = tile_of(hidden)
    tiles = hidden // tile
    given = [] if sums is None else [sums]
    scalars = list(starts)
    args = [*pieces, w_gate, w_up, *given]
    scratch = [
        pltpu.VMEM((rows, depth), jnp.bfloat16),
        pltpu.VMEM((tiles, depth, 2 * tile), jnp.bfloat16),
        pltpu.VMEM((tiles, rows, 2 * tile), jnp.float32),
    ]
    scratch += [dma(tiles)] * (2 * count + 2)
    flops = 4 * rows * depth * hidden
    moved = 4 * depth * hidden + 16 * rows * hidden
    if back is None:
        out_shape = [jax.ShapeDtypeStruct((tiles, rows, 2 * tile), jnp.float32)]
        out_specs = [hbm()]
    else:
        w_down, columns, width = back
        wide = tile_of(width, 1024)
        drops = len(columns) * width // wide
        scratch += [pltpu.VMEM((drops, hidden, wide), jnp.bfloat16), dma(drops)]
        scalars += list(columns)
        args += [w_down]
        out_shape = [
            jax.ShapeDtypeStruct((rows, hidden), jnp.bfloat16),
            jax.ShapeDtypeStruct((rows, len(columns) * width), jnp.bfloat16),
        ]
        out_specs = [vmem(), vmem()]
        flops += 2 * rows * hidden * len(columns) * width
        moved += 2 * hidden * len(columns) * width

    def kernel(at, *refs):
        parts, refs = refs[:count], refs[count:]
        (gate_from, up_from), refs = refs[:2], refs[2:]
        before, refs = refs[: len(given)], refs[len(given) :]
        more = len(args) - count - 2 - len(given)
        down_from, refs = refs[:more], refs[more:]
        outs, refs = refs[: len(out_shape)], refs[len(out_shape) :]
        whole, both, totals = refs[:3]
        sems, (sum_sems, out_sems) = refs[3 : 3 + 2 * count], refs[3 + 2 * count : 5 + 2 * count]
        groups = []
        for n in range(tiles):
            across = pl.ds(n * tile, tile)
            group = []
            row = 0
            for i, size in enumerate(depths):
                begin = pl.multiple_of(at[i], 128)
                for side, source in enumerate((gate_from, up_from)):
                    group.append(
                        pltpu.make_async_copy(
                            source.at[pl.ds(begin, size), across],
                            both.at[n, pl.ds(row, size), pl.ds(side * tile, tile)],
                            sems[2 * i + side].at[n],
                        )
                    )
                row += size
            for source in before:
                group.append(
                    pltpu.make_async_copy(source.at[n], totals.at[n], sum_sems.at[n])
                )
            groups.append(group)
        if back is not None:
            ranges = [at[count + i] for i in range(len(columns))]
            groups += column_groups(down_from[0], ranges, width, refs[-2], refs[-1])
        wait = in_turn(groups, 2)
        row = 0
        for part, size in zip(parts, depths):
            whole[:, row : row + size] = part[...]
            row += size

        def store(n):
            return pltpu.make_async_copy(totals.at[n], outs[0].at[n], out_sems.at[n])

        def settle(n, product):
            if given:
                product = product + totals[n]
            if back is None:
                totals[n] = product
                store(n).start()
            else:
                gate, up = product[:, :tile], product[:, tile:]
                value = gate / (1.0 + jnp.exp(-gate)) * up
                outs[0][:, n * tile : (n + 1) * tile] = value.astype(jnp.bfloat16)

        held = None
        for n in range(tiles):
            wait()
            product = jnp.dot(whole[...], both[n], preferred_element_type=jnp.float32)
            if held is not None:
                settle(n - 1, held)
            held = product
        settle(tiles - 1, held)
        if back is None:
            for n in range(tiles):
                store(n).wait()
        else:
            for n in range(drops):
                wait()
                drop_tile(outs[0], refs[-2], n, outs[1])

    return pl.pallas_call(
        kernel,
        out_shape=out_shape,
        in_specs=[pl.BlockSpec(memory_space=pltpu.SMEM)]
        + [vmem()] * count
        + [hbm()] * (len(args) - count),
        out_specs=out_specs,
        scratch_shapes=scratch,
        compiler_params=pltpu.CompilerParams(vmem_limit_bytes=VMEM_BYTES),
        cost_estimate=pl.CostEstimate(
            flops=flops,
            bytes_accessed=moved,
            transcendentals=rows * hidden,
        ),
        name="lift",
    )(jnp.stack(scalars).astype(jnp.int32), *args)


def drop(hidden, w_down, start, width, dtype):
    rows, depth = hidden.shape
    tile = tile_of(width, 1024)

    def kernel(at, hidden, w_down, out, weight, sems):
        wait = in_turn(column_groups(w_down, [at[0]], width, weight, sems), 2)
        for n in range(width // tile):
            wait()
            drop_tile(hidden, weight, n, out)

    return pl.pallas_call(
        kernel,
        out_shape=jax.ShapeDtypeStruct((rows, width), dtype),
        in_specs=[pl.BlockSpec(memory_space=pltpu.SMEM), vmem(), hbm()],
        out_specs=vmem(),
        scratch_shapes=[
            pltpu.VMEM((width // tile, depth, tile), jnp.bfloat16),
            dma(width // tile),
        ],
        compiler_params=pltpu.CompilerParams(vmem_limit_bytes=VMEM_BYTES),
        cost_estimate=pl.CostEstimate(
            flops=2 * rows * depth * width, bytes_accessed=2 * depth * width, transcendentals=0
        ),
        name="drop",
    )(jnp.reshape(start, (1,)).astype(jnp.int32), hidden, w_down)


def selectors(expert_ids, gate_probs, experts):
    rows = expert_ids.shape[0]
    blocks = rows // BLOCK
    match = expert_ids.T[:, None, :] == jnp.arange(experts, dtype=jnp.int32)[None, :, None]
    named = jnp.any(match, axis=0)
    weight = jnp.sum(jnp.where(match, gate_probs.T[:, None, :], 0.0), axis=0)
    row = jnp.arange(rows, dtype=jnp.int32)
    same = row[:, None] // BLOCK == row[None, :] // BLOCK
    earlier = ((row[:, None] < row[None, :]) & same).astype(jnp.bfloat16)
    before = jnp.dot(named.astype(jnp.bfloat16), earlier, preferred_element_type=jnp.float32)
    place = before.astype(jnp.int32) + (row // BLOCK * CAP)[None, :]
    slots = jnp.arange(blocks * CAP, dtype=jnp.int32)
    hit = named[:, None, :] & (place[:, None, :] == slots[None, :, None])
    high = weight.astype(jnp.bfloat16)
    rest = weight - high.astype(jnp.float32)
    middle = rest.astype(jnp.bfloat16)
    low = (rest - middle.astype(jnp.float32)).astype(jnp.bfloat16)
    flat = (experts * blocks * CAP, rows)
    return [
        jnp.where(hit, part[:, None, :], 0).astype(jnp.bfloat16).reshape(flat)
        for part in (high, middle, low)
    ]


def place(tokens, expert_ids, experts, start, width):
    rows = tokens.shape[0]
    slots = rows // BLOCK * CAP

    def kernel(at, ids, tokens, chosen, out, part, picked, sem):
        begin = pl.multiple_of(at[0], 128)
        copy = pltpu.make_async_copy(tokens.at[:, pl.ds(begin, width)], part, sem)
        copy.start()
        expert = lax.broadcasted_iota(jnp.int32, (experts, rows), 0)
        named = jnp.zeros((experts, rows), jnp.float32)
        for k in range(TOP):
            named = named + jnp.where(ids[k : k + 1] == expert, 1.0, 0.0)
        row = lax.broadcasted_iota(jnp.int32, (rows, rows), 0)
        later = lax.broadcasted_iota(jnp.int32, (rows, rows), 1)
        same = row // BLOCK == later // BLOCK
        earlier = jnp.where((row < later) & same, 1.0, 0.0).astype(jnp.bfloat16)
        before = jnp.dot(
            named.astype(jnp.bfloat16), earlier, preferred_element_type=jnp.float32
        ).astype(jnp.int32)
        block = lax.broadcasted_iota(jnp.int32, (experts, rows), 1) // BLOCK
        where = jnp.where(named > 0.0, before + block * CAP, -1)
        slot = lax.broadcasted_iota(jnp.int32, (slots, rows), 0)
        for e in range(experts):
            picked[e * slots : (e + 1) * slots] = jnp.where(where[e : e + 1] == slot, 1.0, 0.0)
        chosen[...] = picked[...].astype(jnp.bfloat16)
        copy.wait()
        value = jnp.dot(chosen[...], part[...], preferred_element_type=jnp.float32)
        out[...] = value.astype(jnp.bfloat16)

    return pl.pallas_call(
        kernel,
        out_shape=[
            jax.ShapeDtypeStruct((experts * slots, rows), jnp.bfloat16),
            jax.ShapeDtypeStruct((experts * slots, width), jnp.bfloat16),
        ],
        in_specs=[pl.BlockSpec(memory_space=pltpu.SMEM), vmem(), hbm()],
        out_specs=[vmem(), vmem()],
        scratch_shapes=[
            pltpu.VMEM((rows, width), jnp.bfloat16),
            pltpu.VMEM((experts * slots, rows), jnp.float32),
            pltpu.SemaphoreType.DMA,
        ],
        compiler_params=pltpu.CompilerParams(vmem_limit_bytes=VMEM_BYTES // 2),
        cost_estimate=pl.CostEstimate(
            flops=2 * experts * slots * rows * width,
            bytes_accessed=2 * rows * width,
            transcendentals=0,
        ),
        name="place",
    )(jnp.reshape(start, (1,)).astype(jnp.int32), expert_ids.T, tokens)


def swap(value, experts):
    slots, width = value.shape
    return lax.all_to_all(
        value.reshape(experts, slots // experts, width),
        "expert",
        split_axis=0,
        concat_axis=0,
        tiled=True,
    ).reshape(slots, width)


def mix(weights, returned):
    return sum(
        lax.dot_general(
            w, returned, (((0,), (0,)), ((), ())), preferred_element_type=jnp.float32
        )
        for w in weights
    )


def add_join(groups):
    rows = groups[0][0].shape[0]
    widths = [group[0].shape[1] for group in groups]
    count = len(groups[0])
    flat = [term for group in groups for term in group]

    def kernel(*refs):
        out = refs[-1]
        at = 0
        for i, width in enumerate(widths):
            value = refs[i * count][...]
            for term in refs[i * count + 1 : (i + 1) * count]:
                value = value + term[...].astype(jnp.float32)
            out[:, at : at + width] = value.astype(jnp.bfloat16)
            at += width

    return pl.pallas_call(
        kernel,
        out_shape=jax.ShapeDtypeStruct((rows, sum(widths)), jnp.bfloat16),
        in_specs=[vmem()] * len(flat),
        out_specs=vmem(),
        compiler_params=pltpu.CompilerParams(vmem_limit_bytes=VMEM_BYTES // 2),
        cost_estimate=pl.CostEstimate(
            flops=count * rows * sum(widths),
            bytes_accessed=8 * rows * sum(widths),
            transcendentals=0,
        ),
        name="add_join",
    )(*flat)


def mix_last(weights, returned, first):
    rows = weights[0].shape[1]
    early = first[0].shape[1]
    late = returned.shape[1]
    count = len(weights)

    def kernel(*refs):
        parts, back, terms, out = refs[:count], refs[count], refs[count + 1 : -1], refs[-1]
        out[:, :early] = sum(term[...] for term in terms).astype(jnp.bfloat16)
        for at in range(0, late, 2 * LANES):
            end = min(at + 2 * LANES, late)
            out[:, early + at : early + end] = mix(
                [part[...] for part in parts], back[:, at:end]
            ).astype(jnp.bfloat16)

    return pl.pallas_call(
        kernel,
        out_shape=jax.ShapeDtypeStruct((rows, early + late), jnp.bfloat16),
        in_specs=[vmem()] * (count + 1 + len(first)),
        out_specs=vmem(),
        compiler_params=pltpu.CompilerParams(vmem_limit_bytes=VMEM_BYTES // 2),
        cost_estimate=pl.CostEstimate(
            flops=2 * count * returned.shape[0] * rows * late,
            bytes_accessed=2 * rows * (early + late),
            transcendentals=0,
        ),
        name="mix_last",
    )(*weights, returned, *first)


def on_device(tokens, expert_ids, gate_probs, w_gate, w_up, w_down):
    width = tokens.shape[1]
    experts = lax.axis_size("expert")
    ranks = lax.axis_size("tensor")
    me = lax.axis_index("tensor")
    w_gate = lax.all_gather(w_gate, "dp", axis=1, tiled=True)[0]
    w_up = lax.all_gather(w_up, "dp", axis=1, tiled=True)[0]
    w_down = lax.all_gather(w_down, "dp", axis=2, tiled=True)[0]
    weights = selectors(expert_ids, gate_probs, experts)

    def rank_at(step):
        return lax.rem(me + step, ranks)

    def send_up(value, step):
        return lax.ppermute(value, "tensor", [(i, (i + step) % ranks) for i in range(ranks)])

    share = width // ranks
    shared = round(share * 5 / 8 / LANES) * LANES
    direct_at = ranks * shared

    chosen, placed = place(tokens, expert_ids, experts, me * shared, shared)
    own = swap(placed, experts)
    cut = pl.cdiv(shared, 2 * LANES) * LANES
    others = []
    for begin, end in ((0, cut), (cut, shared)):
        for step in range(1, ranks):
            sent = send_up(own[:, begin:end], ranks - step)
            others.append((sent, rank_at(step) * shared + begin))
    placed = jnp.dot(chosen, tokens[:, direct_at:], preferred_element_type=jnp.float32)
    direct = swap(placed.astype(jnp.bfloat16), experts)
    (sums,) = lift([own], [me * shared], w_gate, w_up)
    for piece, at in others[:-1]:
        (sums,) = lift([piece], [at], w_gate, w_up, sums)

    early = round(share * 3 / 8 / 128) * 128
    columns = [jnp.int32(rank * share) for rank in range(ranks)]
    last, last_at = others[-1]
    hidden, partial = lift(
        [last, direct],
        [last_at, jnp.int32(direct_at)],
        w_gate,
        w_up,
        sums,
        (w_down, columns, early),
    )
    returned = swap(partial, experts)
    edges = [early, early + (share - early) // 512 * 256, share] if share - early >= 512 else [early, share]
    owned = []
    for at, end in zip(edges[:-1], edges[1:]):
        cut = end - at
        arrived = [
            send_up(drop(hidden, w_down, rank_at(step) * share + at, cut, jnp.bfloat16), step)
            for step in range(1, ranks)
        ]
        value = drop(hidden, w_down, me * share + at, cut, jnp.float32)
        owned.append([value, *arrived])
    returned, owned = lax.optimization_barrier((returned, add_join(owned)))
    first = mix(weights, returned)

    def part_of(rank):
        return lax.dynamic_slice_in_dim(first, rank * early, early, axis=1)

    terms = [part_of(me)]
    for step in range(1, ranks):
        terms.append(send_up(part_of(rank_at(step)), step))
    return mix_last(weights, swap(owned, experts), terms)


def solution(mesh):
    placed = (
        P(("groups", "dp", "expert"), None),
        P(("groups", "dp", "expert"), None),
        P(("groups", "dp", "expert"), None),
        P("expert", "dp", "tensor"),
        P("expert", "dp", "tensor"),
        P("expert", "tensor", "dp"),
    )
    return jax.shard_map(
        on_device,
        mesh=mesh,
        in_specs=placed,
        out_specs=P(("groups", "dp", "expert"), "tensor"),
        check_vma=False,
    )
```

```python
import jax
import jax.numpy as jnp
from jax import lax
from jax.experimental import pallas as pl
from jax.experimental.pallas import tpu as pltpu
from jax.sharding import PartitionSpec as P

TOP = 2
BLOCK = 128
CAP = 24
LANES = 256
VMEM_BYTES = 50 * 1024 * 1024


def tile_of(width, most=LANES):
    for tile in range(most, 127, -128):
        if width % tile == 0:
            return tile
    return width


def vmem():
    return pl.BlockSpec(memory_space=pltpu.VMEM)


def hbm():
    return pl.BlockSpec(memory_space=pl.ANY)


def dma(count):
    return pltpu.SemaphoreType.DMA((count,))


def in_turn(groups, ahead):
    for group in groups[:ahead]:
        for copy in group:
            copy.start()
    left = iter(range(len(groups)))

    def wait():
        now = next(left)
        if now + ahead < len(groups):
            for copy in groups[now + ahead]:
                copy.start()
        for copy in groups[now]:
            copy.wait()

    return wait


def column_groups(source, starts, width, target, sems):
    tiles, depth, tile = target.shape
    each = width // tile
    groups = []
    for n in range(tiles):
        at = pl.multiple_of(starts[n // each] + (n % each) * tile, 128)
        groups.append(
            [pltpu.make_async_copy(source.at[:, pl.ds(at, tile)], target.at[n], sems.at[n])]
        )
    return groups


def drop_tile(hidden, tiles, n, out):
    tile = tiles.shape[2]
    value = jnp.dot(hidden[...], tiles[n], preferred_element_type=jnp.float32)
    out[:, n * tile : (n + 1) * tile] = value.astype(out.dtype)


def lift(pieces, starts, w_gate, w_up, sums=None, back=None):
    rows = pieces[0].shape[0]
    depths = [piece.shape[1] for piece in pieces]
    depth = sum(depths)
    count = len(pieces)
    hidden = w_gate.shape[1]
    tile = tile_of(hidden)
    tiles = hidden // tile
    given = [] if sums is None else [sums]
    scalars = list(starts)
    args = [*pieces, w_gate, w_up, *given]
    scratch = [
        pltpu.VMEM((rows, depth), jnp.bfloat16),
        pltpu.VMEM((tiles, depth, 2 * tile), jnp.bfloat16),
        pltpu.VMEM((tiles, rows, 2 * tile), jnp.float32),
    ]
    scratch += [dma(tiles)] * (2 * count + 2)
    flops = 4 * rows * depth * hidden
    moved = 4 * depth * hidden + 16 * rows * hidden
    if back is None:
        out_shape = [jax.ShapeDtypeStruct((tiles, rows, 2 * tile), jnp.float32)]
        out_specs = [hbm()]
    else:
        w_down, columns, width = back
        wide = tile_of(width, 1024)
        drops = len(columns) * width // wide
        scratch += [pltpu.VMEM((drops, hidden, wide), jnp.bfloat16), dma(drops)]
        scalars += list(columns)
        args += [w_down]
        out_shape = [
            jax.ShapeDtypeStruct((rows, hidden), jnp.bfloat16),
            jax.ShapeDtypeStruct((rows, len(columns) * width), jnp.bfloat16),
        ]
        out_specs = [vmem(), vmem()]
        flops += 2 * rows * hidden * len(columns) * width
        moved += 2 * hidden * len(columns) * width

    def kernel(at, *refs):
        parts, refs = refs[:count], refs[count:]
        (gate_from, up_from), refs = refs[:2], refs[2:]
        before, refs = refs[: len(given)], refs[len(given) :]
        more = len(args) - count - 2 - len(given)
        down_from, refs = refs[:more], refs[more:]
        outs, refs = refs[: len(out_shape)], refs[len(out_shape) :]
        whole, both, totals = refs[:3]
        sems, (sum_sems, out_sems) = refs[3 : 3 + 2 * count], refs[3 + 2 * count : 5 + 2 * count]
        groups = []
        for n in range(tiles):
            across = pl.ds(n * tile, tile)
            group = []
            row = 0
            for i, size in enumerate(depths):
                begin = pl.multiple_of(at[i], 128)
                for side, source in enumerate((gate_from, up_from)):
                    group.append(
                        pltpu.make_async_copy(
                            source.at[pl.ds(begin, size), across],
                            both.at[n, pl.ds(row, size), pl.ds(side * tile, tile)],
                            sems[2 * i + side].at[n],
                        )
                    )
                row += size
            for source in before:
                group.append(
                    pltpu.make_async_copy(source.at[n], totals.at[n], sum_sems.at[n])
                )
            groups.append(group)
        if back is not None:
            ranges = [at[count + i] for i in range(len(columns))]
            groups += column_groups(down_from[0], ranges, width, refs[-2], refs[-1])
        wait = in_turn(groups, 2)
        row = 0
        for part, size in zip(parts, depths):
            whole[:, row : row + size] = part[...]
            row += size

        def store(n):
            return pltpu.make_async_copy(totals.at[n], outs[0].at[n], out_sems.at[n])

        def settle(n, product):
            if given:
                product = product + totals[n]
            if back is None:
                totals[n] = product
                store(n).start()
            else:
                gate, up = product[:, :tile], product[:, tile:]
                value = gate / (1.0 + jnp.exp(-gate)) * up
                outs[0][:, n * tile : (n + 1) * tile] = value.astype(jnp.bfloat16)

        held = None
        for n in range(tiles):
            wait()
            product = jnp.dot(whole[...], both[n], preferred_element_type=jnp.float32)
            if held is not None:
                settle(n - 1, held)
            held = product
        settle(tiles - 1, held)
        if back is None:
            for n in range(tiles):
                store(n).wait()
        else:
            for n in range(drops):
                wait()
                drop_tile(outs[0], refs[-2], n, outs[1])

    return pl.pallas_call(
        kernel,
        out_shape=out_shape,
        in_specs=[pl.BlockSpec(memory_space=pltpu.SMEM)]
        + [vmem()] * count
        + [hbm()] * (len(args) - count),
        out_specs=out_specs,
        scratch_shapes=scratch,
        compiler_params=pltpu.CompilerParams(vmem_limit_bytes=VMEM_BYTES),
        cost_estimate=pl.CostEstimate(
            flops=flops,
            bytes_accessed=moved,
            transcendentals=rows * hidden,
        ),
        name="lift",
    )(jnp.stack(scalars).astype(jnp.int32), *args)


def drop(hidden, w_down, start, width, dtype):
    rows, depth = hidden.shape
    tile = tile_of(width, 1024)

    def kernel(at, hidden, w_down, out, weight, sems):
        wait = in_turn(column_groups(w_down, [at[0]], width, weight, sems), 2)
        for n in range(width // tile):
            wait()
            drop_tile(hidden, weight, n, out)

    return pl.pallas_call(
        kernel,
        out_shape=jax.ShapeDtypeStruct((rows, width), dtype),
        in_specs=[pl.BlockSpec(memory_space=pltpu.SMEM), vmem(), hbm()],
        out_specs=vmem(),
        scratch_shapes=[
            pltpu.VMEM((width // tile, depth, tile), jnp.bfloat16),
            dma(width // tile),
        ],
        compiler_params=pltpu.CompilerParams(vmem_limit_bytes=VMEM_BYTES),
        cost_estimate=pl.CostEstimate(
            flops=2 * rows * depth * width, bytes_accessed=2 * depth * width, transcendentals=0
        ),
        name="drop",
    )(jnp.reshape(start, (1,)).astype(jnp.int32), hidden, w_down)


def selectors(expert_ids, gate_probs, experts):
    rows = expert_ids.shape[0]
    blocks = rows // BLOCK
    match = expert_ids.T[:, None, :] == jnp.arange(experts, dtype=jnp.int32)[None, :, None]
    named = jnp.any(match, axis=0)
    weight = jnp.sum(jnp.where(match, gate_probs.T[:, None, :], 0.0), axis=0)
    row = jnp.arange(rows, dtype=jnp.int32)
    same = row[:, None] // BLOCK == row[None, :] // BLOCK
    earlier = ((row[:, None] < row[None, :]) & same).astype(jnp.bfloat16)
    before = jnp.dot(named.astype(jnp.bfloat16), earlier, preferred_element_type=jnp.float32)
    place = before.astype(jnp.int32) + (row // BLOCK * CAP)[None, :]
    slots = jnp.arange(blocks * CAP, dtype=jnp.int32)
    hit = named[:, None, :] & (place[:, None, :] == slots[None, :, None])
    high = weight.astype(jnp.bfloat16)
    rest = weight - high.astype(jnp.float32)
    middle = rest.astype(jnp.bfloat16)
    low = (rest - middle.astype(jnp.float32)).astype(jnp.bfloat16)
    flat = (experts * blocks * CAP, rows)
    return [
        jnp.where(hit, part[:, None, :], 0).astype(jnp.bfloat16).reshape(flat)
        for part in (high, middle, low)
    ]


def place(tokens, expert_ids, experts, start, width):
    rows = tokens.shape[0]
    slots = rows // BLOCK * CAP

    def kernel(at, ids, tokens, chosen, out, part, picked, sem):
        begin = pl.multiple_of(at[0], 128)
        copy = pltpu.make_async_copy(tokens.at[:, pl.ds(begin, width)], part, sem)
        copy.start()
        expert = lax.broadcasted_iota(jnp.int32, (experts, rows), 0)
        named = jnp.zeros((experts, rows), jnp.float32)
        for k in range(TOP):
            named = named + jnp.where(ids[k : k + 1] == expert, 1.0, 0.0)
        row = lax.broadcasted_iota(jnp.int32, (rows, rows), 0)
        later = lax.broadcasted_iota(jnp.int32, (rows, rows), 1)
        same = row // BLOCK == later // BLOCK
        earlier = jnp.where((row < later) & same, 1.0, 0.0).astype(jnp.bfloat16)
        before = jnp.dot(
            named.astype(jnp.bfloat16), earlier, preferred_element_type=jnp.float32
        ).astype(jnp.int32)
        block = lax.broadcasted_iota(jnp.int32, (experts, rows), 1) // BLOCK
        where = jnp.where(named > 0.0, before + block * CAP, -1)
        slot = lax.broadcasted_iota(jnp.int32, (slots, rows), 0)
        for e in range(experts):
            picked[e * slots : (e + 1) * slots] = jnp.where(where[e : e + 1] == slot, 1.0, 0.0)
        chosen[...] = picked[...].astype(jnp.bfloat16)
        copy.wait()
        value = jnp.dot(chosen[...], part[...], preferred_element_type=jnp.float32)
        out[...] = value.astype(jnp.bfloat16)

    return pl.pallas_call(
        kernel,
        out_shape=[
            jax.ShapeDtypeStruct((experts * slots, rows), jnp.bfloat16),
            jax.ShapeDtypeStruct((experts * slots, width), jnp.bfloat16),
        ],
        in_specs=[pl.BlockSpec(memory_space=pltpu.SMEM), vmem(), hbm()],
        out_specs=[vmem(), vmem()],
        scratch_shapes=[
            pltpu.VMEM((rows, width), jnp.bfloat16),
            pltpu.VMEM((experts * slots, rows), jnp.float32),
            pltpu.SemaphoreType.DMA,
        ],
        compiler_params=pltpu.CompilerParams(vmem_limit_bytes=VMEM_BYTES // 2),
        cost_estimate=pl.CostEstimate(
            flops=2 * experts * slots * rows * width,
            bytes_accessed=2 * rows * width,
            transcendentals=0,
        ),
        name="place",
    )(jnp.reshape(start, (1,)).astype(jnp.int32), expert_ids.T, tokens)


def swap(value, experts):
    slots, width = value.shape
    return lax.all_to_all(
        value.reshape(experts, slots // experts, width),
        "expert",
        split_axis=0,
        concat_axis=0,
        tiled=True,
    ).reshape(slots, width)


def mix(weights, returned):
    return sum(
        lax.dot_general(
            w, returned, (((0,), (0,)), ((), ())), preferred_element_type=jnp.float32
        )
        for w in weights
    )


def add_join(groups):
    rows = groups[0][0].shape[0]
    widths = [group[0].shape[1] for group in groups]
    count = len(groups[0])
    flat = [term for group in groups for term in group]

    def kernel(*refs):
        out = refs[-1]
        at = 0
        for i, width in enumerate(widths):
            value = refs[i * count][...]
            for term in refs[i * count + 1 : (i + 1) * count]:
                value = value + term[...].astype(jnp.float32)
            out[:, at : at + width] = value.astype(jnp.bfloat16)
            at += width

    return pl.pallas_call(
        kernel,
        out_shape=jax.ShapeDtypeStruct((rows, sum(widths)), jnp.bfloat16),
        in_specs=[vmem()] * len(flat),
        out_specs=vmem(),
        compiler_params=pltpu.CompilerParams(vmem_limit_bytes=VMEM_BYTES // 2),
        cost_estimate=pl.CostEstimate(
            flops=count * rows * sum(widths),
            bytes_accessed=8 * rows * sum(widths),
            transcendentals=0,
        ),
        name="add_join",
    )(*flat)


def mix_last(weights, returned, first):
    rows = weights[0].shape[1]
    early = first[0].shape[1]
    late = returned.shape[1]
    count = len(weights)

    def kernel(*refs):
        parts, back, terms, out = refs[:count], refs[count], refs[count + 1 : -1], refs[-1]
        out[:, :early] = sum(term[...] for term in terms).astype(jnp.bfloat16)
        for at in range(0, late, 2 * LANES):
            end = min(at + 2 * LANES, late)
            out[:, early + at : early + end] = mix(
                [part[...] for part in parts], back[:, at:end]
            ).astype(jnp.bfloat16)

    return pl.pallas_call(
        kernel,
        out_shape=jax.ShapeDtypeStruct((rows, early + late), jnp.bfloat16),
        in_specs=[vmem()] * (count + 1 + len(first)),
        out_specs=vmem(),
        compiler_params=pltpu.CompilerParams(vmem_limit_bytes=VMEM_BYTES // 2),
        cost_estimate=pl.CostEstimate(
            flops=2 * count * returned.shape[0] * rows * late,
            bytes_accessed=2 * rows * (early + late),
            transcendentals=0,
        ),
        name="mix_last",
    )(*weights, returned, *first)


def on_device(tokens, expert_ids, gate_probs, w_gate, w_up, w_down):
    width = tokens.shape[1]
    experts = lax.axis_size("expert")
    ranks = lax.axis_size("tensor")
    me = lax.axis_index("tensor")
    w_gate = lax.all_gather(w_gate, "dp", axis=1, tiled=True)[0]
    w_up = lax.all_gather(w_up, "dp", axis=1, tiled=True)[0]
    w_down = lax.all_gather(w_down, "dp", axis=2, tiled=True)[0]
    weights = selectors(expert_ids, gate_probs, experts)

    def rank_at(step):
        return lax.rem(me + step, ranks)

    def send_up(value, step):
        return lax.ppermute(value, "tensor", [(i, (i + step) % ranks) for i in range(ranks)])

    share = width // ranks
    shared = round(share * 5 / 8 / LANES) * LANES
    direct_at = ranks * shared

    chosen, placed = place(tokens, expert_ids, experts, me * shared, shared)
    own = swap(placed, experts)
    cut = pl.cdiv(shared, 2 * LANES) * LANES
    others = []
    for begin, end in ((0, cut), (cut, shared)):
        for step in range(1, ranks):
            sent = send_up(own[:, begin:end], ranks - step)
            others.append((sent, rank_at(step) * shared + begin))
    placed = jnp.dot(chosen, tokens[:, direct_at:], preferred_element_type=jnp.float32)
    direct = swap(placed.astype(jnp.bfloat16), experts)
    (sums,) = lift([own], [me * shared], w_gate, w_up)
    for piece, at in others[:-1]:
        (sums,) = lift([piece], [at], w_gate, w_up, sums)

    early = round(share * 7 / 16 / 128) * 128
    columns = [jnp.int32(rank * share) for rank in range(ranks)]
    last, last_at = others[-1]
    hidden, partial = lift(
        [last, direct],
        [last_at, jnp.int32(direct_at)],
        w_gate,
        w_up,
        sums,
        (w_down, columns, early),
    )
    returned = swap(partial, experts)
    edges = [early, early + (share - early) // 512 * 256, share] if share - early >= 512 else [early, share]
    owned = []
    for at, end in zip(edges[:-1], edges[1:]):
        cut = end - at
        arrived = [
            send_up(drop(hidden, w_down, rank_at(step) * share + at, cut, jnp.bfloat16), step)
            for step in range(1, ranks)
        ]
        value = drop(hidden, w_down, me * share + at, cut, jnp.float32)
        owned.append([value, *arrived])
    returned, owned = lax.optimization_barrier((returned, add_join(owned)))
    first = mix(weights, returned)

    def part_of(rank):
        return lax.dynamic_slice_in_dim(first, rank * early, early, axis=1)

    terms = [part_of(me)]
    for step in range(1, ranks):
        terms.append(send_up(part_of(rank_at(step)), step))
    return mix_last(weights, swap(owned, experts), terms)


def solution(mesh):
    placed = (
        P(("groups", "dp", "expert"), None),
        P(("groups", "dp", "expert"), None),
        P(("groups", "dp", "expert"), None),
        P("expert", "dp", "tensor"),
        P("expert", "dp", "tensor"),
        P("expert", "tensor", "dp"),
    )
    return jax.shard_map(
        on_device,
        mesh=mesh,
        in_specs=placed,
        out_specs=P(("groups", "dp", "expert"), "tensor"),
        check_vma=False,
    )
```

```python
import jax
import jax.numpy as jnp
from jax import lax
from jax.experimental import pallas as pl
from jax.experimental.pallas import tpu as pltpu
from jax.sharding import PartitionSpec as P

TOP = 2
BLOCK = 128
CAP = 24
LANES = 256
VMEM_BYTES = 50 * 1024 * 1024


def tile_of(width, most=LANES):
    for tile in range(most, 127, -128):
        if width % tile == 0:
            return tile
    return width


def vmem():
    return pl.BlockSpec(memory_space=pltpu.VMEM)


def hbm():
    return pl.BlockSpec(memory_space=pl.ANY)


def dma(count):
    return pltpu.SemaphoreType.DMA((count,))


def in_turn(groups, ahead):
    for group in groups[:ahead]:
        for copy in group:
            copy.start()
    left = iter(range(len(groups)))

    def wait():
        now = next(left)
        if now + ahead < len(groups):
            for copy in groups[now + ahead]:
                copy.start()
        for copy in groups[now]:
            copy.wait()

    return wait


def column_groups(source, starts, width, target, sems):
    tiles, depth, tile = target.shape
    each = width // tile
    groups = []
    for n in range(tiles):
        at = pl.multiple_of(starts[n // each] + (n % each) * tile, 128)
        groups.append(
            [pltpu.make_async_copy(source.at[:, pl.ds(at, tile)], target.at[n], sems.at[n])]
        )
    return groups


def drop_tile(hidden, tiles, n, out):
    tile = tiles.shape[2]
    value = jnp.dot(hidden[...], tiles[n], preferred_element_type=jnp.float32)
    out[:, n * tile : (n + 1) * tile] = value.astype(out.dtype)


def lift(pieces, starts, w_gate, w_up, sums=None, back=None):
    rows = pieces[0].shape[0]
    depths = [piece.shape[1] for piece in pieces]
    depth = sum(depths)
    count = len(pieces)
    hidden = w_gate.shape[1]
    tile = tile_of(hidden)
    tiles = hidden // tile
    given = [] if sums is None else [sums]
    scalars = list(starts)
    args = [*pieces, w_gate, w_up, *given]
    scratch = [
        pltpu.VMEM((rows, depth), jnp.bfloat16),
        pltpu.VMEM((tiles, depth, 2 * tile), jnp.bfloat16),
        pltpu.VMEM((tiles, rows, 2 * tile), jnp.float32),
    ]
    scratch += [dma(tiles)] * (2 * count + 2)
    flops = 4 * rows * depth * hidden
    moved = 4 * depth * hidden + 16 * rows * hidden
    if back is None:
        out_shape = [jax.ShapeDtypeStruct((tiles, rows, 2 * tile), jnp.float32)]
        out_specs = [hbm()]
    else:
        w_down, columns, width = back
        wide = tile_of(width, 1024)
        drops = len(columns) * width // wide
        scratch += [pltpu.VMEM((drops, hidden, wide), jnp.bfloat16), dma(drops)]
        scalars += list(columns)
        args += [w_down]
        out_shape = [
            jax.ShapeDtypeStruct((rows, hidden), jnp.bfloat16),
            jax.ShapeDtypeStruct((rows, len(columns) * width), jnp.bfloat16),
        ]
        out_specs = [vmem(), vmem()]
        flops += 2 * rows * hidden * len(columns) * width
        moved += 2 * hidden * len(columns) * width

    def kernel(at, *refs):
        parts, refs = refs[:count], refs[count:]
        (gate_from, up_from), refs = refs[:2], refs[2:]
        before, refs = refs[: len(given)], refs[len(given) :]
        more = len(args) - count - 2 - len(given)
        down_from, refs = refs[:more], refs[more:]
        outs, refs = refs[: len(out_shape)], refs[len(out_shape) :]
        whole, both, totals = refs[:3]
        sems, (sum_sems, out_sems) = refs[3 : 3 + 2 * count], refs[3 + 2 * count : 5 + 2 * count]
        groups = []
        for n in range(tiles):
            across = pl.ds(n * tile, tile)
            group = []
            row = 0
            for i, size in enumerate(depths):
                begin = pl.multiple_of(at[i], 128)
                for side, source in enumerate((gate_from, up_from)):
                    group.append(
                        pltpu.make_async_copy(
                            source.at[pl.ds(begin, size), across],
                            both.at[n, pl.ds(row, size), pl.ds(side * tile, tile)],
                            sems[2 * i + side].at[n],
                        )
                    )
                row += size
            for source in before:
                group.append(
                    pltpu.make_async_copy(source.at[n], totals.at[n], sum_sems.at[n])
                )
            groups.append(group)
        if back is not None:
            ranges = [at[count + i] for i in range(len(columns))]
            groups += column_groups(down_from[0], ranges, width, refs[-2], refs[-1])
        wait = in_turn(groups, 3)
        row = 0
        for part, size in zip(parts, depths):
            whole[:, row : row + size] = part[...]
            row += size

        def store(n):
            return pltpu.make_async_copy(totals.at[n], outs[0].at[n], out_sems.at[n])

        def settle(n, product):
            if given:
                product = product + totals[n]
            if back is None:
                totals[n] = product
                store(n).start()
            else:
                gate, up = product[:, :tile], product[:, tile:]
                value = gate / (1.0 + jnp.exp(-gate)) * up
                outs[0][:, n * tile : (n + 1) * tile] = value.astype(jnp.bfloat16)

        held = None
        for n in range(tiles):
            wait()
            product = jnp.dot(whole[...], both[n], preferred_element_type=jnp.float32)
            if held is not None:
                settle(n - 1, held)
            held = product
        settle(tiles - 1, held)
        if back is None:
            for n in range(tiles):
                store(n).wait()
        else:
            for n in range(drops):
                wait()
                drop_tile(outs[0], refs[-2], n, outs[1])

    return pl.pallas_call(
        kernel,
        out_shape=out_shape,
        in_specs=[pl.BlockSpec(memory_space=pltpu.SMEM)]
        + [vmem()] * count
        + [hbm()] * (len(args) - count),
        out_specs=out_specs,
        scratch_shapes=scratch,
        compiler_params=pltpu.CompilerParams(vmem_limit_bytes=VMEM_BYTES),
        cost_estimate=pl.CostEstimate(
            flops=flops,
            bytes_accessed=moved,
            transcendentals=rows * hidden,
        ),
        name="lift",
    )(jnp.stack(scalars).astype(jnp.int32), *args)


def drop(hidden, w_down, start, width, dtype):
    rows, depth = hidden.shape
    tile = tile_of(width, 1024)

    def kernel(at, hidden, w_down, out, weight, sems):
        wait = in_turn(column_groups(w_down, [at[0]], width, weight, sems), 2)
        for n in range(width // tile):
            wait()
            drop_tile(hidden, weight, n, out)

    return pl.pallas_call(
        kernel,
        out_shape=jax.ShapeDtypeStruct((rows, width), dtype),
        in_specs=[pl.BlockSpec(memory_space=pltpu.SMEM), vmem(), hbm()],
        out_specs=vmem(),
        scratch_shapes=[
            pltpu.VMEM((width // tile, depth, tile), jnp.bfloat16),
            dma(width // tile),
        ],
        compiler_params=pltpu.CompilerParams(vmem_limit_bytes=VMEM_BYTES),
        cost_estimate=pl.CostEstimate(
            flops=2 * rows * depth * width, bytes_accessed=2 * depth * width, transcendentals=0
        ),
        name="drop",
    )(jnp.reshape(start, (1,)).astype(jnp.int32), hidden, w_down)


def selectors(expert_ids, gate_probs, experts):
    rows = expert_ids.shape[0]
    blocks = rows // BLOCK
    match = expert_ids.T[:, None, :] == jnp.arange(experts, dtype=jnp.int32)[None, :, None]
    named = jnp.any(match, axis=0)
    weight = jnp.sum(jnp.where(match, gate_probs.T[:, None, :], 0.0), axis=0)
    row = jnp.arange(rows, dtype=jnp.int32)
    same = row[:, None] // BLOCK == row[None, :] // BLOCK
    earlier = ((row[:, None] < row[None, :]) & same).astype(jnp.bfloat16)
    before = jnp.dot(named.astype(jnp.bfloat16), earlier, preferred_element_type=jnp.float32)
    place = before.astype(jnp.int32) + (row // BLOCK * CAP)[None, :]
    slots = jnp.arange(blocks * CAP, dtype=jnp.int32)
    hit = named[:, None, :] & (place[:, None, :] == slots[None, :, None])
    high = weight.astype(jnp.bfloat16)
    rest = weight - high.astype(jnp.float32)
    middle = rest.astype(jnp.bfloat16)
    low = (rest - middle.astype(jnp.float32)).astype(jnp.bfloat16)
    flat = (experts * blocks * CAP, rows)
    return [
        jnp.where(hit, part[:, None, :], 0).astype(jnp.bfloat16).reshape(flat)
        for part in (high, middle, low)
    ]


def place(tokens, expert_ids, experts, start, width):
    rows = tokens.shape[0]
    slots = rows // BLOCK * CAP

    def kernel(at, ids, tokens, chosen, out, part, picked, sem):
        begin = pl.multiple_of(at[0], 128)
        copy = pltpu.make_async_copy(tokens.at[:, pl.ds(begin, width)], part, sem)
        copy.start()
        expert = lax.broadcasted_iota(jnp.int32, (experts, rows), 0)
        named = jnp.zeros((experts, rows), jnp.float32)
        for k in range(TOP):
            named = named + jnp.where(ids[k : k + 1] == expert, 1.0, 0.0)
        row = lax.broadcasted_iota(jnp.int32, (rows, rows), 0)
        later = lax.broadcasted_iota(jnp.int32, (rows, rows), 1)
        same = row // BLOCK == later // BLOCK
        earlier = jnp.where((row < later) & same, 1.0, 0.0).astype(jnp.bfloat16)
        before = jnp.dot(
            named.astype(jnp.bfloat16), earlier, preferred_element_type=jnp.float32
        ).astype(jnp.int32)
        block = lax.broadcasted_iota(jnp.int32, (experts, rows), 1) // BLOCK
        where = jnp.where(named > 0.0, before + block * CAP, -1)
        slot = lax.broadcasted_iota(jnp.int32, (slots, rows), 0)
        for e in range(experts):
            picked[e * slots : (e + 1) * slots] = jnp.where(where[e : e + 1] == slot, 1.0, 0.0)
        chosen[...] = picked[...].astype(jnp.bfloat16)
        copy.wait()
        value = jnp.dot(chosen[...], part[...], preferred_element_type=jnp.float32)
        out[...] = value.astype(jnp.bfloat16)

    return pl.pallas_call(
        kernel,
        out_shape=[
            jax.ShapeDtypeStruct((experts * slots, rows), jnp.bfloat16),
            jax.ShapeDtypeStruct((experts * slots, width), jnp.bfloat16),
        ],
        in_specs=[pl.BlockSpec(memory_space=pltpu.SMEM), vmem(), hbm()],
        out_specs=[vmem(), vmem()],
        scratch_shapes=[
            pltpu.VMEM((rows, width), jnp.bfloat16),
            pltpu.VMEM((experts * slots, rows), jnp.float32),
            pltpu.SemaphoreType.DMA,
        ],
        compiler_params=pltpu.CompilerParams(vmem_limit_bytes=VMEM_BYTES // 2),
        cost_estimate=pl.CostEstimate(
            flops=2 * experts * slots * rows * width,
            bytes_accessed=2 * rows * width,
            transcendentals=0,
        ),
        name="place",
    )(jnp.reshape(start, (1,)).astype(jnp.int32), expert_ids.T, tokens)


def swap(value, experts):
    slots, width = value.shape
    return lax.all_to_all(
        value.reshape(experts, slots // experts, width),
        "expert",
        split_axis=0,
        concat_axis=0,
        tiled=True,
    ).reshape(slots, width)


def mix(weights, returned):
    return sum(
        lax.dot_general(
            w, returned, (((0,), (0,)), ((), ())), preferred_element_type=jnp.float32
        )
        for w in weights
    )


def add_join(groups):
    rows = groups[0][0].shape[0]
    widths = [group[0].shape[1] for group in groups]
    count = len(groups[0])
    flat = [term for group in groups for term in group]

    def kernel(*refs):
        out = refs[-1]
        at = 0
        for i, width in enumerate(widths):
            value = refs[i * count][...]
            for term in refs[i * count + 1 : (i + 1) * count]:
                value = value + term[...].astype(jnp.float32)
            out[:, at : at + width] = value.astype(jnp.bfloat16)
            at += width

    return pl.pallas_call(
        kernel,
        out_shape=jax.ShapeDtypeStruct((rows, sum(widths)), jnp.bfloat16),
        in_specs=[vmem()] * len(flat),
        out_specs=vmem(),
        compiler_params=pltpu.CompilerParams(vmem_limit_bytes=VMEM_BYTES // 2),
        cost_estimate=pl.CostEstimate(
            flops=count * rows * sum(widths),
            bytes_accessed=8 * rows * sum(widths),
            transcendentals=0,
        ),
        name="add_join",
    )(*flat)


def mix_last(weights, returned, first):
    rows = weights[0].shape[1]
    early = first[0].shape[1]
    late = returned.shape[1]
    count = len(weights)

    def kernel(*refs):
        parts, back, terms, out = refs[:count], refs[count], refs[count + 1 : -1], refs[-1]
        out[:, :early] = sum(term[...] for term in terms).astype(jnp.bfloat16)
        for at in range(0, late, 2 * LANES):
            end = min(at + 2 * LANES, late)
            out[:, early + at : early + end] = mix(
                [part[...] for part in parts], back[:, at:end]
            ).astype(jnp.bfloat16)

    return pl.pallas_call(
        kernel,
        out_shape=jax.ShapeDtypeStruct((rows, early + late), jnp.bfloat16),
        in_specs=[vmem()] * (count + 1 + len(first)),
        out_specs=vmem(),
        compiler_params=pltpu.CompilerParams(vmem_limit_bytes=VMEM_BYTES // 2),
        cost_estimate=pl.CostEstimate(
            flops=2 * count * returned.shape[0] * rows * late,
            bytes_accessed=2 * rows * (early + late),
            transcendentals=0,
        ),
        name="mix_last",
    )(*weights, returned, *first)


def on_device(tokens, expert_ids, gate_probs, w_gate, w_up, w_down):
    width = tokens.shape[1]
    experts = lax.axis_size("expert")
    ranks = lax.axis_size("tensor")
    me = lax.axis_index("tensor")
    w_gate = lax.all_gather(w_gate, "dp", axis=1, tiled=True)[0]
    w_up = lax.all_gather(w_up, "dp", axis=1, tiled=True)[0]
    w_down = lax.all_gather(w_down, "dp", axis=2, tiled=True)[0]
    weights = selectors(expert_ids, gate_probs, experts)

    def rank_at(step):
        return lax.rem(me + step, ranks)

    def send_up(value, step):
        return lax.ppermute(value, "tensor", [(i, (i + step) % ranks) for i in range(ranks)])

    share = width // ranks
    shared = round(share * 5 / 8 / LANES) * LANES
    direct_at = ranks * shared

    chosen, placed = place(tokens, expert_ids, experts, me * shared, shared)
    own = swap(placed, experts)
    cut = pl.cdiv(shared, 2 * LANES) * LANES
    others = []
    for begin, end in ((0, cut), (cut, shared)):
        for step in range(1, ranks):
            sent = send_up(own[:, begin:end], ranks - step)
            others.append((sent, rank_at(step) * shared + begin))
    placed = jnp.dot(chosen, tokens[:, direct_at:], preferred_element_type=jnp.float32)
    direct = swap(placed.astype(jnp.bfloat16), experts)
    (sums,) = lift([own], [me * shared], w_gate, w_up)
    for piece, at in others[:-1]:
        (sums,) = lift([piece], [at], w_gate, w_up, sums)

    early = round(share * 3 / 8 / 128) * 128
    columns = [jnp.int32(rank * share) for rank in range(ranks)]
    last, last_at = others[-1]
    hidden, partial = lift(
        [last, direct],
        [last_at, jnp.int32(direct_at)],
        w_gate,
        w_up,
        sums,
        (w_down, columns, early),
    )
    returned = swap(partial, experts)
    edges = [early, early + (share - early) // 512 * 256, share] if share - early >= 512 else [early, share]
    owned = []
    for at, end in zip(edges[:-1], edges[1:]):
        cut = end - at
        arrived = [
            send_up(drop(hidden, w_down, rank_at(step) * share + at, cut, jnp.bfloat16), step)
            for step in range(1, ranks)
        ]
        value = drop(hidden, w_down, me * share + at, cut, jnp.float32)
        owned.append([value, *arrived])
    returned, owned = lax.optimization_barrier((returned, add_join(owned)))
    first = mix(weights, returned)

    def part_of(rank):
        return lax.dynamic_slice_in_dim(first, rank * early, early, axis=1)

    terms = [part_of(me)]
    for step in range(1, ranks):
        terms.append(send_up(part_of(rank_at(step)), step))
    return mix_last(weights, swap(owned, experts), terms)


def solution(mesh):
    placed = (
        P(("groups", "dp", "expert"), None),
        P(("groups", "dp", "expert"), None),
        P(("groups", "dp", "expert"), None),
        P("expert", "dp", "tensor"),
        P("expert", "dp", "tensor"),
        P("expert", "tensor", "dp"),
    )
    return jax.shard_map(
        on_device,
        mesh=mesh,
        in_specs=placed,
        out_specs=P(("groups", "dp", "expert"), "tensor"),
        check_vma=False,
    )
```
